32 devices in a mesh: gx: 4 (over y, x), gy: 2 (over core), gz: 4 (over z).
Axes of the slice: x: 2, y: 2, z: 4, core: 2. Of those that a mesh axis runs over, the one named last changes fastest.
Arguments:
- features: bfloat16 [64, 32, 48, 512], P('gx', 'gy', 'gz'), may hold values from -6 to 6
- cotangent: bfloat16 [64, 32, 48, 512], P('gx', 'gy', 'gz'), may hold values from -6 to 6
- reduce_weight: bfloat16 [512, 128], replicated, may hold values from -0.25 to 0.25
- project_weight: bfloat16 [512, 64], replicated, may hold values from -0.25 to 0.25
- expand_weight: bfloat16 [512, 128], replicated, may hold values from -0.5 to 0.5
- adjacency: float32 [64, 64], replicated, may hold values from -0.75 to 0.75
- node_weight: float32 [128, 128], replicated, may hold values from -0.5 to 0.5
Outputs:
- grad_features: bfloat16 [64, 32, 48, 512], P('gx', 'gy', 'gz')
- grad_reduce: float32 [512, 128], P(('gx', 'gy', 'gz'))
- grad_project: float32 [512, 64], P(('gx', 'gy', 'gz'))
- grad_expand: float32 [512, 128], P(('gx', 'gy', 'gz'))
- grad_adjacency: float32 [64, 64], replicated
- grad_node: float32 [128, 128], replicated
The draws below stay inside these ranges and needn't reach their ends.
All inputs are finite; a program needn't handle non-finite values.
Results may differ from the reference program's by a relative error of at most 0.0064.
Values sent between devices are 32-bit elements; how exact they have to be, the bound alone decides.
No kernel may reach another device: no remote copies, remote signals or barrier semaphores. Data moves between devices by JAX's collectives and lax.ppermute only.
A program may use at most 64 MiB of HBM per device.

```python
import math
import jax
import jax.numpy as jnp
from jax import lax

C = 512
CR = 128
NODES = 64
VX = 64
VY = 32
VZ = 48


def block_levels(rng, shape, shards, smallest, largest):
    def one(position, blocks):
        draws = jax.random.uniform(jax.random.fold_in(jax.random.fold_in(rng, 6), position), (blocks,), jnp.float32, smallest / len(shards), largest / len(shards))
        return jnp.repeat(jnp.exp(draws), shape[position] // blocks).reshape((-1,) + (1,) * (len(shape) - position - 1))

    loudness = one(*shards[0])
    for cut in shards[1:]:
        loudness = loudness * one(*cut)
    return loudness


def centred(key, dims, deviation, limit, shards=(), kind=jnp.bfloat16):
    level = block_levels(key, dims, shards, -0.22, 0.18) if shards else 1.0
    drawn = jax.random.normal(key, dims, jnp.float32) * deviation * level
    return jnp.minimum(jnp.maximum(drawn, -limit), limit).astype(kind)


def setup_inputs(seed: int = 0) -> dict:
    seeds = jax.random.split(jax.random.key(seed), 8)
    return {
        "features": centred(seeds[0], (VX, VY, VZ, C), 1.0, 6.0, ((0, 4), (1, 2), (2, 4))),
        "cotangent": centred(seeds[1], (VX, VY, VZ, C), 1.0, 6.0, ((0, 4), (1, 2), (2, 4))),
        "reduce_weight": centred(seeds[2], (C, CR), C ** -0.5, 0.25),
        "project_weight": centred(seeds[3], (C, NODES), C ** -0.5, 0.25),
        "expand_weight": centred(seeds[4], (C, CR), CR ** -0.5, 0.5),
        "adjacency": centred(seeds[5], (NODES, NODES), NODES ** -0.5, 0.75, (), jnp.float32),
        "node_weight": centred(seeds[6], (CR, CR), CR ** -0.5, 0.5, (), jnp.float32),
    }


def exact(a, b):
    return jnp.dot(a, b, precision=lax.Precision.HIGHEST)

def reference(features, cotangent, reduce_weight, project_weight, expand_weight, adjacency, node_weight):
    total = features.shape[0] * features.shape[1] * features.shape[2]
    scale = 1.0 / math.sqrt(total)
    flat_x = features.reshape(total, C)
    flat_g = cotangent.reshape(total, C)
    reduced = jnp.dot(flat_x, reduce_weight, preferred_element_type=jnp.float32).astype(jnp.bfloat16)
    projection = jnp.dot(flat_x, project_weight, preferred_element_type=jnp.float32).astype(jnp.bfloat16)
    nodes = scale * jnp.dot(projection.T, reduced, preferred_element_type=jnp.float32)
    hidden = nodes - exact(adjacency, nodes)
    pre = exact(hidden, node_weight)
    node_out = jnp.maximum(pre, 0.0).astype(jnp.bfloat16)
    d_mapped = jnp.dot(flat_g, expand_weight, preferred_element_type=jnp.float32).astype(jnp.bfloat16)
    d_node_out = jnp.dot(projection.T, d_mapped, preferred_element_type=jnp.float32)
    d_pre = jnp.where(pre > 0.0, d_node_out, jnp.float32(0.0))
    grad_node = scale * exact(hidden.T, d_pre)
    d_hidden = exact(d_pre, node_weight.T)
    grad_adjacency = -scale * exact(d_hidden, nodes.T)
    d_nodes = d_hidden - exact(adjacency.T, d_hidden)
    d_nodes_b = d_nodes.astype(jnp.bfloat16)
    d_projection = (jnp.dot(d_mapped, node_out.T, preferred_element_type=jnp.float32) + scale * jnp.dot(reduced, d_nodes_b.T, preferred_element_type=jnp.float32)).astype(jnp.bfloat16)
    d_reduced = (scale * jnp.dot(projection, d_nodes_b, preferred_element_type=jnp.float32)).astype(jnp.bfloat16)
    grad_flat = flat_g.astype(jnp.float32) + jnp.dot(d_reduced, reduce_weight.T, preferred_element_type=jnp.float32) + jnp.dot(d_projection, project_weight.T, preferred_element_type=jnp.float32)
    grad_features = grad_flat.astype(jnp.bfloat16).reshape(features.shape)
    cross = jnp.dot(flat_x.T, projection, preferred_element_type=jnp.float32)
    x_dm = jnp.dot(flat_x.T, d_mapped, preferred_element_type=jnp.float32)
    x_red = jnp.dot(flat_x.T, reduced, preferred_element_type=jnp.float32)
    g_proj = jnp.dot(flat_g.T, projection, preferred_element_type=jnp.float32)
    node_f = node_out.astype(jnp.float32)
    dn_f = d_nodes_b.astype(jnp.float32)
    grad_reduce = scale * scale * exact(cross, dn_f)
    grad_project = scale * exact(x_dm, node_f.T) + scale * scale * exact(x_red, dn_f.T)
    grad_expand = scale * exact(g_proj, node_f)
    return (grad_features, grad_reduce, grad_project, grad_expand, grad_adjacency, grad_node)
```

```python
import functools
import math

import jax
import jax.numpy as jnp
from jax import lax
from jax.experimental import pallas as pl
from jax.experimental.pallas import tpu as pltpu
from jax.sharding import PartitionSpec as P

AXES = ("gx", "gy", "gz")
RING = ("gy", "gx", "gz")
F32 = jnp.float32
BF16 = jnp.bfloat16
VMEM_LIMIT = 40 * 1024 * 1024


def exact(a, b, dims=((1,), (0,))):
    return lax.dot_general(
        a, b, (dims, ((), ())), precision=lax.Precision.HIGHEST, preferred_element_type=F32
    )


def mxu(a, b, dims=((1,), (0,))):
    return lax.dot_general(a, b, (dims, ((), ())), preferred_element_type=F32)


def params():
    return pltpu.CompilerParams(vmem_limit_bytes=VMEM_LIMIT)


def cost(flops, nbytes):
    return pl.CostEstimate(flops=flops, bytes_accessed=nbytes, transcendentals=0)


def whole(shape):
    return pl.BlockSpec(shape, lambda *_: (0,) * len(shape))


def row_block(total):
    for size in (512, 384, 256, 128, 64, 32, 16):
        if total % size == 0:
            return size
    return total


def project_kernel(x_ref, g_ref, wr_ref, wpt_ref, we_ref, rd_ref, p_ref, term_ref, wcat_ref):
    cr = wr_ref.shape[1]
    nodes = wpt_ref.shape[0]

    @pl.when(pl.program_id(0) == 0)
    def _():
        wcat_ref[:, :cr] = wr_ref[...]
        padded = jnp.concatenate([wpt_ref[...], jnp.zeros_like(wpt_ref)], axis=0)
        wcat_ref[:, cr:] = padded.T
        term_ref[...] = jnp.zeros_like(term_ref)

    both = mxu(x_ref[...], wcat_ref[...]).astype(BF16)
    mapped = mxu(g_ref[...], we_ref[...]).astype(BF16)
    rd = jnp.concatenate([both[:, :cr], mapped], axis=1)
    proj = both[:, cr:]
    rd_ref[...] = rd
    p_ref[...] = proj
    term_ref[...] += mxu(proj, rd, ((0,), (0,)))[:nodes]


def project(x, g, wr, wpt, we):
    rows, chan = x.shape
    cr, nodes = wr.shape[1], wpt.shape[0]
    step = row_block(rows)
    rowspec = lambda width: pl.BlockSpec((step, width), lambda i: (i, 0))
    return pl.pallas_call(
        project_kernel,
        grid=(rows // step,),
        in_specs=[rowspec(chan), rowspec(chan), whole(wr.shape), whole(wpt.shape), whole(we.shape)],
        out_specs=[
            rowspec(2 * cr),
            rowspec(2 * nodes),
            whole((nodes, 2 * cr)),
            whole((chan, cr + 2 * nodes)),
        ],
        out_shape=[
            jax.ShapeDtypeStruct((rows, 2 * cr), BF16),
            jax.ShapeDtypeStruct((rows, 2 * nodes), BF16),
            jax.ShapeDtypeStruct((nodes, 2 * cr), F32),
            jax.ShapeDtypeStruct((chan, cr + 2 * nodes), BF16),
        ],
        compiler_params=params(),
        cost_estimate=cost(2 * rows * chan * 512, rows * chan * 4 + rows * 768),
        name="project",
    )(x, g, wr, wpt, we)


def weight_kernel(count, index_ref, x_ref, g_ref, rd_ref, p_ref, *rest):
    outs, sums_ref = rest[:count], rest[count]
    step = pl.program_id(0)
    nodes = p_ref.shape[1] // 2
    wide = rd_ref.shape[1]

    @pl.when(step == 0)
    def _():
        sums_ref[...] = jnp.zeros_like(sums_ref)

    proj = p_ref[...][:, :nodes]
    x = x_ref[...]
    sums_ref[:wide] += mxu(rd_ref[...], x, ((0,), (0,)))
    sums_ref[wide : wide + nodes] += mxu(proj, x, ((0,), (0,)))
    sums_ref[wide + nodes :] += mxu(proj, g_ref[...], ((0,), (0,)))

    @pl.when(step == pl.num_programs(0) - 1)
    def _():
        first, _, third, width = outs[0].shape[0], count, outs[0].shape[1], outs[0].shape[2]
        total = sums_ref[...].T.reshape(first, count, third, width)
        scatter(total, 1, count, index_ref, outs)


def scatter(total, axis, count, index_ref, outs):
    me = index_ref[0]
    for peer in range(count):
        for block in range(count):
            @pl.when(lax.bitwise_xor(me, peer) == block)
            def _():
                if axis == 1:
                    outs[peer][...] = total[:, block]
                else:
                    outs[peer][...] = total[block]


def weight_terms(x, g, rd, p, index, sizes):
    rows, chan = x.shape
    step = row_block(rows)
    gx, gy, gz = sizes
    width = rd.shape[1] + p.shape[1]
    part = (gx, chan // (gx * gy), width)
    rowspec = lambda wide: pl.BlockSpec((step, wide), lambda i: (i, 0))
    return pl.pallas_call(
        functools.partial(weight_kernel, gy),
        grid=(rows // step,),
        in_specs=[
            pl.BlockSpec(memory_space=pltpu.SMEM),
            rowspec(chan),
            rowspec(chan),
            rowspec(rd.shape[1]),
            rowspec(p.shape[1]),
        ],
        out_specs=[whole(part)] * gy,
        out_shape=[jax.ShapeDtypeStruct(part, F32)] * gy,
        scratch_shapes=[pltpu.VMEM((width, chan), F32)],
        compiler_params=params(),
        cost_estimate=cost(2 * rows * chan * 512, rows * chan * 4 + rows * 768 + width * chan * 4),
        name="weight_terms",
    )(index, x, g, rd, p)


def split_kernel(ins, count, index_ref, *refs):
    total = refs[0][...]
    for ref in refs[1:ins]:
        total = total + ref[...]
    scatter(total, 0, count, index_ref, refs[ins:])


def split(parts, count, index):
    first, third, width = parts[0].shape
    if first != count:
        parts = [p.reshape(count, third // count, width) for p in parts]
    shape = parts[0].shape
    return pl.pallas_call(
        functools.partial(split_kernel, len(parts), count),
        in_specs=[pl.BlockSpec(memory_space=pltpu.SMEM)] + [pl.BlockSpec(memory_space=pltpu.VMEM)] * len(parts),
        out_specs=[pl.BlockSpec(memory_space=pltpu.VMEM)] * count,
        out_shape=[jax.ShapeDtypeStruct(shape[1:], F32)] * count,
        compiler_params=params(),
        cost_estimate=cost(0, 8 * math.prod(shape) * len(parts)),
        name="split",
    )(index, *parts)


def swap(value, axis, peer):
    size = lax.axis_size(axis)
    return lax.ppermute(value, axis, [(i, i ^ peer) for i in range(size)])


def feature_kernel(
    ins, scale, *refs
):
    terms = refs[:ins]
    (adj_ref, nw_ref, wcat_ref, g_ref, rd_ref, p_ref) = refs[ins : ins + 6]
    (out_ref, ga_ref, gn_ref, no_ref, dn_ref, mix_ref, dnb_ref) = refs[ins + 6 :]
    nodes_n, cr = no_ref.shape

    @pl.when(pl.program_id(0) == 0)
    def _():
        total = terms[0][...]
        for ref in terms[1:]:
            total = total + ref[...]
        adj, nw = adj_ref[...], nw_ref[...]
        nodes = scale * total[:, :cr]
        d_node_out = total[:, cr:]
        hidden = nodes - exact(adj, nodes)
        pre = exact(hidden, nw)
        node_out = jnp.maximum(pre, 0.0).astype(BF16)
        d_pre = jnp.where(pre > 0.0, d_node_out, 0.0)
        gn_ref[...] = scale * exact(hidden, d_pre, ((0,), (0,)))
        d_hidden = exact(d_pre, nw, ((1,), (1,)))
        ga_ref[...] = -scale * exact(d_hidden, nodes, ((1,), (1,)))
        d_nodes = d_hidden - exact(adj, d_hidden, ((0,), (0,)))
        dn = d_nodes.astype(BF16)
        no_ref[...] = node_out.astype(F32)
        dn_ref[...] = dn.astype(F32)
        dnb_ref[:nodes_n] = dn
        dnb_ref[nodes_n:] = jnp.zeros((nodes_n, cr), BF16)
        blank = jnp.zeros((cr, cr), BF16)
        zero = jnp.zeros((nodes_n, cr), F32)
        dn_t = jnp.concatenate([dn.astype(F32), zero], axis=0).T.astype(BF16)
        no_t = jnp.concatenate([node_out.astype(F32), zero], axis=0).T.astype(BF16)
        mix_ref[:cr, :cr] = dn_t
        mix_ref[cr:, :cr] = blank
        mix_ref[:cr, cr:] = blank
        mix_ref[cr:, cr:] = no_t

    mixed = mxu(rd_ref[...], mix_ref[...])
    d_proj = (mixed[:, cr:] + scale * mixed[:, :cr]).astype(BF16)
    d_red = (scale * mxu(p_ref[...], dnb_ref[...])).astype(BF16)
    both = jnp.concatenate([d_red, d_proj], axis=1)
    out = g_ref[...].astype(F32) + mxu(both, wcat_ref[...], ((1,), (1,)))
    out_ref[...] = out.astype(BF16)


def feature_grads(terms, adjacency, node_weight, wcat, g, rd, p, scale):
    rows, chan = g.shape
    nodes, cr = adjacency.shape[0], node_weight.shape[0]
    step = row_block(rows)
    rowspec = lambda width: pl.BlockSpec((step, width), lambda i: (i, 0))
    return pl.pallas_call(
        functools.partial(feature_kernel, len(terms), scale),
        grid=(rows // step,),
        in_specs=[whole(t.shape) for t in terms]
        + [
            whole(adjacency.shape),
            whole(node_weight.shape),
            whole(wcat.shape),
            rowspec(chan),
            rowspec(rd.shape[1]),
            rowspec(p.shape[1]),
        ],
        out_specs=[
            rowspec(chan),
            whole((nodes, nodes)),
            whole((cr, cr)),
            whole((nodes, cr)),
            whole((nodes, cr)),
        ],
        out_shape=[
            jax.ShapeDtypeStruct((rows, chan), BF16),
            jax.ShapeDtypeStruct((nodes, nodes), F32),
            jax.ShapeDtypeStruct((cr, cr), F32),
            jax.ShapeDtypeStruct((nodes, cr), F32),
            jax.ShapeDtypeStruct((nodes, cr), F32),
        ],
        scratch_shapes=[pltpu.VMEM((2 * cr, 2 * cr), BF16), pltpu.VMEM((2 * nodes, cr), BF16)],
        compiler_params=params(),
        cost_estimate=cost(2 * rows * 4 * 65536, rows * chan * 4 + rows * 768),
        name="feature_grads",
    )(*terms, adjacency, node_weight, wcat, g, rd, p)


def finish_kernel(ins, scale, *refs):
    total = refs[0][...]
    for ref in refs[1:ins]:
        total = total + ref[...]
    no_ref, dn_ref, gr_ref, gp_ref, ge_ref = refs[ins:]
    nodes, cr = no_ref.shape
    no, dn = no_ref[...], dn_ref[...]
    x_red, x_dm = total[:, :cr], total[:, cr : 2 * cr]
    cross = total[:, 2 * cr : 2 * cr + nodes]
    g_proj = total[:, 2 * cr + nodes :]
    gr_ref[...] = scale * scale * exact(cross, dn)
    gp_ref[...] = scale * exact(x_dm, no, ((1,), (1,))) + scale * scale * exact(
        x_red, dn, ((1,), (1,))
    )
    ge_ref[...] = scale * exact(g_proj, no)


def finish(parts, no, dn, scale):
    rows = parts[0].shape[0]
    nodes, cr = no.shape
    vmem = pl.BlockSpec(memory_space=pltpu.VMEM)
    return pl.pallas_call(
        functools.partial(finish_kernel, len(parts), scale),
        in_specs=[vmem] * (len(parts) + 2),
        out_specs=[vmem] * 3,
        out_shape=[
            jax.ShapeDtypeStruct((rows, cr), F32),
            jax.ShapeDtypeStruct((rows, nodes), F32),
            jax.ShapeDtypeStruct((rows, cr), F32),
        ],
        compiler_params=params(),
        cost_estimate=cost(0, rows * 4096),
        name="finish",
    )(*parts, no, dn)


def on_device(
    features, cotangent, reduce_weight, project_weight, expand_weight, adjacency, node_weight
):
    size_x, size_y, size_z, chan = features.shape
    local = size_x * size_y * size_z
    sizes = tuple(lax.axis_size(axis) for axis in AXES)
    total = local * math.prod(sizes)
    scale = 1.0 / math.sqrt(total)
    flat_x = features.transpose(0, 2, 1, 3).reshape(local, chan)
    flat_g = cotangent.transpose(0, 2, 1, 3).reshape(local, chan)
    where = {axis: lax.axis_index(axis).reshape(1).astype(jnp.int32) for axis in AXES}

    rd, p, term, wcat = project(flat_x, flat_g, reduce_weight, project_weight.T, expand_weight)

    terms = [term]
    for axis in RING:
        held = terms[0] if len(terms) == 1 else functools.reduce(jnp.add, terms)
        terms = [held] + [swap(held, axis, k) for k in range(1, lax.axis_size(axis))]

    parts = weight_terms(flat_x, flat_g, rd, p, where["gy"], sizes)
    parts = [parts[0]] + [swap(part, "gy", k) for k, part in enumerate(parts) if k]
    for axis in ("gx", "gz"):
        parts = split(parts, lax.axis_size(axis), where[axis])
        parts = [parts[0]] + [swap(part, axis, k) for k, part in enumerate(parts) if k]
        if axis == "gx":
            parts = [part[None] for part in parts]

    flat_out, grad_adjacency, grad_node, no, dn = feature_grads(
        terms, adjacency, node_weight, wcat, flat_g, rd, p, scale
    )
    grad_reduce, grad_project, grad_expand = finish(parts, no, dn, scale)
    grad_features = flat_out.reshape(size_x, size_z, size_y, chan).transpose(0, 2, 1, 3)
    return (grad_features, grad_reduce, grad_project, grad_expand, grad_adjacency, grad_node)


def solution(mesh):
    return jax.shard_map(
        on_device,
        mesh=mesh,
        in_specs=(P("gx", "gy", "gz", None), P("gx", "gy", "gz", None), P(), P(), P(), P(), P()),
        out_specs=(
            P("gx", "gy", "gz", None),
            P(AXES, None),
            P(AXES, None),
            P(AXES, None),
            P(),
            P(),
        ),
        check_vma=False,
    )
```

```python
import functools
import math

import jax
import jax.numpy as jnp
from jax import lax
from jax.experimental import pallas as pl
from jax.experimental.pallas import tpu as pltpu
from jax.sharding import PartitionSpec as P

AXES = ("gx", "gy", "gz")
F32 = jnp.float32
BF16 = jnp.bfloat16
HBM = pl.BlockSpec(memory_space=pltpu.HBM)
VMEM = pl.BlockSpec(memory_space=pltpu.VMEM)
SMEM = pl.BlockSpec(memory_space=pltpu.SMEM)
VMEM_LIMIT = 24 * 1024 * 1024


def exact(a, b, dims=((1,), (0,))):
    return lax.dot_general(
        a, b, (dims, ((), ())), precision=lax.Precision.HIGHEST, preferred_element_type=F32
    )


def mxu(a, b, dims=((1,), (0,))):
    return lax.dot_general(a, b, (dims, ((), ())), preferred_element_type=F32)


def held(shape, kind):
    return pltpu.VMEM(shape, kind)


def params():
    return pltpu.CompilerParams(vmem_limit_bytes=VMEM_LIMIT)


def cost(flops, nbytes):
    return pl.CostEstimate(flops=flops, bytes_accessed=nbytes, transcendentals=0)


def row_block(total):
    for size in (512, 384, 256, 128, 64, 32, 16):
        if total % size == 0:
            return size
    return total


def project_kernel(
    step, x_hbm, g_hbm, wr_hbm, wpt_hbm, we_hbm, adj_hbm, nw_hbm,
    x_ref, g_ref, rd_ref, p_ref, term_ref, wcat_ref, adj_ref, nw_ref, wpt_ref, we_ref, sems, xsem, gsem,
):
    rows = x_ref.shape[0]
    nodes = wpt_ref.shape[0]
    cr = we_ref.shape[1]
    chunks = [pl.ds(start, step) for start in range(0, rows, step)]
    load = lambda src, dst, sem: pltpu.make_async_copy(src, dst, sem)
    small = [
        load(wr_hbm, wcat_ref.at[:, pl.ds(0, cr)], sems.at[0]),
        load(wpt_hbm, wpt_ref, sems.at[1]),
        load(we_hbm, we_ref, sems.at[2]),
        load(adj_hbm, adj_ref, sems.at[3]),
        load(nw_hbm, nw_ref, sems.at[4]),
    ]
    xs = [load(x_hbm.at[c], x_ref.at[c], xsem.at[i]) for i, c in enumerate(chunks)]
    gs = [load(g_hbm.at[c], g_ref.at[c], gsem.at[i]) for i, c in enumerate(chunks)]
    for copy in small[:3]:
        copy.start()
    for x_copy, g_copy in zip(xs, gs):
        x_copy.start()
        g_copy.start()
    for copy in small[3:]:
        copy.start()
    for copy in small[:3]:
        copy.wait()
    padded = jnp.concatenate([wpt_ref[...], jnp.zeros_like(wpt_ref)], axis=0)
    wcat_ref[:, cr:] = padded.T
    for i, c in enumerate(chunks):
        xs[i].wait()
        both = mxu(x_ref[c], wcat_ref[...]).astype(BF16)
        gs[i].wait()
        mapped = mxu(g_ref[c], we_ref[...]).astype(BF16)
        rd = jnp.concatenate([both[:, :cr], mapped], axis=1)
        proj = both[:, cr:]
        rd_ref[c] = rd
        p_ref[c] = proj
        part = mxu(proj, rd, ((0,), (0,)))[:nodes]
        if i == 0:
            term_ref[:nodes] = part[:, :cr]
            term_ref[nodes:] = part[:, cr:]
        else:
            term_ref[:nodes] += part[:, :cr]
            term_ref[nodes:] += part[:, cr:]
    for copy in small[3:]:
        copy.wait()


def project(x, g, wr, wpt, we, adjacency, node_weight):
    rows, chan = x.shape
    cr, nodes = wr.shape[1], wpt.shape[0]
    step = row_block(rows)
    return pl.pallas_call(
        functools.partial(project_kernel, step),
        in_specs=[HBM] * 7,
        out_specs=[VMEM] * 8,
        out_shape=[
            held((rows, chan), BF16),
            held((rows, chan), BF16),
            held((rows, 2 * cr), BF16),
            held((rows, 2 * nodes), BF16),
            held((2 * nodes, cr), F32),
            held((chan, cr + 2 * nodes), BF16),
            held(adjacency.shape, F32),
            held(node_weight.shape, F32),
        ],
        scratch_shapes=[
            pltpu.VMEM(wpt.shape, BF16),
            pltpu.VMEM(we.shape, BF16),
            pltpu.SemaphoreType.DMA((5,)),
            pltpu.SemaphoreType.DMA((rows // step,)),
            pltpu.SemaphoreType.DMA((rows // step,)),
        ],
        compiler_params=params(),
        cost_estimate=cost(2 * rows * chan * 512, rows * chan * 4 + rows * 768),
        name="project",
    )(*(pltpu.with_memory_space_constraint(v, pltpu.HBM) for v in (x, g, wr, wpt, we, adjacency, node_weight)))


def weight_kernel(step, count, index_ref, x_ref, g_ref, rd_ref, p_ref, *rest):
    outs, (sums_ref, turned_ref) = rest[:count], rest[count:]
    rows = x_ref.shape[0]
    nodes = p_ref.shape[1] // 2
    wide = rd_ref.shape[1]
    for start in range(0, rows, step):
        c = pl.ds(start, step)
        proj = p_ref[c][:, :nodes]
        x = x_ref[c]
        pieces = (
            mxu(rd_ref[c], x, ((0,), (0,))),
            mxu(proj, x, ((0,), (0,))),
            mxu(proj, g_ref[c], ((0,), (0,))),
        )
        at = 0
        for piece in pieces:
            span = pl.ds(at, piece.shape[0])
            at += piece.shape[0]
            if start == 0:
                sums_ref[span] = piece
            else:
                sums_ref[span] += piece
    turned_ref[...] = sums_ref[...].T.reshape(turned_ref.shape)
    me = index_ref[0]
    for peer in range(count):
        outs[peer][...] = turned_ref[:, lax.bitwise_xor(me, peer)]


def weight_terms(x, g, rd, p, index, sizes):
    rows, chan = x.shape
    step = row_block(rows)
    gx, gy, gz = sizes
    width = rd.shape[1] + p.shape[1]
    part = (gx, chan // (gx * gy), width)
    return pl.pallas_call(
        functools.partial(weight_kernel, step, gy),
        in_specs=[SMEM] + [VMEM] * 4,
        out_specs=[VMEM] * gy,
        out_shape=[held(part, F32)] * gy,
        scratch_shapes=[
            pltpu.VMEM((width, chan), F32),
            pltpu.VMEM((gx, gy, chan // (gx * gy), width), F32),
        ],
        compiler_params=params(),
        cost_estimate=cost(2 * rows * chan * 512, rows * chan * 4 + rows * 768 + width * chan * 4),
        name="weight_terms",
    )(index, x, g, rd, p)


def split_kernel(ins, count, index_ref, *refs):
    outs, total_ref = refs[ins:-1], refs[-1]
    total = refs[0][...]
    for ref in refs[1:ins]:
        total = total + ref[...]
    total_ref[...] = total
    me = index_ref[0]
    for peer in range(count):
        outs[peer][...] = total_ref[lax.bitwise_xor(me, peer)]


def split(parts, count, index):
    first, third, width = parts[0].shape
    if first != count:
        parts = [p.reshape(count, third // count, width) for p in parts]
    shape = parts[0].shape
    return pl.pallas_call(
        functools.partial(split_kernel, len(parts), count),
        in_specs=[SMEM] + [VMEM] * len(parts),
        out_specs=[VMEM] * count,
        out_shape=[held(shape[1:], F32)] * count,
        scratch_shapes=[pltpu.VMEM(shape, F32)],
        compiler_params=params(),
        cost_estimate=cost(0, 8 * math.prod(shape) * len(parts)),
        name="split",
    )(index, *parts)


def share_kernel(in_ref, out_ref):
    total = jnp.sum(in_ref[...], axis=0, keepdims=True)
    out_ref[...] = jnp.broadcast_to(total, out_ref.shape)


def share(value):
    return pl.pallas_call(
        share_kernel,
        in_specs=[VMEM],
        out_specs=VMEM,
        out_shape=held(value.shape, F32),
        compiler_params=params(),
        name="share",
    )(value)


def node_sum(term):
    devices = math.prod(lax.axis_size(axis) for axis in AXES)
    shape = term.shape
    if term.size % (devices * 128):
        return lax.psum(term, AXES)
    lanes = min(128, term.size // devices)
    parts = term.reshape(devices, -1, lanes)
    got = lax.all_to_all(parts, AXES, 0, 0, tiled=True)
    return lax.all_to_all(share(got), AXES, 0, 0, tiled=True).reshape(shape)


def swap(value, axis, peer):
    size = lax.axis_size(axis)
    return lax.ppermute(value, axis, [(i, i ^ peer) for i in range(size)])


def feature_kernel(
    step, scale, total_ref, adj_ref, nw_ref, wcat_ref, g_ref, rd_ref, p_ref,
    out_hbm, ga_ref, gn_ref, no_ref, dn_ref, out_ref, mix_ref, dnb_ref, sems,
):
    nodes_n, cr = no_ref.shape
    rows = g_ref.shape[0]
    adj, nw = adj_ref[...], nw_ref[...]
    nodes = scale * total_ref[:nodes_n]
    d_node_out = total_ref[nodes_n:]
    hidden = nodes - exact(adj, nodes)
    pre = exact(hidden, nw)
    node_out = jnp.maximum(pre, 0.0).astype(BF16)
    d_pre = jnp.where(pre > 0.0, d_node_out, 0.0)
    d_hidden = exact(d_pre, nw, ((1,), (1,)))
    d_nodes = d_hidden - exact(adj, d_hidden, ((0,), (0,)))
    dn = d_nodes.astype(BF16)
    no_ref[...] = node_out.astype(F32)
    dn_ref[...] = dn.astype(F32)
    dnb_ref[:nodes_n] = dn
    dnb_ref[nodes_n:] = jnp.zeros((nodes_n, cr), BF16)
    blank = jnp.zeros((cr, cr), BF16)
    zero = jnp.zeros((nodes_n, cr), F32)
    mix_ref[:cr, :cr] = jnp.concatenate([dn.astype(F32), zero], axis=0).T.astype(BF16)
    mix_ref[cr:, :cr] = blank
    mix_ref[:cr, cr:] = blank
    mix_ref[cr:, cr:] = jnp.concatenate([node_out.astype(F32), zero], axis=0).T.astype(BF16)
    copies = []
    for i, start in enumerate(range(0, rows, step)):
        c = pl.ds(start, step)
        mixed = mxu(rd_ref[c], mix_ref[...])
        d_proj = (mixed[:, cr:] + scale * mixed[:, :cr]).astype(BF16)
        d_red = (scale * mxu(p_ref[c], dnb_ref[...])).astype(BF16)
        both = jnp.concatenate([d_red, d_proj], axis=1)
        out = g_ref[c].astype(F32) + mxu(both, wcat_ref[...], ((1,), (1,)))
        out_ref[c] = out.astype(BF16)
        copies.append(pltpu.make_async_copy(out_ref.at[c], out_hbm.at[c], sems.at[i]))
        copies[-1].start()
    gn_ref[...] = scale * exact(hidden, d_pre, ((0,), (0,)))
    ga_ref[...] = -scale * exact(d_hidden, nodes, ((1,), (1,)))
    for copy in copies:
        copy.wait()


def feature_grads(total, adjacency, node_weight, wcat, g, rd, p, scale):
    rows, chan = g.shape
    nodes, cr = adjacency.shape[0], node_weight.shape[0]
    step = row_block(rows)
    return pl.pallas_call(
        functools.partial(feature_kernel, step, scale),
        in_specs=[VMEM] * 7,
        out_specs=[HBM] + [VMEM] * 4,
        out_shape=[
            pltpu.HBM((rows, chan), BF16),
            held((nodes, nodes), F32),
            held((cr, cr), F32),
            held((nodes, cr), F32),
            held((nodes, cr), F32),
        ],
        scratch_shapes=[
            pltpu.VMEM((rows, chan), BF16),
            pltpu.VMEM((2 * cr, 2 * cr), BF16),
            pltpu.VMEM((2 * nodes, cr), BF16),
            pltpu.SemaphoreType.DMA((rows // step,)),
        ],
        compiler_params=params(),
        cost_estimate=cost(2 * rows * 4 * 65536, rows * chan * 4 + rows * 768),
        name="feature_grads",
    )(total, adjacency, node_weight, wcat, g, rd, p)


def finish_kernel(ins, scale, *refs):
    total = refs[0][...]
    for ref in refs[1:ins]:
        total = total + ref[...]
    no_ref, dn_ref, gr_ref, gp_ref, ge_ref = refs[ins:]
    nodes, cr = no_ref.shape
    no, dn = no_ref[...], dn_ref[...]
    x_red, x_dm = total[:, :cr], total[:, cr : 2 * cr]
    cross = total[:, 2 * cr : 2 * cr + nodes]
    g_proj = total[:, 2 * cr + nodes :]
    gr_ref[...] = scale * scale * exact(cross, dn)
    gp_ref[...] = scale * exact(x_dm, no, ((1,), (1,))) + scale * scale * exact(
        x_red, dn, ((1,), (1,))
    )
    ge_ref[...] = scale * exact(g_proj, no)


def finish(parts, no, dn, scale):
    rows = parts[0].shape[0]
    nodes, cr = no.shape
    return pl.pallas_call(
        functools.partial(finish_kernel, len(parts), scale),
        in_specs=[VMEM] * (len(parts) + 2),
        out_specs=[VMEM] * 3,
        out_shape=[
            held((rows, cr), F32),
            held((rows, nodes), F32),
            held((rows, cr), F32),
        ],
        compiler_params=params(),
        cost_estimate=cost(0, rows * 4096),
        name="finish",
    )(*parts, no, dn)


def on_device(
    features, cotangent, reduce_weight, project_weight, expand_weight, adjacency, node_weight
):
    size_x, size_y, size_z, chan = features.shape
    local = size_x * size_y * size_z
    sizes = tuple(lax.axis_size(axis) for axis in AXES)
    total = local * math.prod(sizes)
    scale = 1.0 / math.sqrt(total)
    flat_x = features.transpose(0, 2, 1, 3).reshape(local, chan)
    flat_g = cotangent.transpose(0, 2, 1, 3).reshape(local, chan)
    where = {axis: lax.axis_index(axis).reshape(1).astype(jnp.int32) for axis in AXES}

    x, g, rd, p, term, wcat, adj, nw = project(
        flat_x, flat_g, reduce_weight, project_weight.T, expand_weight, adjacency, node_weight
    )
    total_term = node_sum(term)

    parts = weight_terms(x, g, rd, p, where["gy"], sizes)
    parts = [parts[0]] + [swap(part, "gy", k) for k, part in enumerate(parts) if k]
    for axis in ("gx", "gz"):
        parts = split(parts, lax.axis_size(axis), where[axis])
        parts = [parts[0]] + [swap(part, axis, k) for k, part in enumerate(parts) if k]
        if axis == "gx":
            parts = [part[None] for part in parts]

    flat_out, grad_adjacency, grad_node, no, dn = feature_grads(
        total_term, adj, nw, wcat, g, rd, p, scale
    )
    grad_reduce, grad_project, grad_expand = finish(parts, no, dn, scale)
    grad_features = flat_out.reshape(size_x, size_z, size_y, chan).transpose(0, 2, 1, 3)
    return (grad_features, grad_reduce, grad_project, grad_expand, grad_adjacency, grad_node)


def solution(mesh):
    return jax.shard_map(
        on_device,
        mesh=mesh,
        in_specs=(P("gx", "gy", "gz", None), P("gx", "gy", "gz", None), P(), P(), P(), P(), P()),
        out_specs=(
            P("gx", "gy", "gz", None),
            P(AXES, None),
            P(AXES, None),
            P(AXES, None),
            P(),
            P(),
        ),
        check_vma=False,
    )
```

```python
import functools
import math

import jax
import jax.numpy as jnp
from jax import lax
from jax.experimental import pallas as pl
from jax.experimental.pallas import tpu as pltpu
from jax.sharding import PartitionSpec as P

AXES = ("gx", "gy", "gz")
F32 = jnp.float32
BF16 = jnp.bfloat16
HBM = pl.BlockSpec(memory_space=pltpu.HBM)
VMEM = pl.BlockSpec(memory_space=pltpu.VMEM)
SMEM = pl.BlockSpec(memory_space=pltpu.SMEM)
VMEM_LIMIT = 24 * 1024 * 1024
AHEAD = 2


def exact(a, b, dims=((1,), (0,))):
    return lax.dot_general(
        a, b, (dims, ((), ())), precision=lax.Precision.HIGHEST, preferred_element_type=F32
    )


def mxu(a, b, dims=((1,), (0,))):
    return lax.dot_general(a, b, (dims, ((), ())), preferred_element_type=F32)


def held(shape, kind):
    return pltpu.VMEM(shape, kind)


def params():
    return pltpu.CompilerParams(vmem_limit_bytes=VMEM_LIMIT)


def cost(flops, nbytes):
    return pl.CostEstimate(flops=flops, bytes_accessed=nbytes, transcendentals=0)


def row_block(total):
    for size in (512, 384, 256, 128, 64, 32, 16):
        if total % size == 0:
            return size
    return total


def project_kernel(
    step, x_hbm, g_hbm, wr_hbm, wpt_hbm, we_hbm,
    x_ref, g_ref, rd_ref, p_ref, term_ref, rd_hbm, p_hbm, wcat_hbm,
    wcat_ref, wpt_ref, we_ref, small_sem, in_sem, out_sem,
):
    rows = x_ref.shape[0]
    nodes = wpt_ref.shape[0]
    cr = we_ref.shape[1]
    chunks = [pl.ds(start, step) for start in range(0, rows, step)]
    move = pltpu.make_async_copy
    loads = [
        (
            move(x_hbm.at[c], x_ref.at[c], in_sem.at[0, i]),
            move(g_hbm.at[c], g_ref.at[c], in_sem.at[1, i]),
        )
        for i, c in enumerate(chunks)
    ]
    small = [
        move(wr_hbm, wcat_ref.at[:, pl.ds(0, cr)], small_sem.at[0]),
        move(wpt_hbm, wpt_ref, small_sem.at[1]),
        move(we_hbm, we_ref, small_sem.at[2]),
    ]
    for copy in small:
        copy.start()
    for pair in loads[:AHEAD]:
        for copy in pair:
            copy.start()
    small[0].wait()
    small[1].wait()
    padded = jnp.concatenate([wpt_ref[...], jnp.zeros_like(wpt_ref)], axis=0)
    wcat_ref[:, cr:] = padded.T
    small[2].wait()
    stores = [move(wcat_ref, wcat_hbm, small_sem.at[3])]
    stores[0].start()
    for i, c in enumerate(chunks):
        loads[i][0].wait()
        both = mxu(x_ref[c], wcat_ref[...]).astype(BF16)
        loads[i][1].wait()
        if i + AHEAD < len(loads):
            for copy in loads[i + AHEAD]:
                copy.start()
        mapped = mxu(g_ref[c], we_ref[...]).astype(BF16)
        rd = jnp.concatenate([both[:, :cr], mapped], axis=1)
        proj = both[:, cr:]
        rd_ref[c] = rd
        p_ref[c] = proj
        pair = [
            move(rd_ref.at[c], rd_hbm.at[c], out_sem.at[0, i]),
            move(p_ref.at[c], p_hbm.at[c], out_sem.at[1, i]),
        ]
        for copy in pair:
            copy.start()
        stores += pair
        part = mxu(proj, rd, ((0,), (0,)))[:nodes]
        if i == 0:
            term_ref[:nodes] = part[:, :cr]
            term_ref[nodes:] = part[:, cr:]
        else:
            term_ref[:nodes] += part[:, :cr]
            term_ref[nodes:] += part[:, cr:]
    for copy in stores:
        copy.wait()


def from_hbm(*values):
    return [pltpu.with_memory_space_constraint(value, pltpu.HBM) for value in values]


def project(x, g, wr, wpt, we):
    rows, chan = x.shape
    cr, nodes = wr.shape[1], wpt.shape[0]
    step = row_block(rows)
    count = rows // step
    return pl.pallas_call(
        functools.partial(project_kernel, step),
        in_specs=[HBM] * 5,
        out_specs=[VMEM] * 5 + [HBM] * 3,
        out_shape=[
            held((rows, chan), BF16),
            held((rows, chan), BF16),
            held((rows, 2 * cr), BF16),
            held((rows, 2 * nodes), BF16),
            held((2 * nodes, cr), F32),
            pltpu.HBM((rows, 2 * cr), BF16),
            pltpu.HBM((rows, 2 * nodes), BF16),
            pltpu.HBM((chan, cr + 2 * nodes), BF16),
        ],
        scratch_shapes=[
            pltpu.VMEM((chan, cr + 2 * nodes), BF16),
            pltpu.VMEM(wpt.shape, BF16),
            pltpu.VMEM(we.shape, BF16),
            pltpu.SemaphoreType.DMA((4,)),
            pltpu.SemaphoreType.DMA((2, count)),
            pltpu.SemaphoreType.DMA((2, count)),
        ],
        compiler_params=params(),
        cost_estimate=cost(2 * rows * chan * 512, rows * chan * 4 + rows * 768),
        name="project",
    )(*from_hbm(x, g, wr, wpt, we))


def weight_kernel(step, x_ref, g_ref, rd_ref, p_ref, out_ref, sums_ref):
    rows = x_ref.shape[0]
    nodes = p_ref.shape[1] // 2
    for start in range(0, rows, step):
        c = pl.ds(start, step)
        proj = p_ref[c][:, :nodes]
        x = x_ref[c]
        pieces = (
            mxu(rd_ref[c], x, ((0,), (0,))),
            mxu(proj, x, ((0,), (0,))),
            mxu(proj, g_ref[c], ((0,), (0,))),
        )
        at = 0
        for piece in pieces:
            span = pl.ds(at, piece.shape[0])
            at += piece.shape[0]
            if start == 0:
                sums_ref[span] = piece
            else:
                sums_ref[span] += piece
    turned = sums_ref[...].T
    gy, gx, size, _ = out_ref.shape
    for i in range(gx):
        for j in range(gy):
            at = (i * gy + j) * size
            out_ref[j, i] = turned[at : at + size]


def weight_terms(x, g, rd, p, sizes):
    rows, chan = x.shape
    step = row_block(rows)
    gx, gy, gz = sizes
    width = rd.shape[1] + p.shape[1]
    return pl.pallas_call(
        functools.partial(weight_kernel, step),
        in_specs=[VMEM] * 4,
        out_specs=VMEM,
        out_shape=held((gy, gx, chan // (gx * gy), width), F32),
        scratch_shapes=[pltpu.VMEM((width, chan), F32)],
        compiler_params=params(),
        cost_estimate=cost(2 * rows * chan * 512, rows * chan * 4 + rows * 768 + width * chan * 4),
        name="weight_terms",
    )(x, g, rd, p)


def add_kernel(in_ref, out_ref):
    total = in_ref[0]
    for i in range(1, in_ref.shape[0]):
        total = total + in_ref[i]
    out_ref[...] = jnp.broadcast_to(total[None], out_ref.shape)


def add(value, repeats):
    return pl.pallas_call(
        add_kernel,
        in_specs=[VMEM],
        out_specs=VMEM,
        out_shape=held((repeats, *value.shape[1:]), F32),
        compiler_params=params(),
        cost_estimate=cost(0, 8 * value.size),
        name="add",
    )(value)


def exchange(value, axis):
    return lax.all_to_all(value, axis, 0, 0, tiled=True)


def node_sum(term):
    size = {axis: lax.axis_size(axis) for axis in AXES}
    parts = term.reshape(size["gy"], -1, term.shape[1])
    parts = exchange(parts, "gy")
    for axis in ("gx", "gz"):
        parts = exchange(add(parts, size[axis]), axis)
    return exchange(add(parts, size["gy"]), "gy").reshape(term.shape)


def weight_sums(parts):
    size = {axis: lax.axis_size(axis) for axis in AXES}
    parts = add(exchange(parts, "gy"), 1)[0]
    parts = add(exchange(parts, "gx"), 1)[0]
    return exchange(parts.reshape(size["gz"], -1, parts.shape[1]), "gz")


def feature_kernel(
    step, scale, total_ref, adj_hbm, nw_hbm, wcat_hbm, g_hbm, rd_hbm, p_hbm,
    out_hbm, ga_ref, gn_ref, no_ref, dn_ref,
    adj_ref, nw_ref, wcat_ref, g_ref, rd_ref, p_ref, out_ref, mix_ref, dnb_ref,
    small_sem, in_sem, out_sem,
):
    nodes_n, cr = no_ref.shape
    rows = g_ref.shape[0]
    chunks = [pl.ds(start, step) for start in range(0, rows, step)]
    move = pltpu.make_async_copy
    small = [
        move(adj_hbm, adj_ref, small_sem.at[0]),
        move(nw_hbm, nw_ref, small_sem.at[1]),
        move(wcat_hbm, wcat_ref, small_sem.at[2]),
    ]
    loads = [
        [
            move(src.at[c], dst.at[c], in_sem.at[k, i])
            for k, (src, dst) in enumerate(((rd_hbm, rd_ref), (p_hbm, p_ref), (g_hbm, g_ref)))
        ]
        for i, c in enumerate(chunks)
    ]
    for copy in small:
        copy.start()
    for group in loads[:AHEAD]:
        for copy in group:
            copy.start()
    small[0].wait()
    small[1].wait()
    adj, nw = adj_ref[...], nw_ref[...]
    nodes = scale * total_ref[:nodes_n]
    d_node_out = total_ref[nodes_n:]
    hidden = nodes - exact(adj, nodes)
    pre = exact(hidden, nw)
    node_out = jnp.maximum(pre, 0.0).astype(BF16)
    d_pre = jnp.where(pre > 0.0, d_node_out, 0.0)
    d_hidden = exact(d_pre, nw, ((1,), (1,)))
    d_nodes = d_hidden - exact(adj, d_hidden, ((0,), (0,)))
    dn = d_nodes.astype(BF16)
    no_ref[...] = node_out.astype(F32)
    dn_ref[...] = dn.astype(F32)
    dnb_ref[:nodes_n] = dn
    dnb_ref[nodes_n:] = jnp.zeros((nodes_n, cr), BF16)
    blank = jnp.zeros((cr, cr), BF16)
    zero = jnp.zeros((nodes_n, cr), F32)
    mix_ref[:cr, :cr] = jnp.concatenate([dn.astype(F32), zero], axis=0).T.astype(BF16)
    mix_ref[cr:, :cr] = blank
    mix_ref[:cr, cr:] = blank
    mix_ref[cr:, cr:] = jnp.concatenate([node_out.astype(F32), zero], axis=0).T.astype(BF16)
    small[2].wait()
    copies = []
    for i, c in enumerate(chunks):
        for copy in loads[i]:
            copy.wait()
        if i + AHEAD < len(loads):
            for copy in loads[i + AHEAD]:
                copy.start()
        mixed = mxu(rd_ref[c], mix_ref[...])
        d_proj = (mixed[:, cr:] + scale * mixed[:, :cr]).astype(BF16)
        d_red = (scale * mxu(p_ref[c], dnb_ref[...])).astype(BF16)
        both = jnp.concatenate([d_red, d_proj], axis=1)
        out = g_ref[c].astype(F32) + mxu(both, wcat_ref[...], ((1,), (1,)))
        out_ref[c] = out.astype(BF16)
        copies.append(move(out_ref.at[c], out_hbm.at[c], out_sem.at[i]))
        copies[-1].start()
    gn_ref[...] = scale * exact(hidden, d_pre, ((0,), (0,)))
    ga_ref[...] = -scale * exact(d_hidden, nodes, ((1,), (1,)))
    for copy in copies:
        copy.wait()


def feature_grads(total, adjacency, node_weight, wcat, g, rd, p, scale):
    rows, chan = g.shape
    nodes, cr = adjacency.shape[0], node_weight.shape[0]
    step = row_block(rows)
    count = rows // step
    loaded = (adjacency, node_weight, wcat, g, rd, p)
    return pl.pallas_call(
        functools.partial(feature_kernel, step, scale),
        in_specs=[VMEM] + [HBM] * 6,
        out_specs=[HBM] + [VMEM] * 4,
        out_shape=[
            pltpu.HBM((rows, chan), BF16),
            jax.ShapeDtypeStruct((nodes, nodes), F32),
            jax.ShapeDtypeStruct((cr, cr), F32),
            held((nodes, cr), F32),
            held((nodes, cr), F32),
        ],
        scratch_shapes=[pltpu.VMEM(value.shape, value.dtype) for value in loaded]
        + [
            pltpu.VMEM((rows, chan), BF16),
            pltpu.VMEM((2 * cr, 2 * cr), BF16),
            pltpu.VMEM((2 * nodes, cr), BF16),
            pltpu.SemaphoreType.DMA((3,)),
            pltpu.SemaphoreType.DMA((3, count)),
            pltpu.SemaphoreType.DMA((count,)),
        ],
        compiler_params=params(),
        cost_estimate=cost(2 * rows * 4 * 65536, rows * chan * 4 + rows * 768),
        name="feature_grads",
    )(total, *from_hbm(*loaded))


def finish_kernel(scale, parts_ref, no_ref, dn_ref, gr_ref, gp_ref, ge_ref):
    total = parts_ref[0]
    for i in range(1, parts_ref.shape[0]):
        total = total + parts_ref[i]
    nodes, cr = no_ref.shape
    no, dn = no_ref[...], dn_ref[...]
    x_red, x_dm = total[:, :cr], total[:, cr : 2 * cr]
    cross = total[:, 2 * cr : 2 * cr + nodes]
    g_proj = total[:, 2 * cr + nodes :]
    gr_ref[...] = scale * scale * exact(cross, dn)
    gp_ref[...] = scale * exact(x_dm, no, ((1,), (1,))) + scale * scale * exact(
        x_red, dn, ((1,), (1,))
    )
    ge_ref[...] = scale * exact(g_proj, no)


def finish(parts, no, dn, scale):
    rows = parts.shape[1]
    nodes, cr = no.shape
    return pl.pallas_call(
        functools.partial(finish_kernel, scale),
        in_specs=[VMEM] * 3,
        out_specs=[VMEM] * 3,
        out_shape=[
            jax.ShapeDtypeStruct((rows, cr), F32),
            jax.ShapeDtypeStruct((rows, nodes), F32),
            jax.ShapeDtypeStruct((rows, cr), F32),
        ],
        compiler_params=params(),
        cost_estimate=cost(0, rows * 4096),
        name="finish",
    )(parts, no, dn)


def on_device(
    features, cotangent, reduce_weight, project_weight, expand_weight, adjacency, node_weight
):
    size_x, size_y, size_z, chan = features.shape
    local = size_x * size_y * size_z
    sizes = tuple(lax.axis_size(axis) for axis in AXES)
    total = local * math.prod(sizes)
    scale = 1.0 / math.sqrt(total)
    flat_x = features.transpose(0, 2, 1, 3).reshape(local, chan)
    flat_g = cotangent.transpose(0, 2, 1, 3).reshape(local, chan)

    x, g, rd, p, term, rd_far, p_far, wcat = project(
        flat_x, flat_g, reduce_weight, project_weight.T, expand_weight
    )
    node_total = node_sum(term)
    parts = weight_sums(weight_terms(x, g, rd, p, sizes))

    flat_out, grad_adjacency, grad_node, no, dn = feature_grads(
        node_total, adjacency, node_weight, wcat, flat_g, rd_far, p_far, scale
    )
    grad_reduce, grad_project, grad_expand = finish(parts, no, dn, scale)
    grad_features = flat_out.reshape(size_x, size_z, size_y, chan).transpose(0, 2, 1, 3)
    return (grad_features, grad_reduce, grad_project, grad_expand, grad_adjacency, grad_node)


def solution(mesh):
    return jax.shard_map(
        on_device,
        mesh=mesh,
        in_specs=(P("gx", "gy", "gz", None), P("gx", "gy", "gz", None), P(), P(), P(), P(), P()),
        out_specs=(
            P("gx", "gy", "gz", None),
            P(AXES, None),
            P(AXES, None),
            P(AXES, None),
            P(),
            P(),
        ),
        check_vma=False,
    )
```

```python
import functools
import math

import jax
import jax.numpy as jnp
from jax import lax
from jax.experimental import pallas as pl
from jax.experimental.pallas import tpu as pltpu
from jax.sharding import PartitionSpec as P

AXES = ("gx", "gy", "gz")
F32 = jnp.float32
BF16 = jnp.bfloat16
HBM = pl.BlockSpec(memory_space=pltpu.HBM)
VMEM = pl.BlockSpec(memory_space=pltpu.VMEM)
SMEM = pl.BlockSpec(memory_space=pltpu.SMEM)
VMEM_LIMIT = 24 * 1024 * 1024


def exact(a, b, dims=((1,), (0,))):
    return lax.dot_general(
        a, b, (dims, ((), ())), precision=lax.Precision.HIGHEST, preferred_element_type=F32
    )


def mxu(a, b, dims=((1,), (0,))):
    return lax.dot_general(a, b, (dims, ((), ())), preferred_element_type=F32)


def params():
    return pltpu.CompilerParams(vmem_limit_bytes=VMEM_LIMIT)


def cost(flops, nbytes):
    return pl.CostEstimate(flops=flops, bytes_accessed=nbytes, transcendentals=0)


def whole(shape):
    return pl.BlockSpec(shape, lambda *_: (0,) * len(shape))


def in_hbm(*values):
    return [pltpu.with_memory_space_constraint(value, pltpu.HBM) for value in values]


def row_block(total):
    for size in (512, 384, 256, 128, 64, 32, 16):
        if total % size == 0:
            return size
    return total


class Cube:
    def __init__(self, mesh):
        self.size = {axis: mesh.shape[axis] for axis in AXES}
        self.count = math.prod(self.size.values())
        stride = {"gx": self.size["gy"] * self.size["gz"], "gy": self.size["gz"], "gz": 1}
        bits = {
            axis: [stride[axis] << k for k in range(self.size[axis].bit_length() - 1)] for axis in AXES
        }
        self.core = bits["gy"][0]
        rest = bits["gx"] + bits["gy"][1:] + bits["gz"]
        self.orders = [rest, rest]
        if len(bits["gx"]) == 2:
            self.orders = [rest, [rest[1], rest[0]] + rest[2:]]
        self.rounds = len(rest)

    def side(self, device):
        return 1 if device & self.core else 0

    def traced_side(self, device):
        return lax.bitwise_and(lax.div(device, jnp.int32(self.core)), jnp.int32(1))

    def swap(self, value, level):
        masks = [self.core] * 2 if level < 0 else [order[level] for order in self.orders]
        pairs = [(d, d ^ masks[self.side(d)]) for d in range(self.count)]
        return lax.ppermute(value, AXES, pairs)

    def masks(self, side):
        order = self.orders[side]
        last = len(order) - 1
        return [
            sum(order[level] for level in range(len(order)) if j >> (last - level) & 1)
            for j in range(1 << len(order))
        ]


def thirds(value, weight):
    rows = value.shape[0]
    high = value.astype(BF16)
    rest = value - high.astype(F32)
    middle = rest.astype(BF16)
    low = (rest - middle.astype(F32)).astype(BF16)
    out = mxu(jnp.concatenate([high, middle, low], axis=0), weight)
    return (out[2 * rows :] + out[rows : 2 * rows]) + out[:rows]


def gather_kernel(
    cube, where_ref, x_ref, g_ref, wr_ref, wpt_ref, we_ref,
    rd_ref, p_ref, wcat_ref, keep_ref, send_ref, *rest,
):
    sorted_here = len(rest) == 6
    if sorted_here:
        kept_ref, sent_ref, sums_ref, turned_ref, term_ref, cat_ref = rest
    else:
        turned_ref, sums_ref, term_ref, cat_ref = rest
    cr = wr_ref.shape[1]
    nodes = wpt_ref.shape[0]
    wide = 2 * cr

    @pl.when(pl.program_id(0) == 0)
    def _():
        cat_ref[:, :cr] = wr_ref[...]
        padded = jnp.concatenate([wpt_ref[...], jnp.zeros_like(wpt_ref)], axis=0)
        cat_ref[:, cr:] = padded.T
        wcat_ref[...] = cat_ref[...]
        sums_ref[...] = jnp.zeros_like(sums_ref)

    x, g = x_ref[...], g_ref[...]
    both = mxu(x, cat_ref[...]).astype(BF16)
    mapped = mxu(g, we_ref[...]).astype(BF16)
    rd = jnp.concatenate([both[:, :cr], mapped], axis=1)
    rd_ref[...] = rd
    p_ref[...] = both[:, cr:]
    proj = both[:, cr : cr + nodes]
    sums_ref[:wide] += mxu(rd, x, ((0,), (0,)))
    sums_ref[wide : wide + nodes] += mxu(proj, x, ((0,), (0,)))
    sums_ref[wide + nodes :] += mxu(proj, g, ((0,), (0,)))

    @pl.when(pl.program_id(0) == pl.num_programs(0) - 1)
    def _():
        term_ref[0] = thirds(sums_ref[wide : wide + nodes], wr_ref[...])
        term_ref[1] = thirds(sums_ref[wide + nodes :], we_ref[...])
        me = where_ref[0]
        side = cube.traced_side(me)
        keep_ref[...] = term_ref[side]
        send_ref[...] = term_ref[1 - side]
        turned_ref[...] = sums_ref[...].T
        if sorted_here:
            size = kept_ref.shape[1]
            mine = [jnp.where(side == 0, a, b) for a, b in zip(cube.masks(0), cube.masks(1))]
            other = [jnp.where(side == 0, b, a) for a, b in zip(cube.masks(0), cube.masks(1))]
            for masks, base, out_ref in ((mine, me, kept_ref), (other, me ^ cube.core, sent_ref)):
                for j, mask in enumerate(masks):
                    at = pl.multiple_of((base ^ mask) * size, size)
                    out_ref[j] = turned_ref[pl.ds(at, size), :]


def gather(cube, where, x, g, wr, wpt, we):
    rows, chan = x.shape
    cr, nodes = wr.shape[1], wpt.shape[0]
    step = row_block(rows)
    width = 2 * cr + 2 * nodes
    half = cube.count // 2
    size = chan // cube.count
    sorted_here = size % 8 == 0
    rowspec = lambda wide: pl.BlockSpec((step, wide), lambda i: (i, 0))
    outs = [
        (rowspec(2 * cr), pltpu.HBM((rows, 2 * cr), BF16)),
        (rowspec(2 * nodes), pltpu.HBM((rows, 2 * nodes), BF16)),
        (whole((chan, cr + 2 * nodes)), pltpu.HBM((chan, cr + 2 * nodes), BF16)),
        (VMEM, pltpu.VMEM((nodes, cr), F32)),
        (VMEM, pltpu.VMEM((nodes, cr), F32)),
    ]
    scratch = [pltpu.VMEM((width, chan), F32)]
    if sorted_here:
        outs += [(VMEM, pltpu.VMEM((half, size, width), F32))] * 2
        scratch += [pltpu.VMEM((chan, width), F32)]
    else:
        outs += [(VMEM, jax.ShapeDtypeStruct((chan, width), F32))]
    scratch += [pltpu.VMEM((2, nodes, cr), F32), pltpu.VMEM((chan, cr + 2 * nodes), BF16)]
    rd, p, wcat, keep, send, *blocks = pl.pallas_call(
        functools.partial(gather_kernel, cube),
        grid=(rows // step,),
        in_specs=[SMEM, rowspec(chan), rowspec(chan), whole(wr.shape), whole(wpt.shape), whole(we.shape)],
        out_specs=[spec for spec, _ in outs],
        out_shape=[shape for _, shape in outs],
        scratch_shapes=scratch,
        compiler_params=params(),
        cost_estimate=cost(2 * rows * chan * 1024, rows * chan * 4 + rows * 768),
        name="gather",
    )(where, *in_hbm(x, g, wr, wpt, we))
    if not sorted_here:
        me = where[0]
        side = cube.traced_side(me)
        table = jnp.array([cube.masks(0), cube.masks(1)], jnp.int32)
        cut = blocks[0].reshape(cube.count, size, width)
        blocks = [cut[me ^ table[side]], cut[me ^ cube.core ^ table[1 - side]]]
    return rd, p, wcat, keep, send, blocks[0], blocks[1]


def add_kernel(a_ref, b_ref, out_ref):
    out_ref[...] = a_ref[...] + b_ref[...]


def add(a, b):
    return pl.pallas_call(
        add_kernel,
        in_specs=[VMEM] * 2,
        out_specs=VMEM,
        out_shape=pltpu.VMEM(a.shape, F32),
        compiler_params=params(),
        cost_estimate=cost(a.size, 12 * a.size),
        name="add",
    )(a, b)


def halve_kernel(a_ref, b_ref, keep_ref, send_ref):
    half = keep_ref.shape[0]
    keep_ref[...] = a_ref[:half] + b_ref[:half]
    send_ref[...] = a_ref[half:] + b_ref[half:]


def halve(a, b):
    shape = (a.shape[0] // 2, *a.shape[1:])
    return pl.pallas_call(
        halve_kernel,
        in_specs=[VMEM] * 2,
        out_specs=[VMEM] * 2,
        out_shape=[pltpu.VMEM(shape, F32)] * 2,
        compiler_params=params(),
        cost_estimate=cost(a.size, 12 * a.size),
        name="halve",
    )(a, b)


def feature_kernel(
    step, scale, cube, where_ref, mine_ref, other_ref, adj_hbm, nw_hbm, wcat_hbm, rd_hbm, p_hbm, g_hbm,
    out_hbm, ga_ref, gn_ref, no_ref, dn_ref,
    adj_ref, nw_ref, wcat_ref, rd_ref, p_ref, g_ref, out_ref, mix_ref, dnb_ref,
    small_sem, in_sem, out_sem,
):
    nodes_n, cr = no_ref.shape
    rows = g_ref.shape[0]
    chunks = [pl.ds(start, step) for start in range(0, rows, step)]
    move = pltpu.make_async_copy
    small = [
        move(adj_hbm, adj_ref, small_sem.at[0]),
        move(nw_hbm, nw_ref, small_sem.at[1]),
        move(wcat_hbm, wcat_ref, small_sem.at[2]),
    ]
    loads = [
        [
            move(src.at[c], dst.at[c], in_sem.at[k, i])
            for k, (src, dst) in enumerate(((rd_hbm, rd_ref), (p_hbm, p_ref), (g_hbm, g_ref)))
        ]
        for i, c in enumerate(chunks)
    ]
    for copy in small:
        copy.start()
    for group in loads:
        for copy in group:
            copy.start()
    first = cube.traced_side(where_ref[0]) == 0
    mine, other = mine_ref[...], other_ref[...]
    nodes = scale * jnp.where(first, mine, other)
    d_node_out = jnp.where(first, other, mine)
    small[0].wait()
    small[1].wait()
    adj, nw = adj_ref[...], nw_ref[...]
    hidden = nodes - exact(adj, nodes)
    pre = exact(hidden, nw)
    node_out = jnp.maximum(pre, 0.0).astype(BF16)
    d_pre = jnp.where(pre > 0.0, d_node_out, 0.0)
    d_hidden = exact(d_pre, nw, ((1,), (1,)))
    d_nodes = d_hidden - exact(adj, d_hidden, ((0,), (0,)))
    dn = d_nodes.astype(BF16)
    no_ref[...] = node_out.astype(F32)
    dn_ref[...] = dn.astype(F32)
    dnb_ref[:nodes_n] = dn
    dnb_ref[nodes_n:] = jnp.zeros((nodes_n, cr), BF16)
    blank = jnp.zeros((cr, cr), BF16)
    zero = jnp.zeros((nodes_n, cr), F32)
    mix_ref[:cr, :cr] = jnp.concatenate([dn.astype(F32), zero], axis=0).T.astype(BF16)
    mix_ref[cr:, :cr] = blank
    mix_ref[:cr, cr:] = blank
    mix_ref[cr:, cr:] = jnp.concatenate([node_out.astype(F32), zero], axis=0).T.astype(BF16)
    small[2].wait()
    copies = []
    for i, c in enumerate(chunks):
        for copy in loads[i]:
            copy.wait()
        mixed = mxu(rd_ref[c], mix_ref[...])
        d_proj = (mixed[:, cr:] + scale * mixed[:, :cr]).astype(BF16)
        d_red = (scale * mxu(p_ref[c], dnb_ref[...])).astype(BF16)
        both = jnp.concatenate([d_red, d_proj], axis=1)
        out = g_ref[c].astype(F32) + mxu(both, wcat_ref[...], ((1,), (1,)))
        out_ref[c] = out.astype(BF16)
        copies.append(move(out_ref.at[c], out_hbm.at[c], out_sem.at[i]))
        copies[-1].start()
    gn_ref[...] = scale * exact(hidden, d_pre, ((0,), (0,)))
    ga_ref[...] = -scale * exact(d_hidden, nodes, ((1,), (1,)))
    for copy in copies:
        copy.wait()


def feature_grads(cube, where, mine, other, adjacency, node_weight, wcat, rd, p, g, scale):
    rows, chan = g.shape
    nodes, cr = adjacency.shape[0], node_weight.shape[0]
    step = row_block(rows)
    count = rows // step
    loaded = (adjacency, node_weight, wcat, rd, p, g)
    return pl.pallas_call(
        functools.partial(feature_kernel, step, scale, cube),
        in_specs=[SMEM, VMEM, VMEM] + [HBM] * 6,
        out_specs=[HBM] + [VMEM] * 4,
        out_shape=[
            pltpu.HBM((rows, chan), BF16),
            jax.ShapeDtypeStruct((nodes, nodes), F32),
            jax.ShapeDtypeStruct((cr, cr), F32),
            pltpu.VMEM((nodes, cr), F32),
            pltpu.VMEM((nodes, cr), F32),
        ],
        scratch_shapes=[pltpu.VMEM(value.shape, value.dtype) for value in loaded]
        + [
            pltpu.VMEM((rows, chan), BF16),
            pltpu.VMEM((2 * cr, 2 * cr), BF16),
            pltpu.VMEM((2 * nodes, cr), BF16),
            pltpu.SemaphoreType.DMA((3,)),
            pltpu.SemaphoreType.DMA((3, count)),
            pltpu.SemaphoreType.DMA((count,)),
        ],
        compiler_params=params(),
        cost_estimate=cost(2 * rows * 4 * 65536, rows * chan * 4 + rows * 768),
        name="feature_grads",
    )(where, mine, other, *in_hbm(*loaded))


def finish_kernel(scale, kept_ref, got_ref, no_ref, dn_ref, gr_ref, gp_ref, ge_ref):
    total = kept_ref[0] + got_ref[0]
    nodes, cr = no_ref.shape
    no, dn = no_ref[...], dn_ref[...]
    x_red, x_dm = total[:, :cr], total[:, cr : 2 * cr]
    cross = total[:, 2 * cr : 2 * cr + nodes]
    g_proj = total[:, 2 * cr + nodes :]
    gr_ref[...] = scale * scale * exact(cross, dn)
    gp_ref[...] = scale * exact(x_dm, no, ((1,), (1,))) + scale * scale * exact(
        x_red, dn, ((1,), (1,))
    )
    ge_ref[...] = scale * exact(g_proj, no)


def finish(kept, got, no, dn, scale):
    rows = kept.shape[1]
    nodes, cr = no.shape
    return pl.pallas_call(
        functools.partial(finish_kernel, scale),
        in_specs=[VMEM] * 4,
        out_specs=[VMEM] * 3,
        out_shape=[
            jax.ShapeDtypeStruct((rows, cr), F32),
            jax.ShapeDtypeStruct((rows, nodes), F32),
            jax.ShapeDtypeStruct((rows, cr), F32),
        ],
        compiler_params=params(),
        cost_estimate=cost(0, rows * 4096),
        name="finish",
    )(kept, got, no, dn)


def on_device(
    cube, features, cotangent, reduce_weight, project_weight, expand_weight, adjacency, node_weight
):
    size_x, size_y, size_z, chan = features.shape
    local = size_x * size_y * size_z
    scale = 1.0 / math.sqrt(local * cube.count)
    flat_x = features.transpose(0, 2, 1, 3).reshape(local, chan)
    flat_g = cotangent.transpose(0, 2, 1, 3).reshape(local, chan)
    me = lax.axis_index(AXES).astype(jnp.int32)
    where = me.reshape(1)

    rd, p, wcat, keep, send, kept, sent = gather(
        cube, where, flat_x, flat_g, reduce_weight, project_weight.T, expand_weight
    )
    mine = add(keep, cube.swap(send, -1))
    got = cube.swap(sent, -1)
    for level in range(cube.rounds):
        mine_got = cube.swap(mine, level)
        kept, sent = halve(kept, got)
        got = cube.swap(sent, level)
        mine = add(mine, mine_got)
    other = cube.swap(mine, -1)

    flat_out, grad_adjacency, grad_node, no, dn = feature_grads(
        cube, where, mine, other, adjacency, node_weight, wcat, rd, p, flat_g, scale
    )
    grad_reduce, grad_project, grad_expand = finish(kept, got, no, dn, scale)
    grad_features = flat_out.reshape(size_x, size_z, size_y, chan).transpose(0, 2, 1, 3)
    return (grad_features, grad_reduce, grad_project, grad_expand, grad_adjacency, grad_node)


def solution(mesh):
    return jax.shard_map(
        functools.partial(on_device, Cube(mesh)),
        mesh=mesh,
        in_specs=(P("gx", "gy", "gz", None), P("gx", "gy", "gz", None), P(), P(), P(), P(), P()),
        out_specs=(
            P("gx", "gy", "gz", None),
            P(AXES, None),
            P(AXES, None),
            P(AXES, None),
            P(),
            P(),
        ),
        check_vma=False,
    )
```

```python
import functools
import math

import jax
import jax.numpy as jnp
from jax import lax
from jax.experimental import pallas as pl
from jax.experimental.pallas import tpu as pltpu
from jax.sharding import PartitionSpec as P

AXES = ("gx", "gy", "gz")
F32 = jnp.float32
BF16 = jnp.bfloat16
HBM = pl.BlockSpec(memory_space=pltpu.HBM)
VMEM = pl.BlockSpec(memory_space=pltpu.VMEM)
SMEM = pl.BlockSpec(memory_space=pltpu.SMEM)
VMEM_LIMIT = 24 * 1024 * 1024


def exact(a, b, dims=((1,), (0,))):
    return lax.dot_general(
        a, b, (dims, ((), ())), precision=lax.Precision.HIGHEST, preferred_element_type=F32
    )


def mxu(a, b, dims=((1,), (0,))):
    return lax.dot_general(a, b, (dims, ((), ())), preferred_element_type=F32)


def params():
    return pltpu.CompilerParams(vmem_limit_bytes=VMEM_LIMIT)


def cost(flops, nbytes):
    return pl.CostEstimate(flops=flops, bytes_accessed=nbytes, transcendentals=0)


def whole(shape):
    return pl.BlockSpec(shape, lambda *_: (0,) * len(shape))


def in_hbm(*values):
    return [pltpu.with_memory_space_constraint(value, pltpu.HBM) for value in values]


def row_block(total, largest):
    for size in (768, 512, 384, 256, 128, 64, 32, 16):
        if size <= largest and total % size == 0:
            return size
    return total


class Cube:
    def __init__(self, mesh):
        self.size = {axis: mesh.shape[axis] for axis in AXES}
        self.count = math.prod(self.size.values())
        stride = {"gx": self.size["gy"] * self.size["gz"], "gy": self.size["gz"], "gz": 1}
        bits = {
            axis: [stride[axis] << k for k in range(self.size[axis].bit_length() - 1)] for axis in AXES
        }
        self.core = bits["gy"][0]
        rest = bits["gx"] + bits["gy"][1:] + bits["gz"]
        self.orders = [rest, rest]
        if len(bits["gx"]) == 2:
            self.orders = [rest, [rest[1], rest[0]] + rest[2:]]
        self.rounds = len(rest)

    def side(self, device):
        return 1 if device & self.core else 0

    def traced_side(self, device):
        return lax.bitwise_and(lax.div(device, jnp.int32(self.core)), jnp.int32(1))

    def swap(self, value, level):
        masks = [self.core] * 2 if level < 0 else [order[level] for order in self.orders]
        pairs = [(d, d ^ masks[self.side(d)]) for d in range(self.count)]
        return lax.ppermute(value, AXES, pairs)

    def masks(self, side):
        order = self.orders[side]
        last = len(order) - 1
        return [
            sum(order[level] for level in range(len(order)) if j >> (last - level) & 1)
            for j in range(1 << len(order))
        ]


def gather_kernel(
    cube, sorted_here, where_ref, x_ref, g_ref, wr_ref, wpt_ref, we_ref, rd_ref, p_ref, wcat_ref, *rest
):
    if sorted_here:
        kept_ref, sent_ref, sums_ref, turned_ref, term_ref, cat_ref = rest
    else:
        keep_ref, send_ref, turned_ref, sums_ref, term_ref, cat_ref = rest
    cr = wr_ref.shape[1]
    nodes = wpt_ref.shape[0]
    wide = 2 * cr

    @pl.when(pl.program_id(0) == 0)
    def _():
        cat_ref[:, :cr] = wr_ref[...]
        padded = jnp.concatenate([wpt_ref[...], jnp.zeros_like(wpt_ref)], axis=0)
        cat_ref[:, cr:] = padded.T
        wcat_ref[...] = cat_ref[...]
        sums_ref[...] = jnp.zeros_like(sums_ref)
        term_ref[...] = jnp.zeros_like(term_ref)

    x, g = x_ref[...], g_ref[...]
    both = mxu(x, cat_ref[...]).astype(BF16)
    mapped = mxu(g, we_ref[...]).astype(BF16)
    rd = jnp.concatenate([both[:, :cr], mapped], axis=1)
    rd_ref[...] = rd
    p_ref[...] = both[:, cr:]
    turned = jnp.concatenate([rd, both[:, cr:]], axis=1).T
    proj = turned[wide : wide + nodes]
    sums_ref[: wide + nodes] += mxu(turned[: wide + nodes], x)
    sums_ref[wide + nodes :] += mxu(proj, g)
    term = mxu(proj, rd)
    term_ref[0] += term[:, :cr]
    term_ref[1] += term[:, cr:]

    @pl.when(pl.program_id(0) == pl.num_programs(0) - 1)
    def _():
        me = where_ref[0]
        side = cube.traced_side(me)
        turned_ref[...] = sums_ref[...].T
        if not sorted_here:
            keep_ref[...] = term_ref[side]
            send_ref[...] = term_ref[1 - side]
        else:
            kept_ref[:nodes] = term_ref[side]
            sent_ref[:nodes] = term_ref[1 - side]
            size = turned_ref.shape[0] // cube.count
            mine = [jnp.where(side == 0, a, b) for a, b in zip(cube.masks(0), cube.masks(1))]
            other = [jnp.where(side == 0, b, a) for a, b in zip(cube.masks(0), cube.masks(1))]
            for masks, base, out_ref in ((mine, me, kept_ref), (other, me ^ cube.core, sent_ref)):
                to = nodes
                for mask in masks:
                    at = pl.multiple_of((base ^ mask) * size, size)
                    block = turned_ref[pl.ds(at, size), :]
                    for lane in range(0, block.shape[1], cr):
                        out_ref[to : to + size] = block[:, lane : lane + cr]
                        to += size


def gather(cube, where, x, g, wr, wpt, we):
    rows, chan = x.shape
    cr, nodes = wr.shape[1], wpt.shape[0]
    step = row_block(rows, 768)
    width = 2 * cr + 2 * nodes
    half = cube.count // 2
    size = chan // cube.count
    sorted_here = size % 8 == 0
    rowspec = lambda wide: pl.BlockSpec((step, wide), lambda i: (i, 0))
    outs = [
        (rowspec(2 * cr), pltpu.HBM((rows, 2 * cr), BF16)),
        (rowspec(2 * nodes), pltpu.HBM((rows, 2 * nodes), BF16)),
        (whole((chan, cr + 2 * nodes)), pltpu.HBM((chan, cr + 2 * nodes), BF16)),
    ]
    scratch = [pltpu.VMEM((width, chan), F32)]
    if sorted_here:
        outs += [(VMEM, pltpu.VMEM((nodes + half * size * width // cr, cr), F32))] * 2
        scratch += [pltpu.VMEM((chan, width), F32)]
    else:
        outs += [(VMEM, jax.ShapeDtypeStruct((nodes, cr), F32))] * 2
        outs += [(VMEM, jax.ShapeDtypeStruct((chan, width), F32))]
    scratch += [pltpu.VMEM((2, nodes, cr), F32), pltpu.VMEM((chan, cr + 2 * nodes), BF16)]
    rd, p, wcat, kept, sent, *sums = pl.pallas_call(
        functools.partial(gather_kernel, cube, sorted_here),
        grid=(rows // step,),
        in_specs=[SMEM, rowspec(chan), rowspec(chan), whole(wr.shape), whole(wpt.shape), whole(we.shape)],
        out_specs=[spec for spec, _ in outs],
        out_shape=[shape for _, shape in outs],
        scratch_shapes=scratch,
        compiler_params=params(),
        cost_estimate=cost(2 * rows * chan * 1024, rows * chan * 4 + rows * 768),
        name="gather",
    )(where, *in_hbm(x, g, wr, wpt, we))
    if not sorted_here:
        side = cube.traced_side(where[0])
        table = jnp.array([cube.masks(0), cube.masks(1)], jnp.int32)
        cut = sums[0].reshape(cube.count, size, width // cr, cr).transpose(0, 2, 1, 3)
        lay = lambda head, index: jnp.concatenate([head, cut[index].reshape(-1, cr)])
        kept = lay(kept, where[0] ^ table[side])
        sent = lay(sent, where[0] ^ cube.core ^ table[1 - side])
    return rd, p, wcat, kept, sent


def step_kernel(head, a_ref, b_ref, keep_ref, send_ref):
    half = send_ref.shape[0] - head
    nodes = a_ref[:head] + b_ref[:head]
    send_ref[:head] = nodes
    if half:
        keep_ref[:head] = nodes
        keep_ref[head:] = a_ref[head : head + half] + b_ref[head : head + half]
        send_ref[head:] = a_ref[head + half :] + b_ref[head + half :]
    else:
        keep_ref[...] = a_ref[head:] + b_ref[head:]


def step(head, last, a, b):
    rest, lanes = a.shape[0] - head, a.shape[1]
    shapes = (rest, head) if last else (head + rest // 2,) * 2
    return pl.pallas_call(
        functools.partial(step_kernel, head),
        in_specs=[VMEM] * 2,
        out_specs=[VMEM] * 2,
        out_shape=[pltpu.VMEM((size, lanes), F32) for size in shapes],
        compiler_params=params(),
        cost_estimate=cost(a.size, 12 * a.size),
        name="step",
    )(a, b)


def feature_kernel(
    step, scale, cube, where_ref, mine_ref, other_ref, sums_ref,
    adj_hbm, nw_hbm, wcat_hbm, rd_hbm, p_hbm, g_hbm,
    out_hbm, gr_ref, gp_ref, ge_ref, ga_ref, gn_ref,
    adj_ref, nw_ref, wcat_ref, rd_ref, p_ref, g_ref, out_ref, mix_ref, dnb_ref,
    small_sem, in_sem, out_sem,
):
    nodes_n, cr = mine_ref.shape
    rows = g_ref.shape[0]
    chunks = [pl.ds(start, step) for start in range(0, rows, step)]
    move = pltpu.make_async_copy
    small = [
        move(adj_hbm, adj_ref, small_sem.at[0]),
        move(nw_hbm, nw_ref, small_sem.at[1]),
        move(wcat_hbm, wcat_ref, small_sem.at[2]),
    ]
    loads = [
        [
            move(src.at[c], dst.at[c], in_sem.at[k, i])
            for k, (src, dst) in enumerate(((rd_hbm, rd_ref), (p_hbm, p_ref), (g_hbm, g_ref)))
        ]
        for i, c in enumerate(chunks)
    ]
    for copy in small:
        copy.start()
    for group in loads:
        for copy in group:
            copy.start()
    first = cube.traced_side(where_ref[0]) == 0
    mine, other = mine_ref[...], other_ref[...]
    nodes = scale * jnp.where(first, mine, other)
    d_node_out = jnp.where(first, other, mine)
    small[0].wait()
    small[1].wait()
    adj, nw = adj_ref[...], nw_ref[...]
    hidden = nodes - exact(adj, nodes)
    pre = exact(hidden, nw)
    node_out = jnp.maximum(pre, 0.0).astype(BF16)
    d_pre = jnp.where(pre > 0.0, d_node_out, 0.0)
    d_hidden = exact(d_pre, nw, ((1,), (1,)))
    d_nodes = d_hidden - exact(adj, d_hidden, ((0,), (0,)))
    dn = d_nodes.astype(BF16)
    dnb_ref[:nodes_n] = dn
    dnb_ref[nodes_n:] = jnp.zeros((nodes_n, cr), BF16)
    blank = jnp.zeros((cr, cr), BF16)
    zero = jnp.zeros((nodes_n, cr), F32)
    mix_ref[:cr, :cr] = jnp.concatenate([dn.astype(F32), zero], axis=0).T.astype(BF16)
    mix_ref[cr:, :cr] = blank
    mix_ref[:cr, cr:] = blank
    mix_ref[cr:, cr:] = jnp.concatenate([node_out.astype(F32), zero], axis=0).T.astype(BF16)
    small[2].wait()
    copies = []
    for i, c in enumerate(chunks):
        for copy in loads[i]:
            copy.wait()
        mixed = mxu(rd_ref[c], mix_ref[...])
        d_proj = (mixed[:, cr:] + scale * mixed[:, :cr]).astype(BF16)
        d_red = (scale * mxu(p_ref[c], dnb_ref[...])).astype(BF16)
        both = jnp.concatenate([d_red, d_proj], axis=1)
        out = g_ref[c].astype(F32) + mxu(both, wcat_ref[...], ((1,), (1,)))
        out_ref[c] = out.astype(BF16)
        copies.append(move(out_ref.at[c], out_hbm.at[c], out_sem.at[i]))
        copies[-1].start()
    gn_ref[...] = scale * exact(hidden, d_pre, ((0,), (0,)))
    ga_ref[...] = -scale * exact(d_hidden, nodes, ((1,), (1,)))
    no_f, dn_f = node_out.astype(F32), dn.astype(F32)
    size = gr_ref.shape[0]
    x_red, x_dm, with_proj = (sums_ref[k * size : (k + 1) * size] for k in range(3))
    gr_ref[...] = scale * scale * exact(with_proj[:, :nodes_n], dn_f)
    gp_ref[...] = scale * exact(x_dm, no_f, ((1,), (1,))) + scale * scale * exact(
        x_red, dn_f, ((1,), (1,))
    )
    ge_ref[...] = scale * exact(with_proj[:, nodes_n:], no_f)
    for copy in copies:
        copy.wait()


def feature_grads(cube, where, mine, other, sums, adjacency, node_weight, wcat, rd, p, g, scale):
    rows, chan = g.shape
    nodes, cr = adjacency.shape[0], node_weight.shape[0]
    step = row_block(rows, 512)
    count = rows // step
    size = chan // cube.count
    loaded = (adjacency, node_weight, wcat, rd, p, g)
    return pl.pallas_call(
        functools.partial(feature_kernel, step, scale, cube),
        in_specs=[SMEM, VMEM, VMEM, VMEM] + [HBM] * 6,
        out_specs=[HBM] + [VMEM] * 5,
        out_shape=[
            pltpu.HBM((rows, chan), BF16),
            jax.ShapeDtypeStruct((size, cr), F32),
            jax.ShapeDtypeStruct((size, nodes), F32),
            jax.ShapeDtypeStruct((size, cr), F32),
            jax.ShapeDtypeStruct((nodes, nodes), F32),
            jax.ShapeDtypeStruct((cr, cr), F32),
        ],
        scratch_shapes=[pltpu.VMEM(value.shape, value.dtype) for value in loaded]
        + [
            pltpu.VMEM((rows, chan), BF16),
            pltpu.VMEM((2 * cr, 2 * cr), BF16),
            pltpu.VMEM((2 * nodes, cr), BF16),
            pltpu.SemaphoreType.DMA((3,)),
            pltpu.SemaphoreType.DMA((3, count)),
            pltpu.SemaphoreType.DMA((count,)),
        ],
        compiler_params=params(),
        cost_estimate=cost(2 * rows * 4 * 65536, rows * chan * 4 + rows * 768),
        name="feature_grads",
    )(where, mine, other, sums, *in_hbm(*loaded))


def on_device(
    cube, features, cotangent, reduce_weight, project_weight, expand_weight, adjacency, node_weight
):
    size_x, size_y, size_z, chan = features.shape
    local = size_x * size_y * size_z
    scale = 1.0 / math.sqrt(local * cube.count)
    flat_x = features.transpose(0, 2, 1, 3).reshape(local, chan)
    flat_g = cotangent.transpose(0, 2, 1, 3).reshape(local, chan)
    me = lax.axis_index(AXES).astype(jnp.int32)
    where = me.reshape(1)

    rd, p, wcat, kept, sent = gather(
        cube, where, flat_x, flat_g, reduce_weight, project_weight.T, expand_weight
    )
    nodes = adjacency.shape[0]
    for level in range(-1, cube.rounds):
        kept, sent = step(nodes, level == cube.rounds - 1, kept, cube.swap(sent, level))
    other = cube.swap(sent, -1)

    flat_out, grad_reduce, grad_project, grad_expand, grad_adjacency, grad_node = feature_grads(
        cube, where, sent, other, kept, adjacency, node_weight, wcat, rd, p, flat_g, scale
    )
    grad_features = flat_out.reshape(size_x, size_z, size_y, chan).transpose(0, 2, 1, 3)
    return (grad_features, grad_reduce, grad_project, grad_expand, grad_adjacency, grad_node)


def solution(mesh):
    return jax.shard_map(
        functools.partial(on_device, Cube(mesh)),
        mesh=mesh,
        in_specs=(P("gx", "gy", "gz", None), P("gx", "gy", "gz", None), P(), P(), P(), P(), P()),
        out_specs=(
            P("gx", "gy", "gz", None),
            P(AXES, None),
            P(AXES, None),
            P(AXES, None),
            P(),
            P(),
        ),
        check_vma=False,
    )
```

```python
import functools
import math

import jax
import jax.numpy as jnp
from jax import lax
from jax.experimental import pallas as pl
from jax.experimental.pallas import tpu as pltpu
from jax.sharding import PartitionSpec as P

AXES = ("gx", "gy", "gz")
F32 = jnp.float32
BF16 = jnp.bfloat16
HBM = pl.BlockSpec(memory_space=pltpu.HBM)
VMEM = pl.BlockSpec(memory_space=pltpu.VMEM)
SMEM = pl.BlockSpec(memory_space=pltpu.SMEM)
VMEM_LIMIT = 24 * 1024 * 1024


def exact(a, b, dims=((1,), (0,))):
    return lax.dot_general(
        a, b, (dims, ((), ())), precision=lax.Precision.HIGHEST, preferred_element_type=F32
    )


def mxu(a, b, dims=((1,), (0,))):
    return lax.dot_general(a, b, (dims, ((), ())), preferred_element_type=F32)


def params():
    return pltpu.CompilerParams(vmem_limit_bytes=VMEM_LIMIT)


def cost(flops, nbytes):
    return pl.CostEstimate(flops=flops, bytes_accessed=nbytes, transcendentals=0)


def in_hbm(*values):
    return [pltpu.with_memory_space_constraint(value, pltpu.HBM) for value in values]


def row_block(total):
    for size in (768, 512, 384, 256, 128, 64, 32, 16):
        if total % size == 0:
            return size
    return total


class Cube:
    def __init__(self, mesh):
        self.size = {axis: mesh.shape[axis] for axis in AXES}
        self.count = math.prod(self.size.values())
        stride = {"gx": self.size["gy"] * self.size["gz"], "gy": self.size["gz"], "gz": 1}
        bits = {
            axis: [stride[axis] << k for k in range(self.size[axis].bit_length() - 1)] for axis in AXES
        }
        self.core = bits["gy"][0]
        rest = bits["gx"] + bits["gy"][1:] + bits["gz"]
        self.orders = [rest, rest]
        if len(bits["gx"]) == 2:
            self.orders = [rest, [rest[1], rest[0]] + rest[2:]]
        self.rounds = len(rest)

    def side(self, device):
        return 1 if device & self.core else 0

    def traced_side(self, device):
        return lax.bitwise_and(lax.div(device, jnp.int32(self.core)), jnp.int32(1))

    def swap(self, value, level):
        masks = [self.core] * 2 if level < 0 else [order[level] for order in self.orders]
        pairs = [(d, d ^ masks[self.side(d)]) for d in range(self.count)]
        return lax.ppermute(value, AXES, pairs)

    def masks(self, side):
        order = self.orders[side]
        last = len(order) - 1
        return [
            sum(order[level] for level in range(len(order)) if j >> (last - level) & 1)
            for j in range(1 << len(order))
        ]


def gather_kernel(
    cube, step, sorted_here, where_ref, x_hbm, g_hbm, wr_hbm, wpt_hbm, we_hbm, rdp_hbm, wcat_hbm, *rest
):
    if sorted_here:
        kept_ref, sent_ref, turned_ref, *rest = rest
    else:
        keep_ref, send_ref, turned_ref, *rest = rest
    x_ref, g_ref, rdp_ref, cat_ref, wpt_ref, we_ref, sums_ref, term_ref, small_sem, in_sem, out_sem = rest
    rows = x_ref.shape[0]
    cr = we_ref.shape[1]
    nodes = wpt_ref.shape[0]
    wide = 2 * cr
    count = rows // step
    move = pltpu.make_async_copy
    small = [
        move(wr_hbm, cat_ref.at[:, pl.ds(0, cr)], small_sem.at[0]),
        move(wpt_hbm, wpt_ref, small_sem.at[1]),
        move(we_hbm, we_ref, small_sem.at[2]),
    ]
    load_cuts = sorted({0, min(1, count), min(2, count), count})
    store_cuts = sorted({0, max(count - 2, 0), max(count - 1, 0), count})
    span = lambda cuts, i: pl.ds(cuts[i] * step, (cuts[i + 1] - cuts[i]) * step)
    loads = [
        (
            move(x_hbm.at[span(load_cuts, i)], x_ref.at[span(load_cuts, i)], in_sem.at[0, i]),
            move(g_hbm.at[span(load_cuts, i)], g_ref.at[span(load_cuts, i)], in_sem.at[1, i]),
        )
        for i in range(len(load_cuts) - 1)
    ]
    stores = [
        move(rdp_ref.at[span(store_cuts, i)], rdp_hbm.at[span(store_cuts, i)], out_sem.at[i])
        for i in range(len(store_cuts) - 1)
    ]
    for copy in (*small, *loads[0]):
        copy.start()
    sums_ref[...] = jnp.zeros_like(sums_ref)
    term_ref[...] = jnp.zeros_like(term_ref)
    small[0].wait()
    small[1].wait()
    padded = jnp.concatenate([wpt_ref[...], jnp.zeros_like(wpt_ref)], axis=0)
    cat_ref[:, cr:] = padded.T
    keep_weights = move(cat_ref, wcat_hbm, small_sem.at[3])
    keep_weights.start()
    small[2].wait()

    @pl.loop(0, count)
    def _(i):
        for k, pair in enumerate(loads):
            @pl.when(i == load_cuts[k])
            def _():
                for copy in pair:
                    copy.wait()
                if k + 1 < len(loads):
                    for copy in loads[k + 1]:
                        copy.start()

        c = pl.ds(pl.multiple_of(i * step, step), step)
        x, g = x_ref[c], g_ref[c]
        both = mxu(x, cat_ref[...]).astype(BF16)
        mapped = mxu(g, we_ref[...]).astype(BF16)
        rdp = jnp.concatenate([both[:, :cr], mapped, both[:, cr:]], axis=1)
        rdp_ref[c] = rdp
        turned = rdp.T
        proj = turned[wide : wide + nodes]
        sums_ref[: wide + nodes] += mxu(turned[: wide + nodes], x)
        sums_ref[wide + nodes :] += mxu(proj, g)
        term = mxu(proj, rdp[:, :wide])
        term_ref[0] += term[:, :cr]
        term_ref[1] += term[:, cr:]
        for k, copy in enumerate(stores):
            pl.when(i == store_cuts[k + 1] - 1)(copy.start)

    me = where_ref[0]
    side = cube.traced_side(me)
    turned_ref[...] = sums_ref[...].T
    if not sorted_here:
        keep_ref[...] = term_ref[side]
        send_ref[...] = term_ref[1 - side]
    else:
        kept_ref[:nodes] = term_ref[side]
        sent_ref[:nodes] = term_ref[1 - side]
        size = turned_ref.shape[0] // cube.count
        mine = [jnp.where(side == 0, a, b) for a, b in zip(cube.masks(0), cube.masks(1))]
        other = [jnp.where(side == 0, b, a) for a, b in zip(cube.masks(0), cube.masks(1))]
        for masks, base, out_ref in ((mine, me, kept_ref), (other, me ^ cube.core, sent_ref)):
            to = nodes
            for mask in masks:
                at = pl.multiple_of((base ^ mask) * size, size)
                block = turned_ref[pl.ds(at, size), :]
                for lane in range(0, block.shape[1], cr):
                    out_ref[to : to + size] = block[:, lane : lane + cr]
                    to += size
    for copy in (keep_weights, *stores):
        copy.wait()


def gather(cube, where, x, g, wr, wpt, we):
    rows, chan = x.shape
    cr, nodes = wr.shape[1], wpt.shape[0]
    step = row_block(rows)
    width = 2 * cr + 2 * nodes
    half = cube.count // 2
    size = chan // cube.count
    sorted_here = size % 8 == 0
    outs = [
        (HBM, pltpu.HBM((rows, width), BF16)),
        (HBM, pltpu.HBM((chan, cr + 2 * nodes), BF16)),
    ]
    scratch = []
    if sorted_here:
        outs += [(VMEM, pltpu.VMEM((nodes + half * size * width // cr, cr), F32))] * 2
        scratch += [pltpu.VMEM((chan, width), F32)]
    else:
        outs += [(VMEM, jax.ShapeDtypeStruct((nodes, cr), F32))] * 2
        outs += [(VMEM, jax.ShapeDtypeStruct((chan, width), F32))]
    scratch += [
        pltpu.VMEM((rows, chan), BF16),
        pltpu.VMEM((rows, chan), BF16),
        pltpu.VMEM((rows, width), BF16),
        pltpu.VMEM((chan, cr + 2 * nodes), BF16),
        pltpu.VMEM(wpt.shape, BF16),
        pltpu.VMEM(we.shape, BF16),
        pltpu.VMEM((width, chan), F32),
        pltpu.VMEM((2, nodes, cr), F32),
        pltpu.SemaphoreType.DMA((4,)),
        pltpu.SemaphoreType.DMA((2, 3)),
        pltpu.SemaphoreType.DMA((3,)),
    ]
    rdp, wcat, kept, sent, *sums = pl.pallas_call(
        functools.partial(gather_kernel, cube, step, sorted_here),
        in_specs=[SMEM] + [HBM] * 5,
        out_specs=[spec for spec, _ in outs],
        out_shape=[shape for _, shape in outs],
        scratch_shapes=scratch,
        compiler_params=params(),
        cost_estimate=cost(2 * rows * chan * 1024, rows * chan * 4 + rows * 768),
        name="gather",
    )(where, *in_hbm(x, g, wr, wpt, we))
    if not sorted_here:
        side = cube.traced_side(where[0])
        table = jnp.array([cube.masks(0), cube.masks(1)], jnp.int32)
        cut = sums[0].reshape(cube.count, size, width // cr, cr).transpose(0, 2, 1, 3)
        lay = lambda head, index: jnp.concatenate([head, cut[index].reshape(-1, cr)])
        kept = lay(kept, where[0] ^ table[side])
        sent = lay(sent, where[0] ^ cube.core ^ table[1 - side])
    return rdp, wcat, kept, sent


def add_kernel(a_ref, b_ref, out_ref):
    rows = out_ref.shape[0]
    out_ref[...] = a_ref[:rows] + b_ref[:rows]


def add(a, b, rows):
    return pl.pallas_call(
        add_kernel,
        in_specs=[VMEM] * 2,
        out_specs=VMEM,
        out_shape=pltpu.VMEM((rows, a.shape[1]), F32),
        compiler_params=params(),
        cost_estimate=cost(rows * a.shape[1], 12 * rows * a.shape[1]),
        name="add",
    )(a, b)


def halve_kernel(skip, a_ref, b_ref, _, keep_ref, send_ref):
    half = keep_ref.shape[0]
    keep_ref[...] = a_ref[skip : skip + half] + b_ref[skip : skip + half]
    send_ref[...] = a_ref[skip + half :] + b_ref[skip + half :]


def halve(a, b, skip, after):
    shape = ((a.shape[0] - skip) // 2, a.shape[1])
    return pl.pallas_call(
        functools.partial(halve_kernel, skip),
        in_specs=[VMEM] * 2 + [pl.BlockSpec(memory_space=pl.ANY)],
        out_specs=[VMEM] * 2,
        out_shape=[pltpu.VMEM(shape, F32)] * 2,
        compiler_params=params(),
        cost_estimate=cost(a.size, 12 * a.size),
        name="halve",
    )(a, b, after)


def feature_kernel(
    step, scale, cube, where_ref, mine_ref, other_ref, adj_hbm, nw_hbm, wcat_hbm, rdp_hbm, g_hbm,
    out_hbm, ga_ref, gn_ref, no_ref, dn_ref,
    adj_ref, nw_ref, wcat_ref, rdp_ref, g_ref, out_ref, mix_ref, dnb_ref, in_sem, out_sem,
):
    nodes_n, cr = mine_ref.shape
    rows = g_ref.shape[0]
    wide = 2 * cr
    move = pltpu.make_async_copy
    pairs = (
        (adj_hbm, adj_ref), (nw_hbm, nw_ref), (rdp_hbm, rdp_ref), (wcat_hbm, wcat_ref), (g_hbm, g_ref)
    )
    loads = [move(src, dst, in_sem.at[k]) for k, (src, dst) in enumerate(pairs)]
    for copy in loads:
        copy.start()
    first = cube.traced_side(where_ref[0]) == 0
    mine, other = mine_ref[...], other_ref[...]
    nodes = scale * jnp.where(first, mine, other)
    d_node_out = jnp.where(first, other, mine)
    loads[0].wait()
    loads[1].wait()
    adj, nw = adj_ref[...], nw_ref[...]
    hidden = nodes - exact(adj, nodes)
    pre = exact(hidden, nw)
    node_out = jnp.maximum(pre, 0.0).astype(BF16)
    d_pre = jnp.where(pre > 0.0, d_node_out, 0.0)
    d_hidden = exact(d_pre, nw, ((1,), (1,)))
    d_nodes = d_hidden - exact(adj, d_hidden, ((0,), (0,)))
    dn = d_nodes.astype(BF16)
    no_f, dn_f = node_out.astype(F32), dn.astype(F32)
    no_ref[...] = no_f
    dn_ref[...] = dn_f
    dnb_ref[:nodes_n] = dn
    dnb_ref[nodes_n:] = jnp.zeros((nodes_n, cr), BF16)
    blank = jnp.zeros((cr, cr), BF16)
    zero = jnp.zeros((nodes_n, cr), F32)
    mix_ref[:cr, :cr] = jnp.concatenate([dn_f, zero], axis=0).T.astype(BF16)
    mix_ref[cr:, :cr] = blank
    mix_ref[:cr, cr:] = blank
    mix_ref[cr:, cr:] = jnp.concatenate([no_f, zero], axis=0).T.astype(BF16)
    for copy in loads[2:]:
        copy.wait()
    copies = []
    for i, start in enumerate(range(0, rows, step)):
        c = pl.ds(start, step)
        rdp = rdp_ref[c]
        mixed = mxu(rdp[:, :wide], mix_ref[...])
        d_proj = (mixed[:, cr:] + scale * mixed[:, :cr]).astype(BF16)
        d_red = (scale * mxu(rdp[:, wide:], dnb_ref[...])).astype(BF16)
        both = jnp.concatenate([d_red, d_proj], axis=1)
        out = g_ref[c].astype(F32) + mxu(both, wcat_ref[...], ((1,), (1,)))
        out_ref[c] = out.astype(BF16)
        copies.append(move(out_ref.at[c], out_hbm.at[c], out_sem.at[i]))
        copies[-1].start()
    gn_ref[...] = scale * exact(hidden, d_pre, ((0,), (0,)))
    ga_ref[...] = -scale * exact(d_hidden, nodes, ((1,), (1,)))
    for copy in copies:
        copy.wait()


def feature_grads(cube, where, mine, other, adjacency, node_weight, wcat, rdp, g, scale):
    rows, chan = g.shape
    nodes, cr = adjacency.shape[0], node_weight.shape[0]
    step = row_block(rows)
    loaded = (adjacency, node_weight, rdp, wcat, g)
    order = (adjacency, node_weight, wcat, rdp, g)
    return pl.pallas_call(
        functools.partial(feature_kernel, step, scale, cube),
        in_specs=[SMEM, VMEM, VMEM] + [HBM] * len(loaded),
        out_specs=[HBM] + [VMEM] * 4,
        out_shape=[
            pltpu.HBM((rows, chan), BF16),
            jax.ShapeDtypeStruct((nodes, nodes), F32),
            jax.ShapeDtypeStruct((cr, cr), F32),
            pltpu.VMEM((nodes, cr), F32),
            pltpu.VMEM((nodes, cr), F32),
        ],
        scratch_shapes=[pltpu.VMEM(value.shape, value.dtype) for value in order]
        + [
            pltpu.VMEM((rows, chan), BF16),
            pltpu.VMEM((2 * cr, 2 * cr), BF16),
            pltpu.VMEM((2 * nodes, cr), BF16),
            pltpu.SemaphoreType.DMA((len(loaded),)),
            pltpu.SemaphoreType.DMA((rows // step,)),
        ],
        compiler_params=params(),
        cost_estimate=cost(2 * rows * 4 * 65536, rows * chan * 4 + rows * 768),
        name="feature_grads",
    )(where, mine, other, *in_hbm(*order))


def finish_kernel(scale, kept_ref, got_ref, no_ref, dn_ref, gr_ref, gp_ref, ge_ref):
    total = kept_ref[...] + got_ref[...]
    nodes = no_ref.shape[0]
    no, dn = no_ref[...], dn_ref[...]
    size = gr_ref.shape[0]
    x_red, x_dm, with_proj = (total[k * size : (k + 1) * size] for k in range(3))
    gr_ref[...] = scale * scale * exact(with_proj[:, :nodes], dn)
    gp_ref[...] = scale * exact(x_dm, no, ((1,), (1,))) + scale * scale * exact(
        x_red, dn, ((1,), (1,))
    )
    ge_ref[...] = scale * exact(with_proj[:, nodes:], no)


def finish(kept, got, no, dn, size, scale):
    nodes, cr = no.shape
    return pl.pallas_call(
        functools.partial(finish_kernel, scale),
        in_specs=[VMEM] * 4,
        out_specs=[VMEM] * 3,
        out_shape=[
            jax.ShapeDtypeStruct((size, cr), F32),
            jax.ShapeDtypeStruct((size, nodes), F32),
            jax.ShapeDtypeStruct((size, cr), F32),
        ],
        compiler_params=params(),
        cost_estimate=cost(0, size * 4096),
        name="finish",
    )(kept, got, no, dn)


def on_device(
    cube, features, cotangent, reduce_weight, project_weight, expand_weight, adjacency, node_weight
):
    size_x, size_y, size_z, chan = features.shape
    local = size_x * size_y * size_z
    scale = 1.0 / math.sqrt(local * cube.count)
    flat_x = features.transpose(0, 2, 1, 3).reshape(local, chan)
    flat_g = cotangent.transpose(0, 2, 1, 3).reshape(local, chan)
    me = lax.axis_index(AXES).astype(jnp.int32)
    where = me.reshape(1)

    rdp, wcat, kept, sent = gather(
        cube, where, flat_x, flat_g, reduce_weight, project_weight.T, expand_weight
    )
    nodes = adjacency.shape[0]
    got = cube.swap(sent, -1)
    sums = [add(kept, got, nodes)]
    for level in range(cube.rounds):
        sums.append(add(sums[-1], cube.swap(sums[-1], level), nodes))
    mine = sums[-1]
    other = cube.swap(mine, -1)
    for level in range(cube.rounds):
        after = sums[min(level + 1, cube.rounds)] if level else sums[0]
        kept, sent = halve(kept, got, 0 if level else nodes, after)
        got = cube.swap(sent, level)

    flat_out, grad_adjacency, grad_node, no, dn = feature_grads(
        cube, where, mine, other, adjacency, node_weight, wcat, rdp, flat_g, scale
    )
    grad_reduce, grad_project, grad_expand = finish(
        kept, got, no, dn, chan // cube.count, scale
    )
    grad_features = flat_out.reshape(size_x, size_z, size_y, chan).transpose(0, 2, 1, 3)
    return (grad_features, grad_reduce, grad_project, grad_expand, grad_adjacency, grad_node)


def solution(mesh):
    return jax.shard_map(
        functools.partial(on_device, Cube(mesh)),
        mesh=mesh,
        in_specs=(P("gx", "gy", "gz", None), P("gx", "gy", "gz", None), P(), P(), P(), P(), P()),
        out_specs=(
            P("gx", "gy", "gz", None),
            P(AXES, None),
            P(AXES, None),
            P(AXES, None),
            P(),
            P(),
        ),
        check_vma=False,
    )
```

```python
import functools
import math

import jax
import jax.numpy as jnp
from jax import lax
from jax.experimental import pallas as pl
from jax.experimental.pallas import tpu as pltpu
from jax.sharding import PartitionSpec as P

AXES = ("gx", "gy", "gz")
F32 = jnp.float32
BF16 = jnp.bfloat16
HBM = pl.BlockSpec(memory_space=pltpu.HBM)
VMEM = pl.BlockSpec(memory_space=pltpu.VMEM)
SMEM = pl.BlockSpec(memory_space=pltpu.SMEM)
VMEM_LIMIT = 24 * 1024 * 1024


def exact(a, b, dims=((1,), (0,))):
    return lax.dot_general(
        a, b, (dims, ((), ())), precision=lax.Precision.HIGHEST, preferred_element_type=F32
    )


def mxu(a, b, dims=((1,), (0,))):
    return lax.dot_general(a, b, (dims, ((), ())), preferred_element_type=F32)


def params():
    return pltpu.CompilerParams(vmem_limit_bytes=VMEM_LIMIT)


def cost(flops, nbytes):
    return pl.CostEstimate(flops=flops, bytes_accessed=nbytes, transcendentals=0)


def in_hbm(*values):
    return [pltpu.with_memory_space_constraint(value, pltpu.HBM) for value in values]


def row_block(total):
    for size in (768, 512, 384, 256, 128, 64, 32, 16):
        if total % size == 0:
            return size
    return total


class Plan:
    def __init__(self, mesh):
        size = {axis: mesh.shape[axis] for axis in AXES}
        self.count = math.prod(size.values())
        stride = {"gx": size["gy"] * size["gz"], "gy": size["gz"], "gz": 1}
        self.core = stride["gy"]
        spans = ((size["gx"], stride["gx"]), (size["gy"] // 2, 2 * stride["gy"]), (size["gz"], stride["gz"]))
        self.groups = [[k * step for k in range(n)] for n, step in spans if n > 1]
        self.masks = [0]
        for group in self.groups:
            self.masks = [mask | bits for mask in self.masks for bits in group]

    def side(self, device):
        return lax.bitwise_and(lax.div(device, jnp.int32(self.core)), jnp.int32(1))

    def swap(self, value, mask):
        return lax.ppermute(value, AXES, [(d, d ^ mask) for d in range(self.count)])


def gather_kernel(
    plan, step, sorted_here, where_ref, x_hbm, g_hbm, wr_hbm, wpt_hbm, we_hbm, rdp_hbm, wcat_hbm, *rest
):
    if sorted_here:
        kept_ref, sent_ref, turned_ref, *rest = rest
    else:
        keep_ref, send_ref, turned_ref, *rest = rest
    x_ref, g_ref, rdp_ref, cat_ref, wpt_ref, we_ref, sums_ref, term_ref, small_sem, in_sem, out_sem = rest
    rows = x_ref.shape[0]
    cr = we_ref.shape[1]
    nodes = wpt_ref.shape[0]
    wide = 2 * cr
    count = rows // step
    move = pltpu.make_async_copy
    small = [
        move(wr_hbm, cat_ref.at[:, pl.ds(0, cr)], small_sem.at[0]),
        move(wpt_hbm, wpt_ref, small_sem.at[1]),
        move(we_hbm, we_ref, small_sem.at[2]),
    ]
    load_cuts = sorted({0, min(1, count), min(2, count), count})
    store_cuts = sorted({0, max(count - 2, 0), max(count - 1, 0), count})
    span = lambda cuts, i: pl.ds(cuts[i] * step, (cuts[i + 1] - cuts[i]) * step)
    loads = [
        (
            move(x_hbm.at[span(load_cuts, i)], x_ref.at[span(load_cuts, i)], in_sem.at[0, i]),
            move(g_hbm.at[span(load_cuts, i)], g_ref.at[span(load_cuts, i)], in_sem.at[1, i]),
        )
        for i in range(len(load_cuts) - 1)
    ]
    stores = [
        move(rdp_ref.at[span(store_cuts, i)], rdp_hbm.at[span(store_cuts, i)], out_sem.at[i])
        for i in range(len(store_cuts) - 1)
    ]
    for copy in (*small, *loads[0]):
        copy.start()
    sums_ref[...] = jnp.zeros_like(sums_ref)
    term_ref[...] = jnp.zeros_like(term_ref)
    small[0].wait()
    small[1].wait()
    padded = jnp.concatenate([wpt_ref[...], jnp.zeros_like(wpt_ref)], axis=0)
    cat_ref[:, cr:] = padded.T
    keep_weights = move(cat_ref, wcat_hbm, small_sem.at[3])
    keep_weights.start()
    small[2].wait()

    @pl.loop(0, count)
    def _(i):
        for k, pair in enumerate(loads):
            @pl.when(i == load_cuts[k])
            def _():
                for copy in pair:
                    copy.wait()
                if k + 1 < len(loads):
                    for copy in loads[k + 1]:
                        copy.start()

        c = pl.ds(pl.multiple_of(i * step, step), step)
        x, g = x_ref[c], g_ref[c]
        both = mxu(x, cat_ref[...]).astype(BF16)
        mapped = mxu(g, we_ref[...]).astype(BF16)
        rdp = jnp.concatenate([both[:, :cr], mapped, both[:, cr:]], axis=1)
        rdp_ref[c] = rdp
        turned = rdp.T
        proj = turned[wide : wide + nodes]
        sums_ref[: wide + nodes] += mxu(turned[: wide + nodes], x)
        sums_ref[wide + nodes :] += mxu(proj, g)
        term = mxu(proj, rdp[:, :wide])
        term_ref[0] += term[:, :cr]
        term_ref[1] += term[:, cr:]
        for k, copy in enumerate(stores):
            pl.when(i == store_cuts[k + 1] - 1)(copy.start)

    me = where_ref[0]
    side = plan.side(me)
    turned_ref[...] = sums_ref[...].T
    if not sorted_here:
        keep_ref[...] = term_ref[side]
        send_ref[...] = term_ref[1 - side]
    else:
        kept_ref[:nodes] = term_ref[side]
        sent_ref[:nodes] = term_ref[1 - side]
        size = turned_ref.shape[0] // plan.count
        for base, out_ref in ((me, kept_ref), (me ^ plan.core, sent_ref)):
            to = nodes
            for mask in plan.masks:
                at = pl.multiple_of((base ^ mask) * size, size)
                block = turned_ref[pl.ds(at, size), :]
                for lane in range(0, block.shape[1], cr):
                    out_ref[to : to + size] = block[:, lane : lane + cr]
                    to += size
    for copy in (keep_weights, *stores):
        copy.wait()


def gather(plan, where, x, g, wr, wpt, we):
    rows, chan = x.shape
    cr, nodes = wr.shape[1], wpt.shape[0]
    step = row_block(rows)
    width = 2 * cr + 2 * nodes
    half = plan.count // 2
    size = chan // plan.count
    sorted_here = size % 8 == 0
    outs = [
        (HBM, pltpu.HBM((rows, width), BF16)),
        (HBM, pltpu.HBM((chan, cr + 2 * nodes), BF16)),
    ]
    scratch = []
    if sorted_here:
        outs += [(VMEM, pltpu.VMEM((nodes + half * size * width // cr, cr), F32))] * 2
        scratch += [pltpu.VMEM((chan, width), F32)]
    else:
        outs += [(VMEM, jax.ShapeDtypeStruct((nodes, cr), F32))] * 2
        outs += [(VMEM, jax.ShapeDtypeStruct((chan, width), F32))]
    scratch += [
        pltpu.VMEM((rows, chan), BF16),
        pltpu.VMEM((rows, chan), BF16),
        pltpu.VMEM((rows, width), BF16),
        pltpu.VMEM((chan, cr + 2 * nodes), BF16),
        pltpu.VMEM(wpt.shape, BF16),
        pltpu.VMEM(we.shape, BF16),
        pltpu.VMEM((width, chan), F32),
        pltpu.VMEM((2, nodes, cr), F32),
        pltpu.SemaphoreType.DMA((4,)),
        pltpu.SemaphoreType.DMA((2, 3)),
        pltpu.SemaphoreType.DMA((3,)),
    ]
    rdp, wcat, kept, sent, *sums = pl.pallas_call(
        functools.partial(gather_kernel, plan, step, sorted_here),
        in_specs=[SMEM] + [HBM] * 5,
        out_specs=[spec for spec, _ in outs],
        out_shape=[shape for _, shape in outs],
        scratch_shapes=scratch,
        compiler_params=params(),
        cost_estimate=cost(2 * rows * chan * 1024, rows * chan * 4 + rows * 768),
        name="gather",
    )(where, *in_hbm(x, g, wr, wpt, we))
    if not sorted_here:
        table = jnp.array(plan.masks, jnp.int32)
        cut = sums[0].reshape(plan.count, size, width // cr, cr).transpose(0, 2, 1, 3)
        lay = lambda head, index: jnp.concatenate([head, cut[index].reshape(-1, cr)])
        kept = lay(kept, where[0] ^ table)
        sent = lay(sent, where[0] ^ plan.core ^ table)
    return rdp, wcat, kept, sent


def step_kernel(head, ins, parts, *refs):
    terms, outs = refs[:ins], refs[ins:]

    def total(start, size):
        value = terms[0][start : start + size]
        for ref in terms[1:]:
            value = value + ref[start : start + size]
        return value

    nodes = total(0, head)
    rest = terms[0].shape[0] - head
    if parts == 1:
        outs[0][...] = nodes
        outs[1][...] = total(head, rest)
        return
    size = rest // parts
    for k, ref in enumerate(outs):
        ref[:head] = nodes
        ref[head:] = total(head + k * size, size)


def step(head, parts, terms):
    rest, lanes = terms[0].shape[0] - head, terms[0].shape[1]
    shapes = (head, rest) if parts == 1 else (head + rest // parts,) * parts
    return pl.pallas_call(
        functools.partial(step_kernel, head, len(terms), parts),
        in_specs=[VMEM] * len(terms),
        out_specs=[VMEM] * len(shapes),
        out_shape=[pltpu.VMEM((size, lanes), F32) for size in shapes],
        compiler_params=params(),
        cost_estimate=cost(terms[0].size, 12 * terms[0].size),
        name="step",
    )(*terms)


def feature_kernel(
    step, scale, plan, where_ref, mine_ref, other_ref, sums_ref, adj_hbm, nw_hbm, wcat_hbm, rdp_hbm, g_hbm,
    out_hbm, gr_ref, gp_ref, ge_ref, ga_ref, gn_ref,
    adj_ref, nw_ref, wcat_ref, rdp_ref, g_ref, out_ref, mix_ref, dnb_ref, in_sem, out_sem,
):
    nodes_n, cr = mine_ref.shape
    rows = g_ref.shape[0]
    wide = 2 * cr
    move = pltpu.make_async_copy
    pairs = (
        (adj_hbm, adj_ref), (nw_hbm, nw_ref), (rdp_hbm, rdp_ref), (wcat_hbm, wcat_ref), (g_hbm, g_ref)
    )
    loads = [move(src, dst, in_sem.at[k]) for k, (src, dst) in enumerate(pairs)]
    for copy in loads:
        copy.start()
    first = plan.side(where_ref[0]) == 0
    mine, other = mine_ref[...], other_ref[...]
    nodes = scale * jnp.where(first, mine, other)
    d_node_out = jnp.where(first, other, mine)
    loads[0].wait()
    loads[1].wait()
    adj, nw = adj_ref[...], nw_ref[...]
    hidden = nodes - exact(adj, nodes)
    pre = exact(hidden, nw)
    node_out = jnp.maximum(pre, 0.0).astype(BF16)
    d_pre = jnp.where(pre > 0.0, d_node_out, 0.0)
    d_hidden = exact(d_pre, nw, ((1,), (1,)))
    d_nodes = d_hidden - exact(adj, d_hidden, ((0,), (0,)))
    dn = d_nodes.astype(BF16)
    no_f, dn_f = node_out.astype(F32), dn.astype(F32)
    dnb_ref[:nodes_n] = dn
    dnb_ref[nodes_n:] = jnp.zeros((nodes_n, cr), BF16)
    blank = jnp.zeros((cr, cr), BF16)
    zero = jnp.zeros((nodes_n, cr), F32)
    mix_ref[:cr, :cr] = jnp.concatenate([dn_f, zero], axis=0).T.astype(BF16)
    mix_ref[cr:, :cr] = blank
    mix_ref[:cr, cr:] = blank
    mix_ref[cr:, cr:] = jnp.concatenate([no_f, zero], axis=0).T.astype(BF16)
    for copy in loads[2:]:
        copy.wait()
    copies = []
    for i, start in enumerate(range(0, rows, step)):
        c = pl.ds(start, step)
        rdp = rdp_ref[c]
        mixed = mxu(rdp[:, :wide], mix_ref[...])
        d_proj = (mixed[:, cr:] + scale * mixed[:, :cr]).astype(BF16)
        d_red = (scale * mxu(rdp[:, wide:], dnb_ref[...])).astype(BF16)
        both = jnp.concatenate([d_red, d_proj], axis=1)
        out = g_ref[c].astype(F32) + mxu(both, wcat_ref[...], ((1,), (1,)))
        out_ref[c] = out.astype(BF16)
        copies.append(move(out_ref.at[c], out_hbm.at[c], out_sem.at[i]))
        copies[-1].start()
    gn_ref[...] = scale * exact(hidden, d_pre, ((0,), (0,)))
    ga_ref[...] = -scale * exact(d_hidden, nodes, ((1,), (1,)))
    size = gr_ref.shape[0]
    x_red, x_dm, with_proj = (sums_ref[k * size : (k + 1) * size] for k in range(3))
    gr_ref[...] = scale * scale * exact(with_proj[:, :nodes_n], dn_f)
    gp_ref[...] = scale * exact(x_dm, no_f, ((1,), (1,))) + scale * scale * exact(
        x_red, dn_f, ((1,), (1,))
    )
    ge_ref[...] = scale * exact(with_proj[:, nodes_n:], no_f)
    for copy in copies:
        copy.wait()


def feature_grads(plan, where, mine, other, sums, adjacency, node_weight, wcat, rdp, g, scale):
    rows, chan = g.shape
    nodes, cr = adjacency.shape[0], node_weight.shape[0]
    step = row_block(rows)
    size = chan // plan.count
    loaded = (adjacency, node_weight, wcat, rdp, g)
    return pl.pallas_call(
        functools.partial(feature_kernel, step, scale, plan),
        in_specs=[SMEM, VMEM, VMEM, VMEM] + [HBM] * len(loaded),
        out_specs=[HBM] + [VMEM] * 5,
        out_shape=[
            pltpu.HBM((rows, chan), BF16),
            jax.ShapeDtypeStruct((size, cr), F32),
            jax.ShapeDtypeStruct((size, nodes), F32),
            jax.ShapeDtypeStruct((size, cr), F32),
            jax.ShapeDtypeStruct((nodes, nodes), F32),
            jax.ShapeDtypeStruct((cr, cr), F32),
        ],
        scratch_shapes=[pltpu.VMEM(value.shape, value.dtype) for value in loaded]
        + [
            pltpu.VMEM((rows, chan), BF16),
            pltpu.VMEM((2 * cr, 2 * cr), BF16),
            pltpu.VMEM((2 * nodes, cr), BF16),
            pltpu.SemaphoreType.DMA((len(loaded),)),
            pltpu.SemaphoreType.DMA((rows // step,)),
        ],
        compiler_params=params(),
        cost_estimate=cost(2 * rows * 4 * 65536, rows * chan * 4 + rows * 768),
        name="feature_grads",
    )(where, mine, other, sums, *in_hbm(*loaded))


def on_device(
    plan, features, cotangent, reduce_weight, project_weight, expand_weight, adjacency, node_weight
):
    size_x, size_y, size_z, chan = features.shape
    local = size_x * size_y * size_z
    scale = 1.0 / math.sqrt(local * plan.count)
    flat_x = features.transpose(0, 2, 1, 3).reshape(local, chan)
    flat_g = cotangent.transpose(0, 2, 1, 3).reshape(local, chan)
    me = lax.axis_index(AXES).astype(jnp.int32)
    where = me.reshape(1)

    rdp, wcat, kept, sent = gather(
        plan, where, flat_x, flat_g, reduce_weight, project_weight.T, expand_weight
    )
    head = adjacency.shape[0]
    terms = [kept, plan.swap(sent, plan.core)]
    for group in plan.groups:
        parts = step(head, len(group), terms)
        terms = [plan.swap(part, mask) if mask else part for part, mask in zip(parts, group)]
    mine, sums = step(head, 1, terms)
    other = plan.swap(mine, plan.core)

    flat_out, grad_reduce, grad_project, grad_expand, grad_adjacency, grad_node = feature_grads(
        plan, where, mine, other, sums, adjacency, node_weight, wcat, rdp, flat_g, scale
    )
    grad_features = flat_out.reshape(size_x, size_z, size_y, chan).transpose(0, 2, 1, 3)
    return (grad_features, grad_reduce, grad_project, grad_expand, grad_adjacency, grad_node)


def solution(mesh):
    return jax.shard_map(
        functools.partial(on_device, Plan(mesh)),
        mesh=mesh,
        in_specs=(P("gx", "gy", "gz", None), P("gx", "gy", "gz", None), P(), P(), P(), P(), P()),
        out_specs=(
            P("gx", "gy", "gz", None),
            P(AXES, None),
            P(AXES, None),
            P(AXES, None),
            P(),
            P(),
        ),
        check_vma=False,
    )
```

```python
import functools
import math

import jax
import jax.numpy as jnp
from jax import lax
from jax.experimental import pallas as pl
from jax.experimental.pallas import tpu as pltpu
from jax.sharding import PartitionSpec as P

AXES = ("gx", "gy", "gz")
F32 = jnp.float32
BF16 = jnp.bfloat16
HBM = pl.BlockSpec(memory_space=pltpu.HBM)
VMEM = pl.BlockSpec(memory_space=pltpu.VMEM)
SMEM = pl.BlockSpec(memory_space=pltpu.SMEM)
VMEM_LIMIT = 24 * 1024 * 1024
SMALL_LIMIT = 4 * 1024 * 1024


def exact(a, b, dims=((1,), (0,))):
    return lax.dot_general(
        a, b, (dims, ((), ())), precision=lax.Precision.HIGHEST, preferred_element_type=F32
    )


def mxu(a, b, dims=((1,), (0,))):
    return lax.dot_general(a, b, (dims, ((), ())), preferred_element_type=F32)


def params(limit=VMEM_LIMIT):
    return pltpu.CompilerParams(vmem_limit_bytes=limit)


def cost(flops, nbytes):
    return pl.CostEstimate(flops=flops, bytes_accessed=nbytes, transcendentals=0)


def in_hbm(*values):
    return [pltpu.with_memory_space_constraint(value, pltpu.HBM) for value in values]


def row_block(total):
    for size in (1024, 768, 512, 384, 256, 128, 64, 32, 16):
        if total % size == 0:
            return size
    return total


class Plan:
    def __init__(self, mesh):
        size = {axis: mesh.shape[axis] for axis in AXES}
        self.count = math.prod(size.values())
        stride = {"gx": size["gy"] * size["gz"], "gy": size["gz"], "gz": 1}
        self.core = stride["gy"]
        spans = ((size["gx"], stride["gx"]), (size["gy"] // 2, 2 * stride["gy"]), (size["gz"], stride["gz"]))
        self.groups = [[k * step for k in range(n)] for n, step in spans if n > 1]
        self.masks = [0]
        for group in self.groups:
            self.masks = [mask | bits for mask in self.masks for bits in group]

    def side(self, device):
        return lax.bitwise_and(lax.div(device, jnp.int32(self.core)), jnp.int32(1))

    def swap(self, value, mask):
        return lax.ppermute(value, AXES, [(d, d ^ mask) for d in range(self.count)])


def gather_kernel(
    plan, step, sorted_here, where_ref, x_hbm, g_hbm, wr_hbm, wpt_hbm, we_hbm, rdp_hbm, wcat_hbm, *rest
):
    if sorted_here:
        kept_ref, sent_ref, turned_ref, *rest = rest
    else:
        keep_ref, send_ref, turned_ref, *rest = rest
    x_ref, g_ref, rdp_ref, cat_ref, wpt_ref, we_ref, sums_ref, term_ref, small_sem, in_sem, out_sem = rest
    rows = x_ref.shape[0]
    cr = we_ref.shape[1]
    nodes = wpt_ref.shape[0]
    wide = 2 * cr
    count = rows // step
    move = pltpu.make_async_copy
    small = [
        move(wr_hbm, cat_ref.at[:, pl.ds(0, cr)], small_sem.at[0]),
        move(wpt_hbm, wpt_ref, small_sem.at[1]),
        move(we_hbm, we_ref, small_sem.at[2]),
    ]
    load_cuts = sorted({0, min(1, count), min(2, count), count})
    store_cuts = sorted({0, max(count - 2, 0), max(count - 1, 0), count})
    span = lambda cuts, i: pl.ds(cuts[i] * step, (cuts[i + 1] - cuts[i]) * step)
    loads = [
        (
            move(x_hbm.at[span(load_cuts, i)], x_ref.at[span(load_cuts, i)], in_sem.at[0, i]),
            move(g_hbm.at[span(load_cuts, i)], g_ref.at[span(load_cuts, i)], in_sem.at[1, i]),
        )
        for i in range(len(load_cuts) - 1)
    ]
    stores = [
        move(rdp_ref.at[span(store_cuts, i)], rdp_hbm.at[span(store_cuts, i)], out_sem.at[i])
        for i in range(len(store_cuts) - 1)
    ]
    for copy in (*small, *loads[0]):
        copy.start()
    sums_ref[...] = jnp.zeros_like(sums_ref)
    term_ref[...] = jnp.zeros_like(term_ref)
    small[0].wait()
    small[1].wait()
    padded = jnp.concatenate([wpt_ref[...], jnp.zeros_like(wpt_ref)], axis=0)
    cat_ref[:, cr:] = padded.T
    keep_weights = move(cat_ref, wcat_hbm, small_sem.at[3])
    keep_weights.start()
    small[2].wait()

    @pl.loop(0, count)
    def _(i):
        for k, pair in enumerate(loads):
            @pl.when(i == load_cuts[k])
            def _():
                for copy in pair:
                    copy.wait()
                if k + 1 < len(loads):
                    for copy in loads[k + 1]:
                        copy.start()

        c = pl.ds(pl.multiple_of(i * step, step), step)
        x, g = x_ref[c], g_ref[c]
        both = mxu(x, cat_ref[...]).astype(BF16)
        mapped = mxu(g, we_ref[...]).astype(BF16)
        rdp = jnp.concatenate([both[:, :cr], mapped, both[:, cr:]], axis=1)
        rdp_ref[c] = rdp
        turned = rdp.T
        proj = turned[wide : wide + nodes]
        sums_ref[: wide + nodes] += mxu(turned[: wide + nodes], x)
        sums_ref[wide + nodes :] += mxu(proj, g)
        term = mxu(proj, rdp[:, :wide])
        term_ref[0] += term[:, :cr]
        term_ref[1] += term[:, cr:]
        for k, copy in enumerate(stores):
            pl.when(i == store_cuts[k + 1] - 1)(copy.start)

    me = where_ref[0]
    side = plan.side(me)
    turned_ref[...] = sums_ref[...].T
    if not sorted_here:
        keep_ref[...] = term_ref[side]
        send_ref[...] = term_ref[1 - side]
    else:
        kept_ref[:nodes] = term_ref[side]
        sent_ref[:nodes] = term_ref[1 - side]
        size = turned_ref.shape[0] // plan.count
        for base, out_ref in ((me, kept_ref), (me ^ plan.core, sent_ref)):
            to = nodes
            for mask in plan.masks:
                at = pl.multiple_of((base ^ mask) * size, size)
                block = turned_ref[pl.ds(at, size), :]
                for lane in range(0, block.shape[1], cr):
                    out_ref[to : to + size] = block[:, lane : lane + cr]
                    to += size
    for copy in (keep_weights, *stores):
        copy.wait()


def gather(plan, where, x, g, wr, wpt, we):
    rows, chan = x.shape
    cr, nodes = wr.shape[1], wpt.shape[0]
    step = row_block(rows)
    width = 2 * cr + 2 * nodes
    half = plan.count // 2
    size = chan // plan.count
    sorted_here = size % 8 == 0
    outs = [
        (HBM, pltpu.HBM((rows, width), BF16)),
        (HBM, pltpu.HBM((chan, cr + 2 * nodes), BF16)),
    ]
    scratch = []
    if sorted_here:
        outs += [(VMEM, pltpu.VMEM((nodes + half * size * width // cr, cr), F32))] * 2
        scratch += [pltpu.VMEM((chan, width), F32)]
    else:
        outs += [(VMEM, jax.ShapeDtypeStruct((nodes, cr), F32))] * 2
        outs += [(VMEM, jax.ShapeDtypeStruct((chan, width), F32))]
    scratch += [
        pltpu.VMEM((rows, chan), BF16),
        pltpu.VMEM((rows, chan), BF16),
        pltpu.VMEM((rows, width), BF16),
        pltpu.VMEM((chan, cr + 2 * nodes), BF16),
        pltpu.VMEM(wpt.shape, BF16),
        pltpu.VMEM(we.shape, BF16),
        pltpu.VMEM((width, chan), F32),
        pltpu.VMEM((2, nodes, cr), F32),
        pltpu.SemaphoreType.DMA((4,)),
        pltpu.SemaphoreType.DMA((2, 3)),
        pltpu.SemaphoreType.DMA((3,)),
    ]
    rdp, wcat, kept, sent, *sums = pl.pallas_call(
        functools.partial(gather_kernel, plan, step, sorted_here),
        in_specs=[SMEM] + [HBM] * 5,
        out_specs=[spec for spec, _ in outs],
        out_shape=[shape for _, shape in outs],
        scratch_shapes=scratch,
        compiler_params=params(),
        cost_estimate=cost(2 * rows * chan * 1024, rows * chan * 4 + rows * 768),
        name="gather",
    )(where, *in_hbm(x, g, wr, wpt, we))
    if not sorted_here:
        table = jnp.array(plan.masks, jnp.int32)
        cut = sums[0].reshape(plan.count, size, width // cr, cr).transpose(0, 2, 1, 3)
        lay = lambda head, index: jnp.concatenate([head, cut[index].reshape(-1, cr)])
        kept = lay(kept, where[0] ^ table)
        sent = lay(sent, where[0] ^ plan.core ^ table)
    return rdp, wcat, kept, sent


def step_kernel(head, ins, parts, *refs):
    terms, outs = refs[:ins], refs[ins:]

    def total(start, size):
        value = terms[0][start : start + size]
        for ref in terms[1:]:
            value = value + ref[start : start + size]
        return value

    nodes = total(0, head)
    rest = terms[0].shape[0] - head
    if parts == 1:
        outs[0][...] = nodes
        outs[1][...] = total(head, rest)
        return
    size = rest // parts
    for k, ref in enumerate(outs):
        ref[:head] = nodes
        ref[head:] = total(head + k * size, size)


def step(head, parts, terms):
    rest, lanes = terms[0].shape[0] - head, terms[0].shape[1]
    shapes = (head, rest) if parts == 1 else (head + rest // parts,) * parts
    return pl.pallas_call(
        functools.partial(step_kernel, head, len(terms), parts),
        in_specs=[VMEM] * len(terms),
        out_specs=[VMEM] * len(shapes),
        out_shape=[pltpu.VMEM((size, lanes), F32) for size in shapes],
        compiler_params=params(SMALL_LIMIT),
        cost_estimate=cost(terms[0].size, 12 * terms[0].size),
        name="step",
    )(*terms)


def fetch_kernel(_, *refs):
    sems = refs[-1]
    count = len(refs) // 2
    copies = [
        pltpu.make_async_copy(src, dst, sems.at[k])
        for k, (src, dst) in enumerate(zip(refs[:count], refs[count:-1]))
    ]
    for copy in copies:
        copy.start()
    for copy in copies:
        copy.wait()


def fetch(after, *values):
    return pl.pallas_call(
        fetch_kernel,
        in_specs=[pl.BlockSpec(memory_space=pl.ANY)] + [HBM] * len(values),
        out_specs=[VMEM] * len(values),
        out_shape=[pltpu.VMEM(value.shape, value.dtype) for value in values],
        scratch_shapes=[pltpu.SemaphoreType.DMA((len(values),))],
        compiler_params=params(SMALL_LIMIT),
        cost_estimate=cost(0, sum(value.size * value.dtype.itemsize for value in values)),
        name="fetch",
    )(after, *in_hbm(*values))


def feature_kernel(
    step, scale, plan, where_ref, mine_ref, other_ref, sums_ref, adj_ref, nw_ref, wcat_ref, rdp_ref, g_ref,
    out_hbm, gr_ref, gp_ref, ge_ref, ga_ref, gn_ref, out_ref, mix_ref, dnb_ref, out_sem,
):
    nodes_n, cr = mine_ref.shape
    rows = g_ref.shape[0]
    wide = 2 * cr
    first = plan.side(where_ref[0]) == 0
    mine, other = mine_ref[...], other_ref[...]
    nodes = scale * jnp.where(first, mine, other)
    d_node_out = jnp.where(first, other, mine)
    adj, nw = adj_ref[...], nw_ref[...]
    hidden = nodes - exact(adj, nodes)
    pre = exact(hidden, nw)
    node_out = jnp.maximum(pre, 0.0).astype(BF16)
    d_pre = jnp.where(pre > 0.0, d_node_out, 0.0)
    d_hidden = exact(d_pre, nw, ((1,), (1,)))
    d_nodes = d_hidden - exact(adj, d_hidden, ((0,), (0,)))
    dn = d_nodes.astype(BF16)
    no_f, dn_f = node_out.astype(F32), dn.astype(F32)
    dnb_ref[:nodes_n] = dn
    dnb_ref[nodes_n:] = jnp.zeros((nodes_n, cr), BF16)
    blank = jnp.zeros((cr, cr), BF16)
    zero = jnp.zeros((nodes_n, cr), F32)
    mix_ref[:cr, :cr] = jnp.concatenate([dn_f, zero], axis=0).T.astype(BF16)
    mix_ref[cr:, :cr] = blank
    mix_ref[:cr, cr:] = blank
    mix_ref[cr:, cr:] = jnp.concatenate([no_f, zero], axis=0).T.astype(BF16)
    copies = []
    for i, start in enumerate(range(0, rows, step)):
        c = pl.ds(start, step)
        rdp = rdp_ref[c]
        mixed = mxu(rdp[:, :wide], mix_ref[...])
        d_proj = (mixed[:, cr:] + scale * mixed[:, :cr]).astype(BF16)
        d_red = (scale * mxu(rdp[:, wide:], dnb_ref[...])).astype(BF16)
        both = jnp.concatenate([d_red, d_proj], axis=1)
        out = g_ref[c].astype(F32) + mxu(both, wcat_ref[...], ((1,), (1,)))
        out_ref[c] = out.astype(BF16)
        copies.append(pltpu.make_async_copy(out_ref.at[c], out_hbm.at[c], out_sem.at[i]))
        copies[-1].start()
    gn_ref[...] = scale * exact(hidden, d_pre, ((0,), (0,)))
    ga_ref[...] = -scale * exact(d_hidden, nodes, ((1,), (1,)))
    size = gr_ref.shape[0]
    x_red, x_dm, with_proj = (sums_ref[k * size : (k + 1) * size] for k in range(3))
    gr_ref[...] = scale * scale * exact(with_proj[:, :nodes_n], dn_f)
    gp_ref[...] = scale * exact(x_dm, no_f, ((1,), (1,))) + scale * scale * exact(
        x_red, dn_f, ((1,), (1,))
    )
    ge_ref[...] = scale * exact(with_proj[:, nodes_n:], no_f)
    for copy in copies:
        copy.wait()


def feature_grads(plan, where, mine, other, sums, adjacency, node_weight, wcat, rdp, g, scale):
    rows, chan = g.shape
    nodes, cr = adjacency.shape[0], node_weight.shape[0]
    step = row_block(rows // 2)
    size = chan // plan.count
    there = [
        pltpu.with_memory_space_constraint(value, pltpu.VMEM)
        for value in (mine, other, sums, adjacency, node_weight, wcat, rdp, g)
    ]
    return pl.pallas_call(
        functools.partial(feature_kernel, step, scale, plan),
        in_specs=[SMEM] + [VMEM] * len(there),
        out_specs=[HBM] + [VMEM] * 5,
        out_shape=[
            pltpu.HBM((rows, chan), BF16),
            jax.ShapeDtypeStruct((size, cr), F32),
            jax.ShapeDtypeStruct((size, nodes), F32),
            jax.ShapeDtypeStruct((size, cr), F32),
            jax.ShapeDtypeStruct((nodes, nodes), F32),
            jax.ShapeDtypeStruct((cr, cr), F32),
        ],
        scratch_shapes=[
            pltpu.VMEM((rows, chan), BF16),
            pltpu.VMEM((2 * cr, 2 * cr), BF16),
            pltpu.VMEM((2 * nodes, cr), BF16),
            pltpu.SemaphoreType.DMA((rows // step,)),
        ],
        compiler_params=params(),
        cost_estimate=cost(2 * rows * 4 * 65536, rows * chan * 4 + rows * 768),
        name="feature_grads",
    )(where, *there)


def on_device(
    plan, features, cotangent, reduce_weight, project_weight, expand_weight, adjacency, node_weight
):
    size_x, size_y, size_z, chan = features.shape
    local = size_x * size_y * size_z
    scale = 1.0 / math.sqrt(local * plan.count)
    flat_x = features.transpose(0, 2, 1, 3).reshape(local, chan)
    flat_g = cotangent.transpose(0, 2, 1, 3).reshape(local, chan)
    me = lax.axis_index(AXES).astype(jnp.int32)
    where = me.reshape(1)

    rdp, wcat, kept, sent = gather(
        plan, where, flat_x, flat_g, reduce_weight, project_weight.T, expand_weight
    )
    head = adjacency.shape[0]
    terms = [kept, plan.swap(sent, plan.core)]
    for group in plan.groups:
        parts = step(head, len(group), terms)
        terms = [plan.swap(part, mask) if mask else part for part, mask in zip(parts, group)]
    ready = fetch(terms[1], adjacency, node_weight, wcat, rdp, flat_g)
    mine, sums = step(head, 1, terms)
    other = plan.swap(mine, plan.core)

    flat_out, grad_reduce, grad_project, grad_expand, grad_adjacency, grad_node = feature_grads(
        plan, where, mine, other, sums, *ready, scale
    )
    grad_features = flat_out.reshape(size_x, size_z, size_y, chan).transpose(0, 2, 1, 3)
    return (grad_features, grad_reduce, grad_project, grad_expand, grad_adjacency, grad_node)


def solution(mesh):
    return jax.shard_map(
        functools.partial(on_device, Plan(mesh)),
        mesh=mesh,
        in_specs=(P("gx", "gy", "gz", None), P("gx", "gy", "gz", None), P(), P(), P(), P(), P()),
        out_specs=(
            P("gx", "gy", "gz", None),
            P(AXES, None),
            P(AXES, None),
            P(AXES, None),
            P(),
            P(),
        ),
        check_vma=False,
    )
```

```python
import functools
import math

import jax
import jax.numpy as jnp
from jax import lax
from jax.experimental import pallas as pl
from jax.experimental.pallas import tpu as pltpu
from jax.sharding import PartitionSpec as P

AXES = ("gx", "gy", "gz")
F32 = jnp.float32
BF16 = jnp.bfloat16
HBM = pl.BlockSpec(memory_space=pltpu.HBM)
VMEM = pl.BlockSpec(memory_space=pltpu.VMEM)
SMEM = pl.BlockSpec(memory_space=pltpu.SMEM)
VMEM_LIMIT = 24 * 1024 * 1024
SMALL_LIMIT = 4 * 1024 * 1024


def exact(a, b, dims=((1,), (0,))):
    return lax.dot_general(
        a, b, (dims, ((), ())), precision=lax.Precision.HIGHEST, preferred_element_type=F32
    )


def mxu(a, b, dims=((1,), (0,))):
    return lax.dot_general(a, b, (dims, ((), ())), preferred_element_type=F32)


def params(limit=VMEM_LIMIT):
    return pltpu.CompilerParams(vmem_limit_bytes=limit)


def cost(flops, nbytes):
    return pl.CostEstimate(flops=flops, bytes_accessed=nbytes, transcendentals=0)


def in_hbm(*values):
    return [pltpu.with_memory_space_constraint(value, pltpu.HBM) for value in values]


def row_block(total):
    for size in (1024, 768, 512, 384, 256, 128, 64, 32, 16):
        if total % size == 0:
            return size
    return total


class Plan:
    def __init__(self, mesh):
        size = {axis: mesh.shape[axis] for axis in AXES}
        self.count = math.prod(size.values())
        stride = {"gx": size["gy"] * size["gz"], "gy": size["gz"], "gz": 1}
        self.core = stride["gy"]
        spans = (
            (range(size["gx"]), stride["gx"]),
            (range(size["gy"] // 2), 2 * stride["gy"]),
            ([0, *range(2, size["gz"]), 1], stride["gz"]),
        )
        self.groups = [[k * step for k in order] for order, step in spans if len(order) > 1]
        self.masks = [0]
        for group in self.groups:
            self.masks = [mask | bits for mask in self.masks for bits in group]

    def side(self, device):
        return lax.bitwise_and(lax.div(device, jnp.int32(self.core)), jnp.int32(1))

    def swap(self, value, mask):
        return lax.ppermute(value, AXES, [(d, d ^ mask) for d in range(self.count)])


def gather_kernel(
    plan, cuts, sorted_here, where_ref, x_hbm, g_hbm, wr_hbm, wpt_hbm, we_hbm, rdp_hbm, wcat_hbm, *rest
):
    if sorted_here:
        kept_ref, sent_ref, turned_ref, *rest = rest
    else:
        keep_ref, send_ref, turned_ref, *rest = rest
    x_ref, g_ref, rdp_ref, cat_ref, wpt_ref, we_ref, sums_ref, term_ref, small_sem, in_sem, out_sem = rest
    cr = we_ref.shape[1]
    nodes = wpt_ref.shape[0]
    wide = 2 * cr
    move = pltpu.make_async_copy
    small = [
        move(wr_hbm, cat_ref.at[:, pl.ds(0, cr)], small_sem.at[0]),
        move(wpt_hbm, wpt_ref, small_sem.at[1]),
        move(we_hbm, we_ref, small_sem.at[2]),
    ]
    spans = [pl.ds(start, stop - start) for start, stop in zip(cuts, cuts[1:])]
    x_loads = [move(x_hbm.at[c], x_ref.at[c], in_sem.at[0, i]) for i, c in enumerate(spans)]
    g_loads = [move(g_hbm.at[c], g_ref.at[c], in_sem.at[1, i]) for i, c in enumerate(spans)]
    stores = [move(rdp_ref.at[c], rdp_hbm.at[c], out_sem.at[i]) for i, c in enumerate(spans)]
    for copy in (*small, x_loads[0], g_loads[0]):
        copy.start()
    small[0].wait()
    small[1].wait()
    padded = jnp.concatenate([wpt_ref[...], jnp.zeros_like(wpt_ref)], axis=0)
    cat_ref[:, cr:] = padded.T
    keep_weights = move(cat_ref, wcat_hbm, small_sem.at[3])
    small[2].wait()
    for i, c in enumerate(spans):
        x_loads[i].wait()
        if i + 1 < len(spans):
            x_loads[i + 1].start()
        both = mxu(x_ref[c], cat_ref[...]).astype(BF16)
        g_loads[i].wait()
        if i + 1 < len(spans):
            g_loads[i + 1].start()
        mapped = mxu(g_ref[c], we_ref[...]).astype(BF16)
        rdp = jnp.concatenate([both[:, :cr], mapped, both[:, cr:]], axis=1)
        rdp_ref[c] = rdp
        stores[i].start()
        turned = rdp.T
        proj = turned[wide : wide + nodes]
        pieces = (
            (sums_ref.at[: wide + nodes], mxu(turned[: wide + nodes], x_ref[c])),
            (sums_ref.at[wide + nodes :], mxu(proj, g_ref[c])),
            (term_ref, mxu(proj, rdp[:, :wide])),
        )
        for ref, piece in pieces:
            ref[...] = piece if i == 0 else ref[...] + piece
    keep_weights.start()

    me = where_ref[0]
    side = plan.side(me)
    turned_ref[...] = sums_ref[...].T
    if not sorted_here:
        heads = (keep_ref, send_ref)
    else:
        heads = (kept_ref.at[:nodes], sent_ref.at[:nodes])
    left, right = term_ref[:, :cr], term_ref[:, cr:]
    heads[0][...] = jnp.where(side == 0, left, right)
    heads[1][...] = jnp.where(side == 0, right, left)
    if sorted_here:
        size = turned_ref.shape[0] // plan.count
        for base, out_ref in ((me, kept_ref), (me ^ plan.core, sent_ref)):
            to = nodes
            for mask in plan.masks:
                at = pl.multiple_of((base ^ mask) * size, size)
                block = turned_ref[pl.ds(at, size), :]
                for lane in range(0, block.shape[1], cr):
                    out_ref[to : to + size] = block[:, lane : lane + cr]
                    to += size
    for copy in (keep_weights, *stores):
        copy.wait()


def gather(plan, where, x, g, wr, wpt, we):
    rows, chan = x.shape
    cr, nodes = wr.shape[1], wpt.shape[0]
    cuts = sorted({0, rows // 6 // 16 * 16, rows // 2 // 16 * 16, rows})
    width = 2 * cr + 2 * nodes
    half = plan.count // 2
    size = chan // plan.count
    sorted_here = size % 8 == 0
    outs = [
        (HBM, pltpu.HBM((rows, width), BF16)),
        (HBM, pltpu.HBM((chan, cr + 2 * nodes), BF16)),
    ]
    scratch = []
    if sorted_here:
        outs += [(VMEM, pltpu.VMEM((nodes + half * size * width // cr, cr), F32))] * 2
        scratch += [pltpu.VMEM((chan, width), F32)]
    else:
        outs += [(VMEM, jax.ShapeDtypeStruct((nodes, cr), F32))] * 2
        outs += [(VMEM, jax.ShapeDtypeStruct((chan, width), F32))]
    scratch += [
        pltpu.VMEM((rows, chan), BF16),
        pltpu.VMEM((rows, chan), BF16),
        pltpu.VMEM((rows, width), BF16),
        pltpu.VMEM((chan, cr + 2 * nodes), BF16),
        pltpu.VMEM(wpt.shape, BF16),
        pltpu.VMEM(we.shape, BF16),
        pltpu.VMEM((width, chan), F32),
        pltpu.VMEM((nodes, 2 * cr), F32),
        pltpu.SemaphoreType.DMA((4,)),
        pltpu.SemaphoreType.DMA((2, 3)),
        pltpu.SemaphoreType.DMA((3,)),
    ]
    rdp, wcat, kept, sent, *sums = pl.pallas_call(
        functools.partial(gather_kernel, plan, cuts, sorted_here),
        in_specs=[SMEM] + [HBM] * 5,
        out_specs=[spec for spec, _ in outs],
        out_shape=[shape for _, shape in outs],
        scratch_shapes=scratch,
        compiler_params=params(),
        cost_estimate=cost(2 * rows * chan * 1024, rows * chan * 4 + rows * 768),
        name="gather",
    )(where, *in_hbm(x, g, wr, wpt, we))
    if not sorted_here:
        table = jnp.array(plan.masks, jnp.int32)
        cut = sums[0].reshape(plan.count, size, width // cr, cr).transpose(0, 2, 1, 3)
        lay = lambda head, index: jnp.concatenate([head, cut[index].reshape(-1, cr)])
        kept = lay(kept, where[0] ^ table)
        sent = lay(sent, where[0] ^ plan.core ^ table)
    return rdp, wcat, kept, sent


def step_kernel(head, ins, parts, after, *refs):
    terms, outs = refs[:ins], refs[ins + after :]

    def total(start, size):
        value = terms[0][start : start + size]
        for ref in terms[1:]:
            value = value + ref[start : start + size]
        return value

    nodes = total(0, head)
    rest = terms[0].shape[0] - head
    if parts == 1:
        outs[0][...] = nodes
        outs[1][...] = total(head, rest)
        return
    size = rest // parts
    for k, ref in enumerate(outs):
        ref[:head] = nodes
        ref[head:] = total(head + k * size, size)


def step(head, parts, terms, after=()):
    rest, lanes = terms[0].shape[0] - head, terms[0].shape[1]
    shapes = (head, rest) if parts == 1 else (head + rest // parts,) * parts
    return pl.pallas_call(
        functools.partial(step_kernel, head, len(terms), parts, len(after)),
        in_specs=[VMEM] * len(terms) + [pl.BlockSpec(memory_space=pl.ANY)] * len(after),
        out_specs=[VMEM] * len(shapes),
        out_shape=[pltpu.VMEM((size, lanes), F32) for size in shapes],
        compiler_params=params(SMALL_LIMIT),
        cost_estimate=cost(terms[0].size, 12 * terms[0].size),
        name="step",
    )(*terms, *after)


def fetch_kernel(_, *refs):
    sems = refs[-1]
    count = len(refs) // 2
    copies = [
        pltpu.make_async_copy(src, dst, sems.at[k])
        for k, (src, dst) in enumerate(zip(refs[:count], refs[count:-1]))
    ]
    for copy in copies:
        copy.start()
    for copy in copies:
        copy.wait()


def fetch(after, *values):
    return pl.pallas_call(
        fetch_kernel,
        in_specs=[pl.BlockSpec(memory_space=pl.ANY)] + [HBM] * len(values),
        out_specs=[VMEM] * len(values),
        out_shape=[pltpu.VMEM(value.shape, value.dtype) for value in values],
        scratch_shapes=[pltpu.SemaphoreType.DMA((len(values),))],
        compiler_params=params(SMALL_LIMIT),
        cost_estimate=cost(0, sum(value.size * value.dtype.itemsize for value in values)),
        name="fetch",
    )(after, *in_hbm(*values))


def feature_kernel(
    step, scale, plan, where_ref, mine_ref, other_ref, sums_ref, adj_ref, nw_ref, wcat_ref, rdp_ref, g_ref,
    out_hbm, gr_ref, gp_ref, ge_ref, ga_ref, gn_ref, out_ref, mix_ref, dnb_ref, out_sem,
):
    nodes_n, cr = mine_ref.shape
    rows = g_ref.shape[0]
    wide = 2 * cr
    first = plan.side(where_ref[0]) == 0
    mine, other = mine_ref[...], other_ref[...]
    nodes = scale * jnp.where(first, mine, other)
    d_node_out = jnp.where(first, other, mine)
    adj, nw = adj_ref[...], nw_ref[...]
    hidden = nodes - exact(adj, nodes)
    pre = exact(hidden, nw)
    node_out = jnp.maximum(pre, 0.0).astype(BF16)
    d_pre = jnp.where(pre > 0.0, d_node_out, 0.0)
    d_hidden = exact(d_pre, nw, ((1,), (1,)))
    d_nodes = d_hidden - exact(adj, d_hidden, ((0,), (0,)))
    dn = d_nodes.astype(BF16)
    no_f, dn_f = node_out.astype(F32), dn.astype(F32)
    dnb_ref[:nodes_n] = dn
    dnb_ref[nodes_n:] = jnp.zeros((nodes_n, cr), BF16)
    blank = jnp.zeros((cr, cr), BF16)
    zero = jnp.zeros((nodes_n, cr), F32)
    mix_ref[:cr, :cr] = jnp.concatenate([dn_f, zero], axis=0).T.astype(BF16)
    mix_ref[cr:, :cr] = blank
    mix_ref[:cr, cr:] = blank
    mix_ref[cr:, cr:] = jnp.concatenate([no_f, zero], axis=0).T.astype(BF16)
    copies = []
    for i, start in enumerate(range(0, rows, step)):
        c = pl.ds(start, step)
        rdp = rdp_ref[c]
        mixed = mxu(rdp[:, :wide], mix_ref[...])
        d_proj = (mixed[:, cr:] + scale * mixed[:, :cr]).astype(BF16)
        d_red = (scale * mxu(rdp[:, wide:], dnb_ref[...])).astype(BF16)
        both = jnp.concatenate([d_red, d_proj], axis=1)
        out = g_ref[c].astype(F32) + mxu(both, wcat_ref[...], ((1,), (1,)))
        out_ref[c] = out.astype(BF16)
        copies.append(pltpu.make_async_copy(out_ref.at[c], out_hbm.at[c], out_sem.at[i]))
        copies[-1].start()
    gn_ref[...] = scale * exact(hidden, d_pre, ((0,), (0,)))
    ga_ref[...] = -scale * exact(d_hidden, nodes, ((1,), (1,)))
    size = gr_ref.shape[0]
    x_red, x_dm, with_proj = (sums_ref[k * size : (k + 1) * size] for k in range(3))
    gr_ref[...] = scale * scale * exact(with_proj[:, :nodes_n], dn_f)
    gp_ref[...] = scale * exact(x_dm, no_f, ((1,), (1,))) + scale * scale * exact(
        x_red, dn_f, ((1,), (1,))
    )
    ge_ref[...] = scale * exact(with_proj[:, nodes_n:], no_f)
    for copy in copies:
        copy.wait()


def feature_grads(plan, where, mine, other, sums, adjacency, node_weight, wcat, rdp, g, scale):
    rows, chan = g.shape
    nodes, cr = adjacency.shape[0], node_weight.shape[0]
    step = row_block(rows // 2)
    size = chan // plan.count
    there = [
        pltpu.with_memory_space_constraint(value, pltpu.VMEM)
        for value in (mine, other, sums, adjacency, node_weight, wcat, rdp, g)
    ]
    return pl.pallas_call(
        functools.partial(feature_kernel, step, scale, plan),
        in_specs=[SMEM] + [VMEM] * len(there),
        out_specs=[HBM] + [VMEM] * 5,
        out_shape=[
            pltpu.HBM((rows, chan), BF16),
            jax.ShapeDtypeStruct((size, cr), F32),
            jax.ShapeDtypeStruct((size, nodes), F32),
            jax.ShapeDtypeStruct((size, cr), F32),
            jax.ShapeDtypeStruct((nodes, nodes), F32),
            jax.ShapeDtypeStruct((cr, cr), F32),
        ],
        scratch_shapes=[
            pltpu.VMEM((rows, chan), BF16),
            pltpu.VMEM((2 * cr, 2 * cr), BF16),
            pltpu.VMEM((2 * nodes, cr), BF16),
            pltpu.SemaphoreType.DMA((rows // step,)),
        ],
        compiler_params=params(),
        cost_estimate=cost(2 * rows * 4 * 65536, rows * chan * 4 + rows * 768),
        name="feature_grads",
    )(where, *there)


def on_device(
    plan, features, cotangent, reduce_weight, project_weight, expand_weight, adjacency, node_weight
):
    size_x, size_y, size_z, chan = features.shape
    local = size_x * size_y * size_z
    scale = 1.0 / math.sqrt(local * plan.count)
    flat_x = features.transpose(0, 2, 1, 3).reshape(local, chan)
    flat_g = cotangent.transpose(0, 2, 1, 3).reshape(local, chan)
    me = lax.axis_index(AXES).astype(jnp.int32)
    where = me.reshape(1)

    rdp, wcat, kept, sent = gather(
        plan, where, flat_x, flat_g, reduce_weight, project_weight.T, expand_weight
    )
    head = adjacency.shape[0]
    terms = [kept, plan.swap(sent, plan.core)]
    for group in plan.groups:
        parts = step(head, len(group), terms)
        terms = [plan.swap(part, mask) if mask else part for part, mask in zip(parts, group)]
    ready = fetch(terms[1], adjacency, node_weight, wcat, rdp, flat_g)
    mine, sums = step(head, 1, terms, ready[:1])
    other = plan.swap(mine, plan.core)

    flat_out, grad_reduce, grad_project, grad_expand, grad_adjacency, grad_node = feature_grads(
        plan, where, mine, other, sums, *ready, scale
    )
    grad_features = flat_out.reshape(size_x, size_z, size_y, chan).transpose(0, 2, 1, 3)
    return (grad_features, grad_reduce, grad_project, grad_expand, grad_adjacency, grad_node)


def solution(mesh):
    return jax.shard_map(
        functools.partial(on_device, Plan(mesh)),
        mesh=mesh,
        in_specs=(P("gx", "gy", "gz", None), P("gx", "gy", "gz", None), P(), P(), P(), P(), P()),
        out_specs=(
            P("gx", "gy", "gz", None),
            P(AXES, None),
            P(AXES, None),
            P(AXES, None),
            P(),
            P(),
        ),
        check_vma=False,
    )
```

```python
import functools
import math

import jax
import jax.numpy as jnp
from jax import lax
from jax.experimental import pallas as pl
from jax.experimental.pallas import tpu as pltpu
from jax.sharding import PartitionSpec as P

AXES = ("gx", "gy", "gz")
F32 = jnp.float32
BF16 = jnp.bfloat16
HBM = pl.BlockSpec(memory_space=pltpu.HBM)
VMEM = pl.BlockSpec(memory_space=pltpu.VMEM)
SMEM = pl.BlockSpec(memory_space=pltpu.SMEM)
VMEM_LIMIT = 24 * 1024 * 1024
SMALL_LIMIT = 4 * 1024 * 1024


def exact(a, b, dims=((1,), (0,))):
    return lax.dot_general(
        a, b, (dims, ((), ())), precision=lax.Precision.HIGHEST, preferred_element_type=F32
    )


def mxu(a, b, dims=((1,), (0,))):
    return lax.dot_general(a, b, (dims, ((), ())), preferred_element_type=F32)


def params(limit=VMEM_LIMIT):
    return pltpu.CompilerParams(vmem_limit_bytes=limit)


def cost(flops, nbytes):
    return pl.CostEstimate(flops=flops, bytes_accessed=nbytes, transcendentals=0)


def in_hbm(*values):
    return [pltpu.with_memory_space_constraint(value, pltpu.HBM) for value in values]


def row_block(total, largest):
    for size in (1024, 768, 512, 384, 256, 128, 64, 32, 16):
        if size <= largest and total % size == 0:
            return size
    return total


class Plan:
    def __init__(self, mesh):
        size = {axis: mesh.shape[axis] for axis in AXES}
        self.count = math.prod(size.values())
        stride = {"gx": size["gy"] * size["gz"], "gy": size["gz"], "gz": 1}
        self.core = stride["gy"]
        spans = (
            ([0, *sorted(range(1, size["gx"]), key=lambda k: -k.bit_count())], stride["gx"]),
            (range(size["gy"] // 2), 2 * stride["gy"]),
            ([0, *range(2, size["gz"]), 1], stride["gz"]),
        )
        self.groups = [[k * step for k in order] for order, step in spans if len(order) > 1]
        self.masks = [0]
        for group in self.groups:
            self.masks = [mask | bits for mask in self.masks for bits in group]

    def side(self, device):
        return lax.bitwise_and(lax.div(device, jnp.int32(self.core)), jnp.int32(1))

    def swap(self, value, mask):
        return lax.ppermute(value, AXES, [(d, d ^ mask) for d in range(self.count)])


def gather_kernel(
    plan, step, sorted_here, where_ref, x_hbm, g_hbm, wr_hbm, wpt_hbm, we_hbm, rdp_hbm, wcat_hbm, *rest
):
    if sorted_here:
        kept_ref, sent_ref, turned_ref, *rest = rest
    else:
        keep_ref, send_ref, turned_ref, *rest = rest
    x_ref, g_ref, rdp_ref, cat_ref, wpt_ref, we_ref, sums_ref, term_ref, small_sem, in_sem, out_sem = rest
    rows = x_ref.shape[0]
    cr = we_ref.shape[1]
    nodes = wpt_ref.shape[0]
    wide = 2 * cr
    count = rows // step
    move = pltpu.make_async_copy
    small = [
        move(wr_hbm, cat_ref.at[:, pl.ds(0, cr)], small_sem.at[0]),
        move(wpt_hbm, wpt_ref, small_sem.at[1]),
        move(we_hbm, we_ref, small_sem.at[2]),
    ]
    load_cuts = sorted({0, min(1, count), min(2, count), count})
    store_cuts = sorted({0, max(count - 2, 0), max(count - 1, 0), count})
    span = lambda cuts, i: pl.ds(cuts[i] * step, (cuts[i + 1] - cuts[i]) * step)
    loads = [
        (
            move(x_hbm.at[span(load_cuts, i)], x_ref.at[span(load_cuts, i)], in_sem.at[0, i]),
            move(g_hbm.at[span(load_cuts, i)], g_ref.at[span(load_cuts, i)], in_sem.at[1, i]),
        )
        for i in range(len(load_cuts) - 1)
    ]
    stores = [
        move(rdp_ref.at[span(store_cuts, i)], rdp_hbm.at[span(store_cuts, i)], out_sem.at[i])
        for i in range(len(store_cuts) - 1)
    ]
    for copy in (*small, *loads[0]):
        copy.start()
    sums_ref[...] = jnp.zeros_like(sums_ref)
    term_ref[...] = jnp.zeros_like(term_ref)
    small[0].wait()
    small[1].wait()
    padded = jnp.concatenate([wpt_ref[...], jnp.zeros_like(wpt_ref)], axis=0)
    cat_ref[:, cr:] = padded.T
    keep_weights = move(cat_ref, wcat_hbm, small_sem.at[3])
    keep_weights.start()
    small[2].wait()

    @pl.loop(0, count)
    def _(i):
        for k, pair in enumerate(loads):
            @pl.when(i == load_cuts[k])
            def _():
                for copy in pair:
                    copy.wait()
                if k + 1 < len(loads):
                    for copy in loads[k + 1]:
                        copy.start()

        c = pl.ds(pl.multiple_of(i * step, step), step)
        x, g = x_ref[c], g_ref[c]
        both = mxu(x, cat_ref[...]).astype(BF16)
        mapped = mxu(g, we_ref[...]).astype(BF16)
        rdp = jnp.concatenate([both[:, :cr], mapped, both[:, cr:]], axis=1)
        rdp_ref[c] = rdp
        turned = rdp.T
        proj = turned[wide : wide + nodes]
        sums_ref[: wide + nodes] += mxu(turned[: wide + nodes], x)
        sums_ref[wide + nodes :] += mxu(proj, g)
        term_ref[...] += mxu(proj, rdp[:, :wide])
        for k, copy in enumerate(stores):
            pl.when(i == store_cuts[k + 1] - 1)(copy.start)

    me = where_ref[0]
    side = plan.side(me)
    turned_ref[...] = sums_ref[...].T
    if not sorted_here:
        heads = (keep_ref, send_ref)
    else:
        heads = (kept_ref.at[:nodes], sent_ref.at[:nodes])
    left, right = term_ref[:, :cr], term_ref[:, cr:]
    heads[0][...] = jnp.where(side == 0, left, right)
    heads[1][...] = jnp.where(side == 0, right, left)
    if sorted_here:
        size = turned_ref.shape[0] // plan.count
        for base, out_ref in ((me, kept_ref), (me ^ plan.core, sent_ref)):
            to = nodes
            for mask in plan.masks:
                at = pl.multiple_of((base ^ mask) * size, size)
                block = turned_ref[pl.ds(at, size), :]
                for lane in range(0, block.shape[1], cr):
                    out_ref[to : to + size] = block[:, lane : lane + cr]
                    to += size
    for copy in (keep_weights, *stores):
        copy.wait()


def gather(plan, where, x, g, wr, wpt, we):
    rows, chan = x.shape
    cr, nodes = wr.shape[1], wpt.shape[0]
    step = row_block(rows, 1024)
    width = 2 * cr + 2 * nodes
    half = plan.count // 2
    size = chan // plan.count
    sorted_here = size % 8 == 0
    outs = [
        (HBM, pltpu.HBM((rows, width), BF16)),
        (HBM, pltpu.HBM((chan, cr + 2 * nodes), BF16)),
    ]
    scratch = []
    if sorted_here:
        outs += [(VMEM, pltpu.VMEM((nodes + half * size * width // cr, cr), F32))] * 2
        scratch += [pltpu.VMEM((chan, width), F32)]
    else:
        outs += [(VMEM, jax.ShapeDtypeStruct((nodes, cr), F32))] * 2
        outs += [(VMEM, jax.ShapeDtypeStruct((chan, width), F32))]
    scratch += [
        pltpu.VMEM((rows, chan), BF16),
        pltpu.VMEM((rows, chan), BF16),
        pltpu.VMEM((rows, width), BF16),
        pltpu.VMEM((chan, cr + 2 * nodes), BF16),
        pltpu.VMEM(wpt.shape, BF16),
        pltpu.VMEM(we.shape, BF16),
        pltpu.VMEM((width, chan), F32),
        pltpu.VMEM((nodes, 2 * cr), F32),
        pltpu.SemaphoreType.DMA((4,)),
        pltpu.SemaphoreType.DMA((2, 3)),
        pltpu.SemaphoreType.DMA((3,)),
    ]
    rdp, wcat, kept, sent, *sums = pl.pallas_call(
        functools.partial(gather_kernel, plan, step, sorted_here),
        in_specs=[SMEM] + [HBM] * 5,
        out_specs=[spec for spec, _ in outs],
        out_shape=[shape for _, shape in outs],
        scratch_shapes=scratch,
        compiler_params=params(),
        cost_estimate=cost(2 * rows * chan * 1024, rows * chan * 4 + rows * 768),
        name="gather",
    )(where, *in_hbm(x, g, wr, wpt, we))
    if not sorted_here:
        table = jnp.array(plan.masks, jnp.int32)
        cut = sums[0].reshape(plan.count, size, width // cr, cr).transpose(0, 2, 1, 3)
        lay = lambda head, index: jnp.concatenate([head, cut[index].reshape(-1, cr)])
        kept = lay(kept, where[0] ^ table)
        sent = lay(sent, where[0] ^ plan.core ^ table)
    return rdp, wcat, kept, sent


def step_kernel(head, ins, parts, after, *refs):
    terms, outs = refs[:ins], refs[ins + after :]

    def total(start, size):
        value = terms[0][start : start + size]
        for ref in terms[1:]:
            value = value + ref[start : start + size]
        return value

    nodes = total(0, head)
    rest = terms[0].shape[0] - head
    if parts == 1:
        outs[0][...] = nodes
        outs[1][...] = total(head, rest)
        return
    size = rest // parts
    for k, ref in enumerate(outs):
        ref[:head] = nodes
        ref[head:] = total(head + k * size, size)


def step(head, parts, terms, after=()):
    rest, lanes = terms[0].shape[0] - head, terms[0].shape[1]
    shapes = (head, rest) if parts == 1 else (head + rest // parts,) * parts
    return pl.pallas_call(
        functools.partial(step_kernel, head, len(terms), parts, len(after)),
        in_specs=[VMEM] * len(terms) + [pl.BlockSpec(memory_space=pl.ANY)] * len(after),
        out_specs=[VMEM] * len(shapes),
        out_shape=[pltpu.VMEM((size, lanes), F32) for size in shapes],
        compiler_params=params(SMALL_LIMIT),
        cost_estimate=cost(terms[0].size, 12 * terms[0].size),
        name="step",
    )(*terms, *after)


def fetch_kernel(_, *refs):
    sems = refs[-1]
    count = len(refs) // 2
    copies = [
        pltpu.make_async_copy(src, dst, sems.at[k])
        for k, (src, dst) in enumerate(zip(refs[:count], refs[count:-1]))
    ]
    for copy in copies:
        copy.start()
    for copy in copies:
        copy.wait()


def fetch(after, *values):
    return pl.pallas_call(
        fetch_kernel,
        in_specs=[pl.BlockSpec(memory_space=pl.ANY)] + [HBM] * len(values),
        out_specs=[VMEM] * len(values),
        out_shape=[pltpu.VMEM(value.shape, value.dtype) for value in values],
        scratch_shapes=[pltpu.SemaphoreType.DMA((len(values),))],
        compiler_params=params(SMALL_LIMIT),
        cost_estimate=cost(0, sum(value.size * value.dtype.itemsize for value in values)),
        name="fetch",
    )(after, *in_hbm(*values))


def feature_kernel(
    step, scale, plan, where_ref, mine_ref, other_ref, sums_ref, adj_ref, nw_ref, wcat_ref, rdp_ref, g_ref,
    out_hbm, gr_ref, gp_ref, ge_ref, ga_ref, gn_ref, out_ref, mix_ref, dnb_ref, out_sem,
):
    nodes_n, cr = mine_ref.shape
    rows = g_ref.shape[0]
    wide = 2 * cr
    first = plan.side(where_ref[0]) == 0
    mine, other = mine_ref[...], other_ref[...]
    nodes = scale * jnp.where(first, mine, other)
    d_node_out = jnp.where(first, other, mine)
    adj, nw = adj_ref[...], nw_ref[...]
    hidden = nodes - exact(adj, nodes)
    pre = exact(hidden, nw)
    node_out = jnp.maximum(pre, 0.0).astype(BF16)
    d_pre = jnp.where(pre > 0.0, d_node_out, 0.0)
    d_hidden = exact(d_pre, nw, ((1,), (1,)))
    d_nodes = d_hidden - exact(adj, d_hidden, ((0,), (0,)))
    dn = d_nodes.astype(BF16)
    no_f, dn_f = node_out.astype(F32), dn.astype(F32)
    dnb_ref[:nodes_n] = dn
    dnb_ref[nodes_n:] = jnp.zeros((nodes_n, cr), BF16)
    blank = jnp.zeros((cr, cr), BF16)
    zero = jnp.zeros((nodes_n, cr), F32)
    mix_ref[:cr, :cr] = jnp.concatenate([dn_f, zero], axis=0).T.astype(BF16)
    mix_ref[cr:, :cr] = blank
    mix_ref[:cr, cr:] = blank
    mix_ref[cr:, cr:] = jnp.concatenate([no_f, zero], axis=0).T.astype(BF16)
    def store(i, at):
        c = pl.ds(at, step)
        return pltpu.make_async_copy(out_ref.at[c], out_hbm.at[c], out_sem.at[i])

    @pl.loop(0, rows // step)
    def _(i):
        at = pl.multiple_of(i * step, step)
        c = pl.ds(at, step)
        rdp = rdp_ref[c]
        mixed = mxu(rdp[:, :wide], mix_ref[...])
        d_proj = (mixed[:, cr:] + scale * mixed[:, :cr]).astype(BF16)
        d_red = (scale * mxu(rdp[:, wide:], dnb_ref[...])).astype(BF16)
        both = jnp.concatenate([d_red, d_proj], axis=1)
        out = g_ref[c].astype(F32) + mxu(both, wcat_ref[...], ((1,), (1,)))
        out_ref[c] = out.astype(BF16)
        store(i, at).start()

    gn_ref[...] = scale * exact(hidden, d_pre, ((0,), (0,)))
    ga_ref[...] = -scale * exact(d_hidden, nodes, ((1,), (1,)))
    size = gr_ref.shape[0]
    x_red, x_dm, with_proj = (sums_ref[k * size : (k + 1) * size] for k in range(3))
    gr_ref[...] = scale * scale * exact(with_proj[:, :nodes_n], dn_f)
    gp_ref[...] = scale * exact(x_dm, no_f, ((1,), (1,))) + scale * scale * exact(
        x_red, dn_f, ((1,), (1,))
    )
    ge_ref[...] = scale * exact(with_proj[:, nodes_n:], no_f)
    for i in range(rows // step):
        store(i, i * step).wait()


def feature_grads(plan, where, mine, other, sums, adjacency, node_weight, wcat, rdp, g, scale):
    rows, chan = g.shape
    nodes, cr = adjacency.shape[0], node_weight.shape[0]
    step = row_block(rows, 512)
    size = chan // plan.count
    there = [
        pltpu.with_memory_space_constraint(value, pltpu.VMEM)
        for value in (mine, other, sums, adjacency, node_weight, wcat, rdp, g)
    ]
    return pl.pallas_call(
        functools.partial(feature_kernel, step, scale, plan),
        in_specs=[SMEM] + [VMEM] * len(there),
        out_specs=[HBM] + [VMEM] * 5,
        out_shape=[
            pltpu.HBM((rows, chan), BF16),
            jax.ShapeDtypeStruct((size, cr), F32),
            jax.ShapeDtypeStruct((size, nodes), F32),
            jax.ShapeDtypeStruct((size, cr), F32),
            jax.ShapeDtypeStruct((nodes, nodes), F32),
            jax.ShapeDtypeStruct((cr, cr), F32),
        ],
        scratch_shapes=[
            pltpu.VMEM((rows, chan), BF16),
            pltpu.VMEM((2 * cr, 2 * cr), BF16),
            pltpu.VMEM((2 * nodes, cr), BF16),
            pltpu.SemaphoreType.DMA((rows // step,)),
        ],
        compiler_params=params(),
        cost_estimate=cost(2 * rows * 4 * 65536, rows * chan * 4 + rows * 768),
        name="feature_grads",
    )(where, *there)


def on_device(
    plan, features, cotangent, reduce_weight, project_weight, expand_weight, adjacency, node_weight
):
    size_x, size_y, size_z, chan = features.shape
    local = size_x * size_y * size_z
    scale = 1.0 / math.sqrt(local * plan.count)
    flat_x = features.transpose(0, 2, 1, 3).reshape(local, chan)
    flat_g = cotangent.transpose(0, 2, 1, 3).reshape(local, chan)
    me = lax.axis_index(AXES).astype(jnp.int32)
    where = me.reshape(1)

    rdp, wcat, kept, sent = gather(
        plan, where, flat_x, flat_g, reduce_weight, project_weight.T, expand_weight
    )
    head = adjacency.shape[0]
    terms = [kept, plan.swap(sent, plan.core)]
    ready = None
    for group in plan.groups:
        parts = step(head, len(group), terms, ready[:1] if ready else ())
        terms = [plan.swap(part, mask) if mask else part for part, mask in zip(parts, group)]
        ready = ready or fetch(terms[1], adjacency, node_weight, wcat, rdp, flat_g)
    mine, sums = step(head, 1, terms)
    other = plan.swap(mine, plan.core)

    flat_out, grad_reduce, grad_project, grad_expand, grad_adjacency, grad_node = feature_grads(
        plan, where, mine, other, sums, *ready, scale
    )
    grad_features = flat_out.reshape(size_x, size_z, size_y, chan).transpose(0, 2, 1, 3)
    return (grad_features, grad_reduce, grad_project, grad_expand, grad_adjacency, grad_node)


def solution(mesh):
    return jax.shard_map(
        functools.partial(on_device, Plan(mesh)),
        mesh=mesh,
        in_specs=(P("gx", "gy", "gz", None), P("gx", "gy", "gz", None), P(), P(), P(), P(), P()),
        out_specs=(
            P("gx", "gy", "gz", None),
            P(AXES, None),
            P(AXES, None),
            P(AXES, None),
            P(),
            P(),
        ),
        check_vma=False,
    )
```

```python
import functools
import math

import jax
import jax.numpy as jnp
from jax import lax
from jax.experimental import pallas as pl
from jax.experimental.pallas import tpu as pltpu
from jax.sharding import PartitionSpec as P

AXES = ("gx", "gy", "gz")
F32 = jnp.float32
BF16 = jnp.bfloat16
HBM = pl.BlockSpec(memory_space=pltpu.HBM)
VMEM = pl.BlockSpec(memory_space=pltpu.VMEM)
SMEM = pl.BlockSpec(memory_space=pltpu.SMEM)
VMEM_LIMIT = 24 * 1024 * 1024
SMALL_LIMIT = 4 * 1024 * 1024


def exact(a, b, dims=((1,), (0,))):
    return lax.dot_general(
        a, b, (dims, ((), ())), precision=lax.Precision.HIGHEST, preferred_element_type=F32
    )


def mxu(a, b, dims=((1,), (0,))):
    return lax.dot_general(a, b, (dims, ((), ())), preferred_element_type=F32)


def params(limit=VMEM_LIMIT):
    return pltpu.CompilerParams(vmem_limit_bytes=limit)


def cost(flops, nbytes):
    return pl.CostEstimate(flops=flops, bytes_accessed=nbytes, transcendentals=0)


def in_hbm(*values):
    return [pltpu.with_memory_space_constraint(value, pltpu.HBM) for value in values]


def row_block(total, largest):
    for size in (1536, 1024, 768, 512, 384, 256, 128, 64, 32, 16):
        if size <= largest and total % size == 0:
            return size
    return total


class Plan:
    def __init__(self, mesh):
        size = {axis: mesh.shape[axis] for axis in AXES}
        self.count = math.prod(size.values())
        stride = {"gx": size["gy"] * size["gz"], "gy": size["gz"], "gz": 1}
        self.core = stride["gy"]
        spans = (
            ([0, *sorted(range(1, size["gx"]), key=lambda k: -k.bit_count())], stride["gx"]),
            (range(size["gy"] // 2), 2 * stride["gy"]),
            ([0, *range(2, size["gz"]), 1], stride["gz"]),
        )
        self.groups = [[k * step for k in order] for order, step in spans if len(order) > 1]
        self.masks = [0]
        for group in self.groups:
            self.masks = [mask | bits for mask in self.masks for bits in group]

    def side(self, device):
        return lax.bitwise_and(lax.div(device, jnp.int32(self.core)), jnp.int32(1))

    def swap(self, value, mask):
        return lax.ppermute(value, AXES, [(d, d ^ mask) for d in range(self.count)])


def gather_kernel(
    plan, step, sorted_here, where_ref, x_hbm, g_hbm, wr_hbm, wpt_hbm, we_hbm, rdp_hbm, wcat_hbm, *rest
):
    if sorted_here:
        kept_ref, sent_ref, turned_ref, *rest = rest
    else:
        keep_ref, send_ref, turned_ref, *rest = rest
    x_ref, g_ref, rdp_ref, cat_ref, wpt_ref, we_ref, sums_ref, term_ref, small_sem, in_sem, out_sem = rest
    rows = x_ref.shape[0]
    cr = we_ref.shape[1]
    nodes = wpt_ref.shape[0]
    wide = 2 * cr
    count = rows // step
    move = pltpu.make_async_copy
    small = [
        move(wr_hbm, cat_ref.at[:, pl.ds(0, cr)], small_sem.at[0]),
        move(wpt_hbm, wpt_ref, small_sem.at[1]),
        move(we_hbm, we_ref, small_sem.at[2]),
    ]
    load_cuts = sorted({0, min(1, count), min(2, count), count})
    store_cuts = sorted({0, max(count - 2, 0), max(count - 1, 0), count})
    span = lambda cuts, i: pl.ds(cuts[i] * step, (cuts[i + 1] - cuts[i]) * step)
    loads = [
        (
            move(x_hbm.at[span(load_cuts, i)], x_ref.at[span(load_cuts, i)], in_sem.at[0, i]),
            move(g_hbm.at[span(load_cuts, i)], g_ref.at[span(load_cuts, i)], in_sem.at[1, i]),
        )
        for i in range(len(load_cuts) - 1)
    ]
    stores = [
        move(rdp_ref.at[span(store_cuts, i)], rdp_hbm.at[span(store_cuts, i)], out_sem.at[i])
        for i in range(len(store_cuts) - 1)
    ]
    for copy in (*small, *loads[0]):
        copy.start()
    sums_ref[...] = jnp.zeros_like(sums_ref)
    term_ref[...] = jnp.zeros_like(term_ref)
    small[0].wait()
    small[1].wait()
    padded = jnp.concatenate([wpt_ref[...], jnp.zeros_like(wpt_ref)], axis=0)
    cat_ref[:, cr:] = padded.T
    keep_weights = move(cat_ref, wcat_hbm, small_sem.at[3])
    keep_weights.start()
    small[2].wait()

    @pl.loop(0, count)
    def _(i):
        for k, pair in enumerate(loads):
            @pl.when(i == load_cuts[k])
            def _():
                for copy in pair:
                    copy.wait()
                if k + 1 < len(loads):
                    for copy in loads[k + 1]:
                        copy.start()

        c = pl.ds(pl.multiple_of(i * step, step), step)
        x, g = x_ref[c], g_ref[c]
        both = mxu(x, cat_ref[...]).astype(BF16)
        mapped = mxu(g, we_ref[...]).astype(BF16)
        rdp = jnp.concatenate([both[:, :cr], mapped, both[:, cr:]], axis=1)
        rdp_ref[c] = rdp
        turned = rdp.T
        proj = turned[wide : wide + nodes]
        sums_ref[: wide + nodes] += mxu(turned[: wide + nodes], x)
        sums_ref[wide + nodes :] += mxu(proj, g)
        term_ref[...] += mxu(proj, rdp[:, :wide])
        for k, copy in enumerate(stores):
            pl.when(i == store_cuts[k + 1] - 1)(copy.start)

    me = where_ref[0]
    side = plan.side(me)
    turned_ref[...] = sums_ref[...].T
    if not sorted_here:
        heads = (keep_ref, send_ref)
    else:
        heads = (kept_ref.at[:nodes], sent_ref.at[:nodes])
    left, right = term_ref[:, :cr], term_ref[:, cr:]
    heads[0][...] = jnp.where(side == 0, left, right)
    heads[1][...] = jnp.where(side == 0, right, left)
    if sorted_here:
        size = turned_ref.shape[0] // plan.count
        for base, out_ref in ((me, kept_ref), (me ^ plan.core, sent_ref)):
            to = nodes
            for mask in plan.masks:
                at = pl.multiple_of((base ^ mask) * size, size)
                block = turned_ref[pl.ds(at, size), :]
                for lane in range(0, block.shape[1], cr):
                    out_ref[to : to + size] = block[:, lane : lane + cr]
                    to += size
    for copy in (keep_weights, *stores):
        copy.wait()


def gather(plan, where, x, g, wr, wpt, we):
    rows, chan = x.shape
    cr, nodes = wr.shape[1], wpt.shape[0]
    step = row_block(rows, 1536)
    width = 2 * cr + 2 * nodes
    half = plan.count // 2
    size = chan // plan.count
    sorted_here = size % 8 == 0
    outs = [
        (HBM, pltpu.HBM((rows, width), BF16)),
        (HBM, pltpu.HBM((chan, cr + 2 * nodes), BF16)),
    ]
    scratch = []
    if sorted_here:
        outs += [(VMEM, pltpu.VMEM((nodes + half * size * width // cr, cr), F32))] * 2
        scratch += [pltpu.VMEM((chan, width), F32)]
    else:
        outs += [(VMEM, jax.ShapeDtypeStruct((nodes, cr), F32))] * 2
        outs += [(VMEM, jax.ShapeDtypeStruct((chan, width), F32))]
    scratch += [
        pltpu.VMEM((rows, chan), BF16),
        pltpu.VMEM((rows, chan), BF16),
        pltpu.VMEM((rows, width), BF16),
        pltpu.VMEM((chan, cr + 2 * nodes), BF16),
        pltpu.VMEM(wpt.shape, BF16),
        pltpu.VMEM(we.shape, BF16),
        pltpu.VMEM((width, chan), F32),
        pltpu.VMEM((nodes, 2 * cr), F32),
        pltpu.SemaphoreType.DMA((4,)),
        pltpu.SemaphoreType.DMA((2, 3)),
        pltpu.SemaphoreType.DMA((3,)),
    ]
    rdp, wcat, kept, sent, *sums = pl.pallas_call(
        functools.partial(gather_kernel, plan, step, sorted_here),
        in_specs=[SMEM] + [HBM] * 5,
        out_specs=[spec for spec, _ in outs],
        out_shape=[shape for _, shape in outs],
        scratch_shapes=scratch,
        compiler_params=params(),
        cost_estimate=cost(2 * rows * chan * 1024, rows * chan * 4 + rows * 768),
        name="gather",
    )(where, *in_hbm(x, g, wr, wpt, we))
    if not sorted_here:
        table = jnp.array(plan.masks, jnp.int32)
        cut = sums[0].reshape(plan.count, size, width // cr, cr).transpose(0, 2, 1, 3)
        lay = lambda head, index: jnp.concatenate([head, cut[index].reshape(-1, cr)])
        kept = lay(kept, where[0] ^ table)
        sent = lay(sent, where[0] ^ plan.core ^ table)
    return rdp, wcat, kept, sent


def step_kernel(head, ins, parts, after, *refs):
    terms, outs = refs[:ins], refs[ins + after :]

    def total(start, size):
        value = terms[0][start : start + size]
        for ref in terms[1:]:
            value = value + ref[start : start + size]
        return value

    nodes = total(0, head)
    rest = terms[0].shape[0] - head
    if parts == 1:
        outs[0][...] = nodes
        outs[1][...] = total(head, rest)
        return
    size = rest // parts
    for k, ref in enumerate(outs):
        ref[:head] = nodes
        ref[head:] = total(head + k * size, size)


def step(head, parts, terms, after=()):
    rest, lanes = terms[0].shape[0] - head, terms[0].shape[1]
    shapes = (head, rest) if parts == 1 else (head + rest // parts,) * parts
    return pl.pallas_call(
        functools.partial(step_kernel, head, len(terms), parts, len(after)),
        in_specs=[VMEM] * len(terms) + [pl.BlockSpec(memory_space=pl.ANY)] * len(after),
        out_specs=[VMEM] * len(shapes),
        out_shape=[pltpu.VMEM((size, lanes), F32) for size in shapes],
        compiler_params=params(SMALL_LIMIT),
        cost_estimate=cost(terms[0].size, 12 * terms[0].size),
        name="step",
    )(*terms, *after)


def fetch_kernel(_, *refs):
    sems = refs[-1]
    count = len(refs) // 2
    copies = [
        pltpu.make_async_copy(src, dst, sems.at[k])
        for k, (src, dst) in enumerate(zip(refs[:count], refs[count:-1]))
    ]
    for copy in copies:
        copy.start()
    for copy in copies:
        copy.wait()


def fetch(after, *values):
    return pl.pallas_call(
        fetch_kernel,
        in_specs=[pl.BlockSpec(memory_space=pl.ANY)] + [HBM] * len(values),
        out_specs=[VMEM] * len(values),
        out_shape=[pltpu.VMEM(value.shape, value.dtype) for value in values],
        scratch_shapes=[pltpu.SemaphoreType.DMA((len(values),))],
        compiler_params=params(SMALL_LIMIT),
        cost_estimate=cost(0, sum(value.size * value.dtype.itemsize for value in values)),
        name="fetch",
    )(after, *in_hbm(*values))


def feature_kernel(
    cuts, scale, plan, where_ref, mine_ref, other_ref, sums_ref, adj_ref, nw_ref, wcat_ref, rdp_ref, g_ref,
    out_hbm, gr_ref, gp_ref, ge_ref, ga_ref, gn_ref, out_ref, mix_ref, dnb_ref, out_sem,
):
    nodes_n, cr = mine_ref.shape
    wide = 2 * cr
    first = plan.side(where_ref[0]) == 0
    mine, other = mine_ref[...], other_ref[...]
    nodes = scale * jnp.where(first, mine, other)
    d_node_out = jnp.where(first, other, mine)
    adj, nw = adj_ref[...], nw_ref[...]
    hidden = nodes - exact(adj, nodes)
    pre = exact(hidden, nw)
    node_out = jnp.maximum(pre, 0.0).astype(BF16)
    d_pre = jnp.where(pre > 0.0, d_node_out, 0.0)
    d_hidden = exact(d_pre, nw, ((1,), (1,)))
    d_nodes = d_hidden - exact(adj, d_hidden, ((0,), (0,)))
    dn = d_nodes.astype(BF16)
    no_f, dn_f = node_out.astype(F32), dn.astype(F32)
    dnb_ref[:nodes_n] = dn
    dnb_ref[nodes_n:] = jnp.zeros((nodes_n, cr), BF16)
    blank = jnp.zeros((cr, cr), BF16)
    zero = jnp.zeros((nodes_n, cr), F32)
    mix_ref[:cr, :cr] = jnp.concatenate([dn_f, zero], axis=0).T.astype(BF16)
    mix_ref[cr:, :cr] = blank
    mix_ref[:cr, cr:] = blank
    mix_ref[cr:, cr:] = jnp.concatenate([no_f, zero], axis=0).T.astype(BF16)
    copies = []
    for i, (start, stop) in enumerate(zip(cuts, cuts[1:])):
        c = pl.ds(start, stop - start)
        rdp = rdp_ref[c]
        mixed = mxu(rdp[:, :wide], mix_ref[...])
        d_proj = (mixed[:, cr:] + scale * mixed[:, :cr]).astype(BF16)
        d_red = (scale * mxu(rdp[:, wide:], dnb_ref[...])).astype(BF16)
        both = jnp.concatenate([d_red, d_proj], axis=1)
        out = g_ref[c].astype(F32) + mxu(both, wcat_ref[...], ((1,), (1,)))
        out_ref[c] = out.astype(BF16)
        copies.append(pltpu.make_async_copy(out_ref.at[c], out_hbm.at[c], out_sem.at[i]))
        copies[-1].start()
    gn_ref[...] = scale * exact(hidden, d_pre, ((0,), (0,)))
    ga_ref[...] = -scale * exact(d_hidden, nodes, ((1,), (1,)))
    size = gr_ref.shape[0]
    x_red, x_dm, with_proj = (sums_ref[k * size : (k + 1) * size] for k in range(3))
    gr_ref[...] = scale * scale * exact(with_proj[:, :nodes_n], dn_f)
    gp_ref[...] = scale * exact(x_dm, no_f, ((1,), (1,))) + scale * scale * exact(
        x_red, dn_f, ((1,), (1,))
    )
    ge_ref[...] = scale * exact(with_proj[:, nodes_n:], no_f)
    for copy in copies:
        copy.wait()


def feature_grads(plan, where, mine, other, sums, adjacency, node_weight, wcat, rdp, g, scale):
    rows, chan = g.shape
    nodes, cr = adjacency.shape[0], node_weight.shape[0]
    unit = row_block(rows // 12, 256)
    cuts = sorted({0, *(rows - k * unit for k in (1, 4, 8) if k * unit < rows), rows})
    size = chan // plan.count
    there = [
        pltpu.with_memory_space_constraint(value, pltpu.VMEM)
        for value in (mine, other, sums, adjacency, node_weight, wcat, rdp, g)
    ]
    return pl.pallas_call(
        functools.partial(feature_kernel, cuts, scale, plan),
        in_specs=[SMEM] + [VMEM] * len(there),
        out_specs=[HBM] + [VMEM] * 5,
        out_shape=[
            pltpu.HBM((rows, chan), BF16),
            jax.ShapeDtypeStruct((size, cr), F32),
            jax.ShapeDtypeStruct((size, nodes), F32),
            jax.ShapeDtypeStruct((size, cr), F32),
            jax.ShapeDtypeStruct((nodes, nodes), F32),
            jax.ShapeDtypeStruct((cr, cr), F32),
        ],
        scratch_shapes=[
            pltpu.VMEM((rows, chan), BF16),
            pltpu.VMEM((2 * cr, 2 * cr), BF16),
            pltpu.VMEM((2 * nodes, cr), BF16),
            pltpu.SemaphoreType.DMA((len(cuts) - 1,)),
        ],
        compiler_params=params(),
        cost_estimate=cost(2 * rows * 4 * 65536, rows * chan * 4 + rows * 768),
        name="feature_grads",
    )(where, *there)


def on_device(
    plan, features, cotangent, reduce_weight, project_weight, expand_weight, adjacency, node_weight
):
    size_x, size_y, size_z, chan = features.shape
    local = size_x * size_y * size_z
    scale = 1.0 / math.sqrt(local * plan.count)
    flat_x = features.transpose(0, 2, 1, 3).reshape(local, chan)
    flat_g = cotangent.transpose(0, 2, 1, 3).reshape(local, chan)
    me = lax.axis_index(AXES).astype(jnp.int32)
    where = me.reshape(1)

    rdp, wcat, kept, sent = gather(
        plan, where, flat_x, flat_g, reduce_weight, project_weight.T, expand_weight
    )
    head = adjacency.shape[0]
    terms = [kept, plan.swap(sent, plan.core)]
    ready = None
    for group in plan.groups:
        parts = step(head, len(group), terms, ready[:1] if ready else ())
        terms = [plan.swap(part, mask) if mask else part for part, mask in zip(parts, group)]
        ready = ready or fetch(parts[0], adjacency, node_weight, wcat, rdp, flat_g)
    mine, sums = step(head, 1, terms)
    other = plan.swap(mine, plan.core)

    flat_out, grad_reduce, grad_project, grad_expand, grad_adjacency, grad_node = feature_grads(
        plan, where, mine, other, sums, *ready, scale
    )
    grad_features = flat_out.reshape(size_x, size_z, size_y, chan).transpose(0, 2, 1, 3)
    return (grad_features, grad_reduce, grad_project, grad_expand, grad_adjacency, grad_node)


def solution(mesh):
    return jax.shard_map(
        functools.partial(on_device, Plan(mesh)),
        mesh=mesh,
        in_specs=(P("gx", "gy", "gz", None), P("gx", "gy", "gz", None), P(), P(), P(), P(), P()),
        out_specs=(
            P("gx", "gy", "gz", None),
            P(AXES, None),
            P(AXES, None),
            P(AXES, None),
            P(),
            P(),
        ),
        check_vma=False,
    )
```

```python
import functools
import math

import jax
import jax.numpy as jnp
from jax import lax
from jax.experimental import pallas as pl
from jax.experimental.pallas import tpu as pltpu
from jax.sharding import PartitionSpec as P

AXES = ("gx", "gy", "gz")
F32 = jnp.float32
BF16 = jnp.bfloat16
HBM = pl.BlockSpec(memory_space=pltpu.HBM)
VMEM = pl.BlockSpec(memory_space=pltpu.VMEM)
SMEM = pl.BlockSpec(memory_space=pltpu.SMEM)
VMEM_LIMIT = 24 * 1024 * 1024
SMALL_LIMIT = 4 * 1024 * 1024


def exact(a, b, dims=((1,), (0,))):
    return lax.dot_general(
        a, b, (dims, ((), ())), precision=lax.Precision.HIGHEST, preferred_element_type=F32
    )


def mxu(a, b, dims=((1,), (0,))):
    return lax.dot_general(a, b, (dims, ((), ())), preferred_element_type=F32)


def params(limit=VMEM_LIMIT):
    return pltpu.CompilerParams(vmem_limit_bytes=limit)


def cost(flops, nbytes):
    return pl.CostEstimate(flops=flops, bytes_accessed=nbytes, transcendentals=0)


def in_hbm(*values):
    return [pltpu.with_memory_space_constraint(value, pltpu.HBM) for value in values]


def row_block(total, largest):
    for size in (1536, 1024, 768, 512, 384, 256, 128, 64, 32, 16):
        if size <= largest and total % size == 0:
            return size
    return total


class Plan:
    def __init__(self, mesh):
        size = {axis: mesh.shape[axis] for axis in AXES}
        self.count = math.prod(size.values())
        stride = {"gx": size["gy"] * size["gz"], "gy": size["gz"], "gz": 1}
        self.core = stride["gy"]
        spans = (
            ([0, *sorted(range(1, size["gx"]), key=lambda k: -k.bit_count())], stride["gx"]),
            (range(size["gy"] // 2), 2 * stride["gy"]),
            ([0, *range(2, size["gz"]), 1], stride["gz"]),
        )
        self.groups = [[k * step for k in order] for order, step in spans if len(order) > 1]
        self.masks = [0]
        for group in self.groups:
            self.masks = [mask | bits for mask in self.masks for bits in group]

    def side(self, device):
        return lax.bitwise_and(lax.div(device, jnp.int32(self.core)), jnp.int32(1))

    def swap(self, value, mask):
        return lax.ppermute(value, AXES, [(d, d ^ mask) for d in range(self.count)])


def gather_kernel(
    plan, step, sorted_here, where_ref, x_hbm, g_hbm, wr_hbm, wpt_hbm, we_hbm, rdp_hbm, wcat_hbm, *rest
):
    if sorted_here:
        kept_ref, sent_ref, turned_ref, *rest = rest
    else:
        keep_ref, send_ref, turned_ref, *rest = rest
    x_ref, g_ref, rdp_ref, cat_ref, wpt_ref, we_ref, sums_ref, term_ref, small_sem, in_sem, out_sem = rest
    rows = x_ref.shape[0]
    cr = we_ref.shape[1]
    nodes = wpt_ref.shape[0]
    wide = 2 * cr
    count = rows // step
    move = pltpu.make_async_copy
    small = [
        move(wr_hbm, cat_ref.at[:, pl.ds(0, cr)], small_sem.at[0]),
        move(wpt_hbm, wpt_ref, small_sem.at[1]),
        move(we_hbm, we_ref, small_sem.at[2]),
    ]
    load_cuts = sorted({0, min(1, count), min(2, count), count})
    store_cuts = sorted({0, max(count - 2, 0), max(count - 1, 0), count})
    span = lambda cuts, i: pl.ds(cuts[i] * step, (cuts[i + 1] - cuts[i]) * step)
    loads = [
        (
            move(x_hbm.at[span(load_cuts, i)], x_ref.at[span(load_cuts, i)], in_sem.at[0, i]),
            move(g_hbm.at[span(load_cuts, i)], g_ref.at[span(load_cuts, i)], in_sem.at[1, i]),
        )
        for i in range(len(load_cuts) - 1)
    ]
    stores = [
        move(rdp_ref.at[span(store_cuts, i)], rdp_hbm.at[span(store_cuts, i)], out_sem.at[i])
        for i in range(len(store_cuts) - 1)
    ]
    for copy in (*small, *loads[0]):
        copy.start()
    sums_ref[...] = jnp.zeros_like(sums_ref)
    term_ref[...] = jnp.zeros_like(term_ref)
    small[0].wait()
    small[1].wait()
    padded = jnp.concatenate([wpt_ref[...], jnp.zeros_like(wpt_ref)], axis=0)
    cat_ref[:, cr:] = padded.T
    keep_weights = move(cat_ref, wcat_hbm, small_sem.at[3])
    keep_weights.start()
    small[2].wait()

    @pl.loop(0, count)
    def _(i):
        def arrive(which):
            for k, pair in enumerate(loads):
                @pl.when(i == load_cuts[k])
                def _():
                    pair[which].wait()
                    if k + 1 < len(loads):
                        loads[k + 1][which].start()

        c = pl.ds(pl.multiple_of(i * step, step), step)
        arrive(0)
        x = x_ref[c]
        both = mxu(x, cat_ref[...]).astype(BF16)
        arrive(1)
        g = g_ref[c]
        mapped = mxu(g, we_ref[...]).astype(BF16)
        rdp = jnp.concatenate([both[:, :cr], mapped, both[:, cr:]], axis=1)
        rdp_ref[c] = rdp
        turned = rdp.T
        proj = turned[wide : wide + nodes]
        sums_ref[: wide + nodes] += mxu(turned[: wide + nodes], x)
        sums_ref[wide + nodes :] += mxu(proj, g)
        term_ref[...] += mxu(proj, rdp[:, :wide])
        for k, copy in enumerate(stores):
            pl.when(i == store_cuts[k + 1] - 1)(copy.start)

    me = where_ref[0]
    side = plan.side(me)
    turned_ref[...] = sums_ref[...].T
    if not sorted_here:
        heads = (keep_ref, send_ref)
    else:
        heads = (kept_ref.at[:nodes], sent_ref.at[:nodes])
    left, right = term_ref[:, :cr], term_ref[:, cr:]
    heads[0][...] = jnp.where(side == 0, left, right)
    heads[1][...] = jnp.where(side == 0, right, left)
    if sorted_here:
        size = turned_ref.shape[0] // plan.count
        for base, out_ref in ((me, kept_ref), (me ^ plan.core, sent_ref)):
            to = nodes
            for mask in plan.masks:
                at = pl.multiple_of((base ^ mask) * size, size)
                block = turned_ref[pl.ds(at, size), :]
                for lane in range(0, block.shape[1], cr):
                    out_ref[to : to + size] = block[:, lane : lane + cr]
                    to += size
    for copy in (keep_weights, *stores):
        copy.wait()


def gather(plan, where, x, g, wr, wpt, we):
    rows, chan = x.shape
    cr, nodes = wr.shape[1], wpt.shape[0]
    step = row_block(rows, 1536)
    width = 2 * cr + 2 * nodes
    half = plan.count // 2
    size = chan // plan.count
    sorted_here = size % 8 == 0
    outs = [
        (HBM, pltpu.HBM((rows, width), BF16)),
        (HBM, pltpu.HBM((chan, cr + 2 * nodes), BF16)),
    ]
    scratch = []
    if sorted_here:
        outs += [(VMEM, pltpu.VMEM((nodes + half * size * width // cr, cr), F32))] * 2
        scratch += [pltpu.VMEM((chan, width), F32)]
    else:
        outs += [(VMEM, jax.ShapeDtypeStruct((nodes, cr), F32))] * 2
        outs += [(VMEM, jax.ShapeDtypeStruct((chan, width), F32))]
    scratch += [
        pltpu.VMEM((rows, chan), BF16),
        pltpu.VMEM((rows, chan), BF16),
        pltpu.VMEM((rows, width), BF16),
        pltpu.VMEM((chan, cr + 2 * nodes), BF16),
        pltpu.VMEM(wpt.shape, BF16),
        pltpu.VMEM(we.shape, BF16),
        pltpu.VMEM((width, chan), F32),
        pltpu.VMEM((nodes, 2 * cr), F32),
        pltpu.SemaphoreType.DMA((4,)),
        pltpu.SemaphoreType.DMA((2, 3)),
        pltpu.SemaphoreType.DMA((3,)),
    ]
    rdp, wcat, kept, sent, *sums = pl.pallas_call(
        functools.partial(gather_kernel, plan, step, sorted_here),
        in_specs=[SMEM] + [HBM] * 5,
        out_specs=[spec for spec, _ in outs],
        out_shape=[shape for _, shape in outs],
        scratch_shapes=scratch,
        compiler_params=params(),
        cost_estimate=cost(2 * rows * chan * 1024, rows * chan * 4 + rows * 768),
        name="gather",
    )(where, *in_hbm(x, g, wr, wpt, we))
    if not sorted_here:
        table = jnp.array(plan.masks, jnp.int32)
        cut = sums[0].reshape(plan.count, size, width // cr, cr).transpose(0, 2, 1, 3)
        lay = lambda head, index: jnp.concatenate([head, cut[index].reshape(-1, cr)])
        kept = lay(kept, where[0] ^ table)
        sent = lay(sent, where[0] ^ plan.core ^ table)
    return rdp, wcat, kept, sent


def step_kernel(head, ins, parts, after, *refs):
    terms, outs = refs[:ins], refs[ins + after :]

    def total(start, size):
        value = terms[0][start : start + size]
        for ref in terms[1:]:
            value = value + ref[start : start + size]
        return value

    nodes = total(0, head)
    rest = terms[0].shape[0] - head
    if parts == 1:
        outs[0][...] = nodes
        outs[1][...] = total(head, rest)
        return
    size = rest // parts
    for k, ref in enumerate(outs):
        ref[:head] = nodes
        ref[head:] = total(head + k * size, size)


def step(head, parts, terms, after=()):
    rest, lanes = terms[0].shape[0] - head, terms[0].shape[1]
    shapes = (head, rest) if parts == 1 else (head + rest // parts,) * parts
    return pl.pallas_call(
        functools.partial(step_kernel, head, len(terms), parts, len(after)),
        in_specs=[VMEM] * len(terms) + [pl.BlockSpec(memory_space=pl.ANY)] * len(after),
        out_specs=[VMEM] * len(shapes),
        out_shape=[pltpu.VMEM((size, lanes), F32) for size in shapes],
        compiler_params=params(SMALL_LIMIT),
        cost_estimate=cost(terms[0].size, 12 * terms[0].size),
        name="step",
    )(*terms, *after)


def fetch_kernel(_, *refs):
    sems = refs[-1]
    count = len(refs) // 2
    copies = [
        pltpu.make_async_copy(src, dst, sems.at[k])
        for k, (src, dst) in enumerate(zip(refs[:count], refs[count:-1]))
    ]
    for copy in copies:
        copy.start()
    for copy in copies:
        copy.wait()


def fetch(after, *values):
    return pl.pallas_call(
        fetch_kernel,
        in_specs=[pl.BlockSpec(memory_space=pl.ANY)] + [HBM] * len(values),
        out_specs=[VMEM] * len(values),
        out_shape=[pltpu.VMEM(value.shape, value.dtype) for value in values],
        scratch_shapes=[pltpu.SemaphoreType.DMA((len(values),))],
        compiler_params=params(SMALL_LIMIT),
        cost_estimate=cost(0, sum(value.size * value.dtype.itemsize for value in values)),
        name="fetch",
    )(after, *in_hbm(*values))


def feature_kernel(
    cuts, scale, plan, where_ref, mine_ref, other_ref, sums_ref, adj_ref, nw_ref, wcat_ref, rdp_ref, g_ref,
    out_hbm, gr_ref, gp_ref, ge_ref, ga_ref, gn_ref, out_ref, mix_ref, dnb_ref, out_sem,
):
    nodes_n, cr = mine_ref.shape
    wide = 2 * cr
    first = plan.side(where_ref[0]) == 0
    mine, other = mine_ref[...], other_ref[...]
    nodes = scale * jnp.where(first, mine, other)
    d_node_out = jnp.where(first, other, mine)
    adj, nw = adj_ref[...], nw_ref[...]
    hidden = nodes - exact(adj, nodes)
    pre = exact(hidden, nw)
    node_out = jnp.maximum(pre, 0.0).astype(BF16)
    d_pre = jnp.where(pre > 0.0, d_node_out, 0.0)
    d_hidden = exact(d_pre, nw, ((1,), (1,)))
    d_nodes = d_hidden - exact(adj, d_hidden, ((0,), (0,)))
    dn = d_nodes.astype(BF16)
    no_f, dn_f = node_out.astype(F32), dn.astype(F32)
    dnb_ref[:nodes_n] = dn
    dnb_ref[nodes_n:] = jnp.zeros((nodes_n, cr), BF16)
    mix_ref[...] = jnp.zeros_like(mix_ref)
    mix_ref[:nodes_n, :cr] = dn
    mix_ref[cr : cr + nodes_n, cr:] = node_out
    copies = []
    for i, (start, stop) in enumerate(zip(cuts, cuts[1:])):
        c = pl.ds(start, stop - start)
        rdp = rdp_ref[c]
        mixed = mxu(rdp[:, :wide], mix_ref[...], ((1,), (1,)))
        d_proj = (mixed[:, cr:] + scale * mixed[:, :cr]).astype(BF16)
        d_red = (scale * mxu(rdp[:, wide:], dnb_ref[...])).astype(BF16)
        both = jnp.concatenate([d_red, d_proj], axis=1)
        out = g_ref[c].astype(F32) + mxu(both, wcat_ref[...], ((1,), (1,)))
        out_ref[c] = out.astype(BF16)
        copies.append(pltpu.make_async_copy(out_ref.at[c], out_hbm.at[c], out_sem.at[i]))
        copies[-1].start()
    gn_ref[...] = scale * exact(hidden, d_pre, ((0,), (0,)))
    ga_ref[...] = -scale * exact(d_hidden, nodes, ((1,), (1,)))
    size = gr_ref.shape[0]
    x_red, x_dm, with_proj = (sums_ref[k * size : (k + 1) * size] for k in range(3))
    gr_ref[...] = scale * scale * exact(with_proj[:, :nodes_n], dn_f)
    gp_ref[...] = scale * exact(x_dm, no_f, ((1,), (1,))) + scale * scale * exact(
        x_red, dn_f, ((1,), (1,))
    )
    ge_ref[...] = scale * exact(with_proj[:, nodes_n:], no_f)
    for copy in copies:
        copy.wait()


def feature_grads(plan, where, mine, other, sums, adjacency, node_weight, wcat, rdp, g, scale):
    rows, chan = g.shape
    nodes, cr = adjacency.shape[0], node_weight.shape[0]
    unit = row_block(rows // 12, 256)
    cuts = sorted({0, *(rows - k * unit for k in (1, 4, 8) if k * unit < rows), rows})
    size = chan // plan.count
    there = [
        pltpu.with_memory_space_constraint(value, pltpu.VMEM)
        for value in (mine, other, sums, adjacency, node_weight, wcat, rdp, g)
    ]
    return pl.pallas_call(
        functools.partial(feature_kernel, cuts, scale, plan),
        in_specs=[SMEM] + [VMEM] * len(there),
        out_specs=[HBM] + [VMEM] * 5,
        out_shape=[
            pltpu.HBM((rows, chan), BF16),
            jax.ShapeDtypeStruct((size, cr), F32),
            jax.ShapeDtypeStruct((size, nodes), F32),
            jax.ShapeDtypeStruct((size, cr), F32),
            jax.ShapeDtypeStruct((nodes, nodes), F32),
            jax.ShapeDtypeStruct((cr, cr), F32),
        ],
        scratch_shapes=[
            pltpu.VMEM((rows, chan), BF16),
            pltpu.VMEM((2 * cr, 2 * cr), BF16),
            pltpu.VMEM((2 * nodes, cr), BF16),
            pltpu.SemaphoreType.DMA((len(cuts) - 1,)),
        ],
        compiler_params=params(),
        cost_estimate=cost(2 * rows * 4 * 65536, rows * chan * 4 + rows * 768),
        name="feature_grads",
    )(where, *there)


def on_device(
    plan, features, cotangent, reduce_weight, project_weight, expand_weight, adjacency, node_weight
):
    size_x, size_y, size_z, chan = features.shape
    local = size_x * size_y * size_z
    scale = 1.0 / math.sqrt(local * plan.count)
    flat_x = features.transpose(0, 2, 1, 3).reshape(local, chan)
    flat_g = cotangent.transpose(0, 2, 1, 3).reshape(local, chan)
    me = lax.axis_index(AXES).astype(jnp.int32)
    where = me.reshape(1)

    rdp, wcat, kept, sent = gather(
        plan, where, flat_x, flat_g, reduce_weight, project_weight.T, expand_weight
    )
    head = adjacency.shape[0]
    terms = [kept, plan.swap(sent, plan.core)]
    ready = None
    for group in plan.groups:
        parts = step(head, len(group), terms, ready[:1] if ready else ())
        terms = [plan.swap(part, mask) if mask else part for part, mask in zip(parts, group)]
        ready = ready or fetch(parts[0], adjacency, node_weight, wcat, rdp, flat_g)
    mine, sums = step(head, 1, terms)
    other = plan.swap(mine, plan.core)

    flat_out, grad_reduce, grad_project, grad_expand, grad_adjacency, grad_node = feature_grads(
        plan, where, mine, other, sums, *ready, scale
    )
    grad_features = flat_out.reshape(size_x, size_z, size_y, chan).transpose(0, 2, 1, 3)
    return (grad_features, grad_reduce, grad_project, grad_expand, grad_adjacency, grad_node)


def solution(mesh):
    return jax.shard_map(
        functools.partial(on_device, Plan(mesh)),
        mesh=mesh,
        in_specs=(P("gx", "gy", "gz", None), P("gx", "gy", "gz", None), P(), P(), P(), P(), P()),
        out_specs=(
            P("gx", "gy", "gz", None),
            P(AXES, None),
            P(AXES, None),
            P(AXES, None),
            P(),
            P(),
        ),
        check_vma=False,
    )
```

```python
import functools
import math

import jax
import jax.numpy as jnp
from jax import lax
from jax.experimental import pallas as pl
from jax.experimental.pallas import tpu as pltpu
from jax.sharding import PartitionSpec as P

AXES = ("gx", "gy", "gz")
F32 = jnp.float32
BF16 = jnp.bfloat16
HBM = pl.BlockSpec(memory_space=pltpu.HBM)
VMEM = pl.BlockSpec(memory_space=pltpu.VMEM)
SMEM = pl.BlockSpec(memory_space=pltpu.SMEM)
VMEM_LIMIT = 24 * 1024 * 1024
SMALL_LIMIT = 4 * 1024 * 1024


def exact(a, b, dims=((1,), (0,))):
    return lax.dot_general(
        a, b, (dims, ((), ())), precision=lax.Precision.HIGHEST, preferred_element_type=F32
    )


def mxu(a, b, dims=((1,), (0,))):
    return lax.dot_general(a, b, (dims, ((), ())), preferred_element_type=F32)


def params(limit=VMEM_LIMIT):
    return pltpu.CompilerParams(vmem_limit_bytes=limit)


def cost(flops, nbytes):
    return pl.CostEstimate(flops=flops, bytes_accessed=nbytes, transcendentals=0)


def in_hbm(*values):
    return [pltpu.with_memory_space_constraint(value, pltpu.HBM) for value in values]


def row_block(total, largest):
    for size in (1536, 1024, 768, 512, 384, 256, 128, 64, 32, 16):
        if size <= largest and total % size == 0:
            return size
    return total


class Plan:
    def __init__(self, mesh):
        size = {axis: mesh.shape[axis] for axis in AXES}
        self.count = math.prod(size.values())
        stride = {"gx": size["gy"] * size["gz"], "gy": size["gz"], "gz": 1}
        self.core = stride["gy"]
        spans = (
            ([0, *sorted(range(1, size["gx"]), key=lambda k: -k.bit_count())], stride["gx"]),
            (range(size["gy"] // 2), 2 * stride["gy"]),
            ([0, *range(size["gz"] - 1, 0, -1)], stride["gz"]),
        )
        self.groups = [[k * step for k in order] for order, step in spans if len(order) > 1]
        self.masks = [0]
        for group in self.groups:
            self.masks = [mask | bits for mask in self.masks for bits in group]

    def side(self, device):
        return lax.bitwise_and(lax.div(device, jnp.int32(self.core)), jnp.int32(1))

    def swap(self, value, mask):
        return lax.ppermute(value, AXES, [(d, d ^ mask) for d in range(self.count)])


def gather_kernel(
    plan, step, sorted_here, where_ref, x_hbm, g_hbm, wr_hbm, wpt_hbm, we_hbm, rdp_hbm, wcat_hbm, *rest
):
    if sorted_here:
        kept_ref, sent_ref, turned_ref, *rest = rest
    else:
        keep_ref, send_ref, turned_ref, *rest = rest
    x_ref, g_ref, rdp_ref, cat_ref, wpt_ref, we_ref, sums_ref, term_ref, small_sem, in_sem, out_sem = rest
    rows = x_ref.shape[0]
    cr = we_ref.shape[1]
    nodes = wpt_ref.shape[0]
    wide = 2 * cr
    count = rows // step
    move = pltpu.make_async_copy
    small = [
        move(wr_hbm, cat_ref.at[:, pl.ds(0, cr)], small_sem.at[0]),
        move(wpt_hbm, wpt_ref, small_sem.at[1]),
        move(we_hbm, we_ref, small_sem.at[2]),
    ]
    spans = [pl.ds(start, step) for start in range(0, rows, step)]
    loads = [
        (
            move(x_hbm.at[c], x_ref.at[c], in_sem.at[0, i]),
            move(g_hbm.at[c], g_ref.at[c], in_sem.at[1, i]),
        )
        for i, c in enumerate(spans)
    ]
    stores = [move(rdp_ref.at[c], rdp_hbm.at[c], out_sem.at[i]) for i, c in enumerate(spans)]
    for copy in (*small, *loads[0]):
        copy.start()
    small[0].wait()
    small[1].wait()
    padded = jnp.concatenate([wpt_ref[...], jnp.zeros_like(wpt_ref)], axis=0)
    cat_ref[:, cr:] = padded.T
    keep_weights = move(cat_ref, wcat_hbm, small_sem.at[3])
    keep_weights.start()
    small[2].wait()
    for i, c in enumerate(spans):
        for copy in loads[i]:
            copy.wait()
        if i + 1 < count:
            for copy in loads[i + 1]:
                copy.start()
        x, g = x_ref[c], g_ref[c]
        both = mxu(x, cat_ref[...]).astype(BF16)
        mapped = mxu(g, we_ref[...]).astype(BF16)
        rdp = jnp.concatenate([both[:, :cr], mapped, both[:, cr:]], axis=1)
        rdp_ref[c] = rdp
        turned = rdp.T
        proj = turned[wide : wide + nodes]
        pieces = (
            (sums_ref.at[: wide + nodes], mxu(turned[: wide + nodes], x)),
            (sums_ref.at[wide + nodes :], mxu(proj, g)),
            (term_ref, mxu(proj, rdp[:, :wide])),
        )
        for ref, piece in pieces:
            ref[...] = ref[...] + piece if i else piece
        stores[i].start()

    me = where_ref[0]
    side = plan.side(me)
    turned_ref[...] = sums_ref[...].T
    if not sorted_here:
        heads = (keep_ref, send_ref)
    else:
        heads = (kept_ref.at[:nodes], sent_ref.at[:nodes])
    left, right = term_ref[:, :cr], term_ref[:, cr:]
    heads[0][...] = jnp.where(side == 0, left, right)
    heads[1][...] = jnp.where(side == 0, right, left)
    if sorted_here:
        size = turned_ref.shape[0] // plan.count
        for base, out_ref in ((me, kept_ref), (me ^ plan.core, sent_ref)):
            to = nodes
            for mask in plan.masks:
                at = pl.multiple_of((base ^ mask) * size, size)
                block = turned_ref[pl.ds(at, size), :]
                for lane in range(0, block.shape[1], cr):
                    out_ref[to : to + size] = block[:, lane : lane + cr]
                    to += size
    for copy in (keep_weights, *stores):
        copy.wait()


def gather(plan, where, x, g, wr, wpt, we):
    rows, chan = x.shape
    cr, nodes = wr.shape[1], wpt.shape[0]
    step = row_block(rows, 1536)
    width = 2 * cr + 2 * nodes
    half = plan.count // 2
    size = chan // plan.count
    sorted_here = size % 8 == 0
    outs = [
        (HBM, pltpu.HBM((rows, width), BF16)),
        (HBM, pltpu.HBM((chan, cr + 2 * nodes), BF16)),
    ]
    scratch = []
    if sorted_here:
        outs += [(VMEM, pltpu.VMEM((nodes + half * size * width // cr, cr), F32))] * 2
        scratch += [pltpu.VMEM((chan, width), F32)]
    else:
        outs += [(VMEM, jax.ShapeDtypeStruct((nodes, cr), F32))] * 2
        outs += [(VMEM, jax.ShapeDtypeStruct((chan, width), F32))]
    scratch += [
        pltpu.VMEM((rows, chan), BF16),
        pltpu.VMEM((rows, chan), BF16),
        pltpu.VMEM((rows, width), BF16),
        pltpu.VMEM((chan, cr + 2 * nodes), BF16),
        pltpu.VMEM(wpt.shape, BF16),
        pltpu.VMEM(we.shape, BF16),
        pltpu.VMEM((width, chan), F32),
        pltpu.VMEM((nodes, 2 * cr), F32),
        pltpu.SemaphoreType.DMA((4,)),
        pltpu.SemaphoreType.DMA((2, rows // step)),
        pltpu.SemaphoreType.DMA((rows // step,)),
    ]
    rdp, wcat, kept, sent, *sums = pl.pallas_call(
        functools.partial(gather_kernel, plan, step, sorted_here),
        in_specs=[SMEM] + [HBM] * 5,
        out_specs=[spec for spec, _ in outs],
        out_shape=[shape for _, shape in outs],
        scratch_shapes=scratch,
        compiler_params=params(),
        cost_estimate=cost(2 * rows * chan * 1024, rows * chan * 4 + rows * 768),
        name="gather",
    )(where, *in_hbm(x, g, wr, wpt, we))
    if not sorted_here:
        table = jnp.array(plan.masks, jnp.int32)
        cut = sums[0].reshape(plan.count, size, width // cr, cr).transpose(0, 2, 1, 3)
        lay = lambda head, index: jnp.concatenate([head, cut[index].reshape(-1, cr)])
        kept = lay(kept, where[0] ^ table)
        sent = lay(sent, where[0] ^ plan.core ^ table)
    return rdp, wcat, kept, sent


def step_kernel(head, ins, parts, after, *refs):
    terms, outs = refs[:ins], refs[ins + after :]

    def total(start, size):
        value = terms[0][start : start + size]
        for ref in terms[1:]:
            value = value + ref[start : start + size]
        return value

    nodes = total(0, head)
    rest = terms[0].shape[0] - head
    if parts == 1:
        outs[0][...] = nodes
        outs[1][...] = total(head, rest)
        return
    size = rest // parts
    for k, ref in enumerate(outs):
        ref[:head] = nodes
        ref[head:] = total(head + k * size, size)


def step(head, parts, terms, after=()):
    rest, lanes = terms[0].shape[0] - head, terms[0].shape[1]
    shapes = (head, rest) if parts == 1 else (head + rest // parts,) * parts
    return pl.pallas_call(
        functools.partial(step_kernel, head, len(terms), parts, len(after)),
        in_specs=[VMEM] * len(terms) + [pl.BlockSpec(memory_space=pl.ANY)] * len(after),
        out_specs=[VMEM] * len(shapes),
        out_shape=[pltpu.VMEM((size, lanes), F32) for size in shapes],
        compiler_params=params(SMALL_LIMIT),
        cost_estimate=cost(terms[0].size, 12 * terms[0].size),
        name="step",
    )(*terms, *after)


def fetch_kernel(_, *refs):
    sems = refs[-1]
    count = len(refs) // 2
    copies = [
        pltpu.make_async_copy(src, dst, sems.at[k])
        for k, (src, dst) in enumerate(zip(refs[:count], refs[count:-1]))
    ]
    for copy in copies:
        copy.start()
    for copy in copies:
        copy.wait()


def fetch(after, *values):
    return pl.pallas_call(
        fetch_kernel,
        in_specs=[pl.BlockSpec(memory_space=pl.ANY)] + [HBM] * len(values),
        out_specs=[VMEM] * len(values),
        out_shape=[pltpu.VMEM(value.shape, value.dtype) for value in values],
        scratch_shapes=[pltpu.SemaphoreType.DMA((len(values),))],
        compiler_params=params(SMALL_LIMIT),
        cost_estimate=cost(0, sum(value.size * value.dtype.itemsize for value in values)),
        name="fetch",
    )(after, *in_hbm(*values))


def feature_kernel(
    cuts, scale, plan, where_ref, mine_ref, other_ref, sums_ref, adj_ref, nw_ref, wcat_ref, rdp_ref, g_ref,
    out_hbm, gr_ref, gp_ref, ge_ref, ga_ref, gn_ref, out_ref, mix_ref, dnb_ref, out_sem,
):
    nodes_n, cr = mine_ref.shape
    wide = 2 * cr
    first = plan.side(where_ref[0]) == 0
    mine, other = mine_ref[...], other_ref[...]
    nodes = scale * jnp.where(first, mine, other)
    d_node_out = jnp.where(first, other, mine)
    adj, nw = adj_ref[...], nw_ref[...]
    hidden = nodes - exact(adj, nodes)
    pre = exact(hidden, nw)
    node_out = jnp.maximum(pre, 0.0).astype(BF16)
    d_pre = jnp.where(pre > 0.0, d_node_out, 0.0)
    d_hidden = exact(d_pre, nw, ((1,), (1,)))
    d_nodes = d_hidden - exact(adj, d_hidden, ((0,), (0,)))
    dn = d_nodes.astype(BF16)
    no_f, dn_f = node_out.astype(F32), dn.astype(F32)
    dnb_ref[:nodes_n] = dn
    dnb_ref[nodes_n:] = jnp.zeros((nodes_n, cr), BF16)
    mix_ref[...] = jnp.zeros_like(mix_ref)
    mix_ref[:nodes_n, :cr] = dn
    mix_ref[cr : cr + nodes_n, cr:] = node_out
    copies = []
    for i, (start, stop) in enumerate(zip(cuts, cuts[1:])):
        c = pl.ds(start, stop - start)
        rdp = rdp_ref[c]
        mixed = mxu(rdp[:, :wide], mix_ref[...], ((1,), (1,)))
        d_proj = (mixed[:, cr:] + scale * mixed[:, :cr]).astype(BF16)
        d_red = (scale * mxu(rdp[:, wide:], dnb_ref[...])).astype(BF16)
        both = jnp.concatenate([d_red, d_proj], axis=1)
        out = g_ref[c].astype(F32) + mxu(both, wcat_ref[...], ((1,), (1,)))
        out_ref[c] = out.astype(BF16)
        copies.append(pltpu.make_async_copy(out_ref.at[c], out_hbm.at[c], out_sem.at[i]))
        copies[-1].start()
    gn_ref[...] = scale * exact(hidden, d_pre, ((0,), (0,)))
    ga_ref[...] = -scale * exact(d_hidden, nodes, ((1,), (1,)))
    size = gr_ref.shape[0]
    x_red, x_dm, with_proj = (sums_ref[k * size : (k + 1) * size] for k in range(3))
    gr_ref[...] = scale * scale * exact(with_proj[:, :nodes_n], dn_f)
    gp_ref[...] = scale * exact(x_dm, no_f, ((1,), (1,))) + scale * scale * exact(
        x_red, dn_f, ((1,), (1,))
    )
    ge_ref[...] = scale * exact(with_proj[:, nodes_n:], no_f)
    for copy in copies:
        copy.wait()


def feature_grads(plan, where, mine, other, sums, adjacency, node_weight, wcat, rdp, g, scale):
    rows, chan = g.shape
    nodes, cr = adjacency.shape[0], node_weight.shape[0]
    unit = row_block(rows // 12, 256)
    cuts = sorted({0, *(rows - k * unit for k in (1, 4, 8) if k * unit < rows), rows})
    size = chan // plan.count
    there = [
        pltpu.with_memory_space_constraint(value, pltpu.VMEM)
        for value in (mine, other, sums, adjacency, node_weight, wcat, rdp, g)
    ]
    return pl.pallas_call(
        functools.partial(feature_kernel, cuts, scale, plan),
        in_specs=[SMEM] + [VMEM] * len(there),
        out_specs=[HBM] + [VMEM] * 5,
        out_shape=[
            pltpu.HBM((rows, chan), BF16),
            jax.ShapeDtypeStruct((size, cr), F32),
            jax.ShapeDtypeStruct((size, nodes), F32),
            jax.ShapeDtypeStruct((size, cr), F32),
            jax.ShapeDtypeStruct((nodes, nodes), F32),
            jax.ShapeDtypeStruct((cr, cr), F32),
        ],
        scratch_shapes=[
            pltpu.VMEM((rows, chan), BF16),
            pltpu.VMEM((2 * cr, 2 * cr), BF16),
            pltpu.VMEM((2 * nodes, cr), BF16),
            pltpu.SemaphoreType.DMA((len(cuts) - 1,)),
        ],
        compiler_params=params(),
        cost_estimate=cost(2 * rows * 4 * 65536, rows * chan * 4 + rows * 768),
        name="feature_grads",
    )(where, *there)


def on_device(
    plan, features, cotangent, reduce_weight, project_weight, expand_weight, adjacency, node_weight
):
    size_x, size_y, size_z, chan = features.shape
    local = size_x * size_y * size_z
    scale = 1.0 / math.sqrt(local * plan.count)
    flat_x = features.transpose(0, 2, 1, 3).reshape(local, chan)
    flat_g = cotangent.transpose(0, 2, 1, 3).reshape(local, chan)
    me = lax.axis_index(AXES).astype(jnp.int32)
    where = me.reshape(1)

    rdp, wcat, kept, sent = gather(
        plan, where, flat_x, flat_g, reduce_weight, project_weight.T, expand_weight
    )
    head = adjacency.shape[0]
    terms = [kept, plan.swap(sent, plan.core)]
    ready = None
    for group in plan.groups:
        parts = step(head, len(group), terms, ready[:1] if ready else ())
        terms = [plan.swap(part, mask) if mask else part for part, mask in zip(parts, group)]
        ready = ready or fetch(parts[0], adjacency, node_weight, wcat, rdp, flat_g)
    mine, sums = step(head, 1, terms)
    other = plan.swap(mine, plan.core)

    flat_out, grad_reduce, grad_project, grad_expand, grad_adjacency, grad_node = feature_grads(
        plan, where, mine, other, sums, *ready, scale
    )
    grad_features = flat_out.reshape(size_x, size_z, size_y, chan).transpose(0, 2, 1, 3)
    return (grad_features, grad_reduce, grad_project, grad_expand, grad_adjacency, grad_node)


def solution(mesh):
    return jax.shard_map(
        functools.partial(on_device, Plan(mesh)),
        mesh=mesh,
        in_specs=(P("gx", "gy", "gz", None), P("gx", "gy", "gz", None), P(), P(), P(), P(), P()),
        out_specs=(
            P("gx", "gy", "gz", None),
            P(AXES, None),
            P(AXES, None),
            P(AXES, None),
            P(),
            P(),
        ),
        check_vma=False,
    )
```

```python
import functools
import math

import jax
import jax.numpy as jnp
from jax import lax
from jax.experimental import pallas as pl
from jax.experimental.pallas import tpu as pltpu
from jax.sharding import PartitionSpec as P

AXES = ("gx", "gy", "gz")
F32 = jnp.float32
BF16 = jnp.bfloat16
HBM = pl.BlockSpec(memory_space=pltpu.HBM)
VMEM = pl.BlockSpec(memory_space=pltpu.VMEM)
SMEM = pl.BlockSpec(memory_space=pltpu.SMEM)
VMEM_LIMIT = 24 * 1024 * 1024
SMALL_LIMIT = 4 * 1024 * 1024
LAPS = 2


def exact(a, b, dims=((1,), (0,))):
    return lax.dot_general(
        a, b, (dims, ((), ())), precision=lax.Precision.HIGHEST, preferred_element_type=F32
    )


def mxu(a, b, dims=((1,), (0,))):
    return lax.dot_general(a, b, (dims, ((), ())), preferred_element_type=F32)


def params(limit=VMEM_LIMIT):
    return pltpu.CompilerParams(vmem_limit_bytes=limit)


def cost(flops, nbytes):
    return pl.CostEstimate(flops=flops, bytes_accessed=nbytes, transcendentals=0)


def in_hbm(*values):
    return [pltpu.with_memory_space_constraint(value, pltpu.HBM) for value in values]


def row_block(total, largest):
    for size in (1536, 1024, 768, 512, 384, 256, 128, 64, 32, 16):
        if size <= largest and total % size == 0:
            return size
    return total


class Plan:
    def __init__(self, mesh):
        size = {axis: mesh.shape[axis] for axis in AXES}
        self.count = math.prod(size.values())
        stride = {"gx": size["gy"] * size["gz"], "gy": size["gz"], "gz": 1}
        self.core = stride["gy"]
        spans = (
            ([0, *sorted(range(1, size["gx"]), key=lambda k: -k.bit_count())], stride["gx"]),
            (range(size["gy"] // 2), 2 * stride["gy"]),
            ([0, *range(2, size["gz"]), 1], stride["gz"]),
        )
        self.groups = [[k * step for k in order] for order, step in spans if len(order) > 1]
        self.masks = [0]
        for group in self.groups:
            self.masks = [mask | bits for mask in self.masks for bits in group]

    def side(self, device):
        return lax.bitwise_and(lax.div(device, jnp.int32(self.core)), jnp.int32(1))

    def swap(self, value, mask):
        return lax.ppermute(value, AXES, [(d, d ^ mask) for d in range(self.count)])


def gather_kernel(
    plan, step, sorted_here, where_ref, x_hbm, g_hbm, wr_hbm, wpt_hbm, we_hbm, rdp_hbm, wcat_hbm, *rest
):
    if sorted_here:
        kept_ref, sent_ref, turned_ref, *rest = rest
    else:
        keep_ref, send_ref, turned_ref, *rest = rest
    x_ref, g_ref, rdp_ref, cat_ref, wpt_ref, we_ref, sums_ref, term_ref, small_sem, in_sem, out_sem = rest
    rows = x_ref.shape[0]
    cr = we_ref.shape[1]
    nodes = wpt_ref.shape[0]
    wide = 2 * cr
    count = rows // step
    move = pltpu.make_async_copy
    small = [
        move(wr_hbm, cat_ref.at[:, pl.ds(0, cr)], small_sem.at[0]),
        move(wpt_hbm, wpt_ref, small_sem.at[1]),
        move(we_hbm, we_ref, small_sem.at[2]),
    ]
    load_cuts = sorted({0, min(1, count), min(2, count), count})
    store_cuts = sorted({0, max(count - 2, 0), max(count - 1, 0), count})
    span = lambda cuts, i: pl.ds(cuts[i] * step, (cuts[i + 1] - cuts[i]) * step)
    loads = [
        (
            move(x_hbm.at[span(load_cuts, i)], x_ref.at[span(load_cuts, i)], in_sem.at[0, i]),
            move(g_hbm.at[span(load_cuts, i)], g_ref.at[span(load_cuts, i)], in_sem.at[1, i]),
        )
        for i in range(len(load_cuts) - 1)
    ]
    stores = [
        move(rdp_ref.at[span(store_cuts, i)], rdp_hbm.at[span(store_cuts, i)], out_sem.at[i])
        for i in range(len(store_cuts) - 1)
    ]
    for copy in (*small, *loads[0]):
        copy.start()
    sums_ref[...] = jnp.zeros_like(sums_ref)
    term_ref[...] = jnp.zeros_like(term_ref)
    small[0].wait()
    small[1].wait()
    padded = jnp.concatenate([wpt_ref[...], jnp.zeros_like(wpt_ref)], axis=0)
    cat_ref[:, cr:] = padded.T
    keep_weights = move(cat_ref, wcat_hbm, small_sem.at[3])
    keep_weights.start()
    small[2].wait()

    @pl.loop(0, count)
    def _(i):
        for k, pair in enumerate(loads):
            @pl.when(i == load_cuts[k])
            def _():
                for copy in pair:
                    copy.wait()
                if k + 1 < len(loads):
                    for copy in loads[k + 1]:
                        copy.start()

        c = pl.ds(pl.multiple_of(i * step, step), step)
        x, g = x_ref[c], g_ref[c]
        both = mxu(x, cat_ref[...]).astype(BF16)
        mapped = mxu(g, we_ref[...]).astype(BF16)
        rdp = jnp.concatenate([both[:, :cr], mapped, both[:, cr:]], axis=1)
        rdp_ref[c] = rdp
        turned = rdp.T
        proj = turned[wide : wide + nodes]
        sums_ref[: wide + nodes] += mxu(turned[: wide + nodes], x)
        sums_ref[wide + nodes :] += mxu(proj, g)
        term_ref[...] += mxu(proj, rdp[:, :wide])
        for k, copy in enumerate(stores):
            pl.when(i == store_cuts[k + 1] - 1)(copy.start)

    me = where_ref[0]
    side = plan.side(me)
    turned_ref[...] = sums_ref[...].T
    if not sorted_here:
        heads = (keep_ref, send_ref)
    else:
        heads = (kept_ref.at[:nodes], sent_ref.at[:nodes])
    left, right = term_ref[:, :cr], term_ref[:, cr:]
    heads[0][...] = jnp.where(side == 0, left, right)
    heads[1][...] = jnp.where(side == 0, right, left)
    if sorted_here:
        size = turned_ref.shape[0] // plan.count
        for base, out_ref in ((me, kept_ref), (me ^ plan.core, sent_ref)):
            to = nodes
            for mask in plan.masks:
                at = pl.multiple_of((base ^ mask) * size, size)
                block = turned_ref[pl.ds(at, size), :]
                for lane in range(0, block.shape[1], cr):
                    out_ref[to : to + size] = block[:, lane : lane + cr]
                    to += size
    for copy in (keep_weights, *stores):
        copy.wait()


def gather(plan, where, x, g, wr, wpt, we):
    rows, chan = x.shape
    cr, nodes = wr.shape[1], wpt.shape[0]
    step = row_block(rows, 1536)
    width = 2 * cr + 2 * nodes
    half = plan.count // 2
    size = chan // plan.count
    sorted_here = size % 8 == 0
    outs = [
        (HBM, pltpu.HBM((rows, width), BF16)),
        (HBM, pltpu.HBM((chan, cr + 2 * nodes), BF16)),
    ]
    scratch = []
    if sorted_here:
        outs += [(VMEM, pltpu.VMEM((nodes + half * size * width // cr, cr), F32))] * 2
        scratch += [pltpu.VMEM((chan, width), F32)]
    else:
        outs += [(VMEM, jax.ShapeDtypeStruct((nodes, cr), F32))] * 2
        outs += [(VMEM, jax.ShapeDtypeStruct((chan, width), F32))]
    scratch += [
        pltpu.VMEM((rows, chan), BF16),
        pltpu.VMEM((rows, chan), BF16),
        pltpu.VMEM((rows, width), BF16),
        pltpu.VMEM((chan, cr + 2 * nodes), BF16),
        pltpu.VMEM(wpt.shape, BF16),
        pltpu.VMEM(we.shape, BF16),
        pltpu.VMEM((width, chan), F32),
        pltpu.VMEM((nodes, 2 * cr), F32),
        pltpu.SemaphoreType.DMA((4,)),
        pltpu.SemaphoreType.DMA((2, 3)),
        pltpu.SemaphoreType.DMA((3,)),
    ]
    rdp, wcat, kept, sent, *sums = pl.pallas_call(
        functools.partial(gather_kernel, plan, step, sorted_here),
        in_specs=[SMEM] + [HBM] * 5,
        out_specs=[spec for spec, _ in outs],
        out_shape=[shape for _, shape in outs],
        scratch_shapes=scratch,
        compiler_params=params(),
        cost_estimate=cost(2 * rows * chan * 1024, rows * chan * 4 + rows * 768),
        name="gather",
    )(where, *in_hbm(x, g, wr, wpt, we))
    if not sorted_here:
        table = jnp.array(plan.masks, jnp.int32)
        cut = sums[0].reshape(plan.count, size, width // cr, cr).transpose(0, 2, 1, 3)
        lay = lambda head, index: jnp.concatenate([head, cut[index].reshape(-1, cr)])
        kept = lay(kept, where[0] ^ table)
        sent = lay(sent, where[0] ^ plan.core ^ table)
    return rdp, wcat, kept, sent


def step_kernel(head, ins, parts, after, *refs):
    terms, outs = refs[:ins], refs[ins + after :]

    def total(start, size):
        value = terms[0][start : start + size]
        for ref in terms[1:]:
            value = value + ref[start : start + size]
        return value

    nodes = total(0, head)
    rest = terms[0].shape[0] - head
    if parts == 1:
        outs[0][...] = nodes
        outs[1][...] = total(head, rest)
        return
    size = rest // parts
    for k, ref in enumerate(outs):
        ref[:head] = nodes
        ref[head:] = total(head + k * size, size)


def step(head, parts, terms, after=()):
    rest, lanes = terms[0].shape[0] - head, terms[0].shape[1]
    shapes = (head, rest) if parts == 1 else (head + rest // parts,) * parts
    return pl.pallas_call(
        functools.partial(step_kernel, head, len(terms), parts, len(after)),
        in_specs=[VMEM] * len(terms) + [pl.BlockSpec(memory_space=pl.ANY)] * len(after),
        out_specs=[VMEM] * len(shapes),
        out_shape=[pltpu.VMEM((size, lanes), F32) for size in shapes],
        compiler_params=params(SMALL_LIMIT),
        cost_estimate=cost(terms[0].size, 12 * terms[0].size),
        name="step",
    )(*terms, *after)


def fetch_kernel(_, *refs):
    sems = refs[-1]
    count = len(refs) // 2
    copies = [
        pltpu.make_async_copy(src, dst, sems.at[k])
        for k, (src, dst) in enumerate(zip(refs[:count], refs[count:-1]))
    ]
    for copy in copies:
        copy.start()
    for copy in copies:
        copy.wait()


def fetch(after, *values):
    return pl.pallas_call(
        fetch_kernel,
        in_specs=[pl.BlockSpec(memory_space=pl.ANY)] + [HBM] * len(values),
        out_specs=[VMEM] * len(values),
        out_shape=[pltpu.VMEM(value.shape, value.dtype) for value in values],
        scratch_shapes=[pltpu.SemaphoreType.DMA((len(values),))],
        compiler_params=params(SMALL_LIMIT),
        cost_estimate=cost(0, sum(value.size * value.dtype.itemsize for value in values)),
        name="fetch",
    )(after, *in_hbm(*values))


def feature_kernel(
    cuts, scale, plan, where_ref, mine_ref, other_ref, sums_ref, adj_ref, nw_ref, wcat_ref, rdp_ref, g_ref,
    out_hbm, gr_ref, gp_ref, ge_ref, ga_ref, gn_ref, out_ref, mix_ref, dnb_ref, out_sem,
):
    nodes_n, cr = mine_ref.shape
    wide = 2 * cr
    first = plan.side(where_ref[0]) == 0
    mine, other = mine_ref[...], other_ref[...]
    nodes = scale * jnp.where(first, mine, other)
    d_node_out = jnp.where(first, other, mine)
    adj, nw = adj_ref[...], nw_ref[...]
    hidden = nodes - exact(adj, nodes)
    pre = exact(hidden, nw)
    node_out = jnp.maximum(pre, 0.0).astype(BF16)
    d_pre = jnp.where(pre > 0.0, d_node_out, 0.0)
    d_hidden = exact(d_pre, nw, ((1,), (1,)))
    d_nodes = d_hidden - exact(adj, d_hidden, ((0,), (0,)))
    dn = d_nodes.astype(BF16)
    no_f, dn_f = node_out.astype(F32), dn.astype(F32)
    dnb_ref[:nodes_n] = dn
    dnb_ref[nodes_n:] = jnp.zeros((nodes_n, cr), BF16)
    mix_ref[...] = jnp.zeros_like(mix_ref)
    mix_ref[:nodes_n, :cr] = dn
    mix_ref[cr : cr + nodes_n, cr:] = node_out
    rows = g_ref.shape[0] // LAPS

    def store(lap, part):
        start, stop = cuts[part : part + 2]
        c = pl.ds(pl.multiple_of(lap * rows + start, 16), stop - start)
        return c, pltpu.make_async_copy(out_ref.at[c], out_hbm.at[c], out_sem.at[lap, part])

    @pl.loop(0, LAPS)
    def _(lap):
        for part in range(len(cuts) - 1):
            c, copy = store(lap, part)
            rdp = rdp_ref[c]
            mixed = mxu(rdp[:, :wide], mix_ref[...], ((1,), (1,)))
            d_proj = (mixed[:, cr:] + scale * mixed[:, :cr]).astype(BF16)
            d_red = (scale * mxu(rdp[:, wide:], dnb_ref[...])).astype(BF16)
            both = jnp.concatenate([d_red, d_proj], axis=1)
            out = g_ref[c].astype(F32) + mxu(both, wcat_ref[...], ((1,), (1,)))
            out_ref[c] = out.astype(BF16)
            copy.start()

    gn_ref[...] = scale * exact(hidden, d_pre, ((0,), (0,)))
    ga_ref[...] = -scale * exact(d_hidden, nodes, ((1,), (1,)))
    size = gr_ref.shape[0]
    x_red, x_dm, with_proj = (sums_ref[k * size : (k + 1) * size] for k in range(3))
    gr_ref[...] = scale * scale * exact(with_proj[:, :nodes_n], dn_f)
    gp_ref[...] = scale * exact(x_dm, no_f, ((1,), (1,))) + scale * scale * exact(
        x_red, dn_f, ((1,), (1,))
    )
    ge_ref[...] = scale * exact(with_proj[:, nodes_n:], no_f)
    for lap in range(LAPS):
        for part in range(len(cuts) - 1):
            store(lap, part)[1].wait()


def feature_grads(plan, where, mine, other, sums, adjacency, node_weight, wcat, rdp, g, scale):
    rows, chan = g.shape
    nodes, cr = adjacency.shape[0], node_weight.shape[0]
    lap = rows // LAPS
    cuts = sorted({0, lap - row_block(lap // 6, 256), lap})
    size = chan // plan.count
    there = [
        pltpu.with_memory_space_constraint(value, pltpu.VMEM)
        for value in (mine, other, sums, adjacency, node_weight, wcat, rdp, g)
    ]
    return pl.pallas_call(
        functools.partial(feature_kernel, cuts, scale, plan),
        in_specs=[SMEM] + [VMEM] * len(there),
        out_specs=[HBM] + [VMEM] * 5,
        out_shape=[
            pltpu.HBM((rows, chan), BF16),
            jax.ShapeDtypeStruct((size, cr), F32),
            jax.ShapeDtypeStruct((size, nodes), F32),
            jax.ShapeDtypeStruct((size, cr), F32),
            jax.ShapeDtypeStruct((nodes, nodes), F32),
            jax.ShapeDtypeStruct((cr, cr), F32),
        ],
        scratch_shapes=[
            pltpu.VMEM((rows, chan), BF16),
            pltpu.VMEM((2 * cr, 2 * cr), BF16),
            pltpu.VMEM((2 * nodes, cr), BF16),
            pltpu.SemaphoreType.DMA((LAPS, len(cuts) - 1)),
        ],
        compiler_params=params(),
        cost_estimate=cost(2 * rows * 4 * 65536, rows * chan * 4 + rows * 768),
        name="feature_grads",
    )(where, *there)


def on_device(
    plan, features, cotangent, reduce_weight, project_weight, expand_weight, adjacency, node_weight
):
    size_x, size_y, size_z, chan = features.shape
    local = size_x * size_y * size_z
    scale = 1.0 / math.sqrt(local * plan.count)
    flat_x = features.transpose(0, 2, 1, 3).reshape(local, chan)
    flat_g = cotangent.transpose(0, 2, 1, 3).reshape(local, chan)
    me = lax.axis_index(AXES).astype(jnp.int32)
    where = me.reshape(1)

    rdp, wcat, kept, sent = gather(
        plan, where, flat_x, flat_g, reduce_weight, project_weight.T, expand_weight
    )
    head = adjacency.shape[0]
    terms = [kept, plan.swap(sent, plan.core)]
    ready = None
    for group in plan.groups:
        parts = step(head, len(group), terms, ready[:1] if ready else ())
        terms = [plan.swap(part, mask) if mask else part for part, mask in zip(parts, group)]
        ready = ready or fetch(parts[0], adjacency, node_weight, wcat, rdp, flat_g)
    mine, sums = step(head, 1, terms)
    other = plan.swap(mine, plan.core)

    flat_out, grad_reduce, grad_project, grad_expand, grad_adjacency, grad_node = feature_grads(
        plan, where, mine, other, sums, *ready, scale
    )
    grad_features = flat_out.reshape(size_x, size_z, size_y, chan).transpose(0, 2, 1, 3)
    return (grad_features, grad_reduce, grad_project, grad_expand, grad_adjacency, grad_node)


def solution(mesh):
    return jax.shard_map(
        functools.partial(on_device, Plan(mesh)),
        mesh=mesh,
        in_specs=(P("gx", "gy", "gz", None), P("gx", "gy", "gz", None), P(), P(), P(), P(), P()),
        out_specs=(
            P("gx", "gy", "gz", None),
            P(AXES, None),
            P(AXES, None),
            P(AXES, None),
            P(),
            P(),
        ),
        check_vma=False,
    )
```

```python
import functools
import math

import jax
import jax.numpy as jnp
from jax import lax
from jax.experimental import pallas as pl
from jax.experimental.pallas import tpu as pltpu
from jax.sharding import PartitionSpec as P

AXES = ("gx", "gy", "gz")
F32 = jnp.float32
BF16 = jnp.bfloat16
HBM = pl.BlockSpec(memory_space=pltpu.HBM)
VMEM = pl.BlockSpec(memory_space=pltpu.VMEM)
SMEM = pl.BlockSpec(memory_space=pltpu.SMEM)
VMEM_LIMIT = 24 * 1024 * 1024
SMALL_LIMIT = 4 * 1024 * 1024


def exact(a, b, dims=((1,), (0,))):
    return lax.dot_general(
        a, b, (dims, ((), ())), precision=lax.Precision.HIGHEST, preferred_element_type=F32
    )


def mxu(a, b, dims=((1,), (0,))):
    return lax.dot_general(a, b, (dims, ((), ())), preferred_element_type=F32)


def params(limit=VMEM_LIMIT):
    return pltpu.CompilerParams(vmem_limit_bytes=limit)


def cost(flops, nbytes):
    return pl.CostEstimate(flops=flops, bytes_accessed=nbytes, transcendentals=0)


def in_hbm(*values):
    return [pltpu.with_memory_space_constraint(value, pltpu.HBM) for value in values]


def row_block(total, largest):
    for size in (1536, 1024, 768, 512, 384, 256, 128, 64, 32, 16):
        if size <= largest and total % size == 0:
            return size
    return total


class Plan:
    def __init__(self, mesh):
        size = {axis: mesh.shape[axis] for axis in AXES}
        self.count = math.prod(size.values())
        stride = {"gx": size["gy"] * size["gz"], "gy": size["gz"], "gz": 1}
        self.core = stride["gy"]
        spans = (
            ([0, *sorted(range(1, size["gx"]), key=lambda k: -k.bit_count())], stride["gx"]),
            (range(size["gy"] // 2), 2 * stride["gy"]),
            ([0, *range(2, size["gz"]), 1], stride["gz"]),
        )
        self.groups = [[k * step for k in order] for order, step in spans if len(order) > 1]
        self.masks = [0]
        for group in self.groups:
            self.masks = [mask | bits for mask in self.masks for bits in group]

    def side(self, device):
        return lax.bitwise_and(lax.div(device, jnp.int32(self.core)), jnp.int32(1))

    def swap(self, value, mask):
        return lax.ppermute(value, AXES, [(d, d ^ mask) for d in range(self.count)])


def gather_kernel(
    plan, step, sorted_here, where_ref, x_hbm, g_hbm, wr_hbm, wpt_hbm, we_hbm, rdp_hbm, wcat_hbm, *rest
):
    if sorted_here:
        kept_ref, sent_ref, turned_ref, *rest = rest
    else:
        keep_ref, send_ref, turned_ref, *rest = rest
    x_ref, g_ref, rdp_ref, cat_ref, wpt_ref, we_ref, sums_ref, term_ref, small_sem, in_sem, out_sem = rest
    rows = x_ref.shape[0]
    cr = we_ref.shape[1]
    nodes = wpt_ref.shape[0]
    wide = 2 * cr
    count = rows // step
    move = pltpu.make_async_copy
    small = [
        move(wr_hbm, cat_ref.at[:, pl.ds(0, cr)], small_sem.at[0]),
        move(wpt_hbm, wpt_ref, small_sem.at[1]),
        move(we_hbm, we_ref, small_sem.at[2]),
    ]
    load_cuts = sorted({0, min(1, count), min(2, count), count})
    store_cuts = sorted({0, max(count - 2, 0), max(count - 1, 0), count})
    span = lambda cuts, i: pl.ds(cuts[i] * step, (cuts[i + 1] - cuts[i]) * step)
    loads = [
        (
            move(x_hbm.at[span(load_cuts, i)], x_ref.at[span(load_cuts, i)], in_sem.at[0, i]),
            move(g_hbm.at[span(load_cuts, i)], g_ref.at[span(load_cuts, i)], in_sem.at[1, i]),
        )
        for i in range(len(load_cuts) - 1)
    ]
    stores = [
        move(rdp_ref.at[span(store_cuts, i)], rdp_hbm.at[span(store_cuts, i)], out_sem.at[i])
        for i in range(len(store_cuts) - 1)
    ]
    for copy in (*small, *loads[0]):
        copy.start()
    sums_ref[...] = jnp.zeros_like(sums_ref)
    term_ref[...] = jnp.zeros_like(term_ref)
    small[0].wait()
    small[1].wait()
    padded = jnp.concatenate([wpt_ref[...], jnp.zeros_like(wpt_ref)], axis=0)
    cat_ref[:, cr:] = padded.T
    keep_weights = move(cat_ref, wcat_hbm, small_sem.at[3])
    keep_weights.start()
    small[2].wait()

    @pl.loop(0, count)
    def _(i):
        for k, pair in enumerate(loads):
            @pl.when(i == load_cuts[k])
            def _():
                for copy in pair:
                    copy.wait()
                if k + 1 < len(loads):
                    for copy in loads[k + 1]:
                        copy.start()

        c = pl.ds(pl.multiple_of(i * step, step), step)
        x, g = x_ref[c], g_ref[c]
        both = mxu(x, cat_ref[...]).astype(BF16)
        mapped = mxu(g, we_ref[...]).astype(BF16)
        rdp = jnp.concatenate([both[:, :cr], mapped, both[:, cr:]], axis=1)
        rdp_ref[c] = rdp
        turned = rdp.T
        proj = turned[wide : wide + nodes]
        sums_ref[: wide + nodes] += mxu(turned[: wide + nodes], x)
        sums_ref[wide + nodes :] += mxu(proj, g)
        term_ref[...] += mxu(proj, rdp[:, :wide])
        for k, copy in enumerate(stores):
            pl.when(i == store_cuts[k + 1] - 1)(copy.start)

    me = where_ref[0]
    side = plan.side(me)
    turned_ref[...] = sums_ref[...].T
    if not sorted_here:
        heads = (keep_ref, send_ref)
    else:
        heads = (kept_ref.at[:nodes], sent_ref.at[:nodes])
    left, right = term_ref[:, :cr], term_ref[:, cr:]
    heads[0][...] = jnp.where(side == 0, left, right)
    heads[1][...] = jnp.where(side == 0, right, left)
    if sorted_here:
        size = turned_ref.shape[0] // plan.count
        for base, out_ref in ((me, kept_ref), (me ^ plan.core, sent_ref)):
            to = nodes
            for mask in plan.masks:
                at = pl.multiple_of((base ^ mask) * size, size)
                block = turned_ref[pl.ds(at, size), :]
                for lane in range(0, block.shape[1], cr):
                    out_ref[to : to + size] = block[:, lane : lane + cr]
                    to += size
    for copy in (keep_weights, *stores):
        copy.wait()


def gather(plan, where, x, g, wr, wpt, we):
    rows, chan = x.shape
    cr, nodes = wr.shape[1], wpt.shape[0]
    step = row_block(rows, 1536)
    width = 2 * cr + 2 * nodes
    half = plan.count // 2
    size = chan // plan.count
    sorted_here = size % 8 == 0
    outs = [
        (HBM, pltpu.HBM((rows, width), BF16)),
        (HBM, pltpu.HBM((chan, cr + 2 * nodes), BF16)),
    ]
    scratch = []
    if sorted_here:
        outs += [(VMEM, pltpu.VMEM((nodes + half * size * width // cr, cr), F32))] * 2
        scratch += [pltpu.VMEM((chan, width), F32)]
    else:
        outs += [(VMEM, jax.ShapeDtypeStruct((nodes, cr), F32))] * 2
        outs += [(VMEM, jax.ShapeDtypeStruct((chan, width), F32))]
    scratch += [
        pltpu.VMEM((rows, chan), BF16),
        pltpu.VMEM((rows, chan), BF16),
        pltpu.VMEM((rows, width), BF16),
        pltpu.VMEM((chan, cr + 2 * nodes), BF16),
        pltpu.VMEM(wpt.shape, BF16),
        pltpu.VMEM(we.shape, BF16),
        pltpu.VMEM((width, chan), F32),
        pltpu.VMEM((nodes, 2 * cr), F32),
        pltpu.SemaphoreType.DMA((4,)),
        pltpu.SemaphoreType.DMA((2, 3)),
        pltpu.SemaphoreType.DMA((3,)),
    ]
    rdp, wcat, kept, sent, *sums = pl.pallas_call(
        functools.partial(gather_kernel, plan, step, sorted_here),
        in_specs=[SMEM] + [HBM] * 5,
        out_specs=[spec for spec, _ in outs],
        out_shape=[shape for _, shape in outs],
        scratch_shapes=scratch,
        compiler_params=params(),
        cost_estimate=cost(2 * rows * chan * 1024, rows * chan * 4 + rows * 768),
        name="gather",
    )(where, *in_hbm(x, g, wr, wpt, we))
    if not sorted_here:
        table = jnp.array(plan.masks, jnp.int32)
        cut = sums[0].reshape(plan.count, size, width // cr, cr).transpose(0, 2, 1, 3)
        lay = lambda head, index: jnp.concatenate([head, cut[index].reshape(-1, cr)])
        kept = lay(kept, where[0] ^ table)
        sent = lay(sent, where[0] ^ plan.core ^ table)
    return rdp, wcat, kept, sent


def step_kernel(head, ins, parts, after, *refs):
    terms, outs = refs[:ins], refs[ins + after :]

    def total(start, size):
        value = terms[0][start : start + size]
        for ref in terms[1:]:
            value = value + ref[start : start + size]
        return value

    nodes = total(0, head)
    rest = terms[0].shape[0] - head
    if parts == 1:
        outs[0][...] = nodes
        outs[1][...] = total(head, rest)
        return
    size = rest // parts
    for k, ref in enumerate(outs):
        ref[:head] = nodes
        ref[head:] = total(head + k * size, size)


def step(head, parts, terms, after=()):
    rest, lanes = terms[0].shape[0] - head, terms[0].shape[1]
    shapes = (head, rest) if parts == 1 else (head + rest // parts,) * parts
    return pl.pallas_call(
        functools.partial(step_kernel, head, len(terms), parts, len(after)),
        in_specs=[VMEM] * len(terms) + [pl.BlockSpec(memory_space=pl.ANY)] * len(after),
        out_specs=[VMEM] * len(shapes),
        out_shape=[pltpu.VMEM((size, lanes), F32) for size in shapes],
        compiler_params=params(SMALL_LIMIT),
        cost_estimate=cost(terms[0].size, 12 * terms[0].size),
        name="step",
    )(*terms, *after)


def fetch_kernel(_, *refs):
    sems = refs[-1]
    count = len(refs) // 2
    copies = [
        pltpu.make_async_copy(src, dst, sems.at[k])
        for k, (src, dst) in enumerate(zip(refs[:count], refs[count:-1]))
    ]
    for copy in copies:
        copy.start()
    for copy in copies:
        copy.wait()


def fetch(after, *values):
    return pl.pallas_call(
        fetch_kernel,
        in_specs=[pl.BlockSpec(memory_space=pl.ANY)] + [HBM] * len(values),
        out_specs=[VMEM] * len(values),
        out_shape=[pltpu.VMEM(value.shape, value.dtype) for value in values],
        scratch_shapes=[pltpu.SemaphoreType.DMA((len(values),))],
        compiler_params=params(SMALL_LIMIT),
        cost_estimate=cost(0, sum(value.size * value.dtype.itemsize for value in values)),
        name="fetch",
    )(after, *in_hbm(*values))


def feature_kernel(
    cuts, scale, plan, where_ref, mine_ref, other_ref, sums_ref, adj_ref, nw_ref, wcat_ref, rdp_ref, g_ref,
    out_hbm, gr_ref, gp_ref, ge_ref, ga_ref, gn_ref, out_ref, mix_ref, dnb_ref, out_sem,
):
    nodes_n, cr = mine_ref.shape
    wide = 2 * cr
    first = plan.side(where_ref[0]) == 0
    mine, other = mine_ref[...], other_ref[...]
    nodes = scale * jnp.where(first, mine, other)
    d_node_out = jnp.where(first, other, mine)
    adj, nw = adj_ref[...], nw_ref[...]
    hidden = nodes - exact(adj, nodes)
    pre = exact(hidden, nw)
    node_out = jnp.maximum(pre, 0.0).astype(BF16)
    d_pre = jnp.where(pre > 0.0, d_node_out, 0.0)
    d_hidden = exact(d_pre, nw, ((1,), (1,)))
    d_nodes = d_hidden - exact(adj, d_hidden, ((0,), (0,)))
    dn = d_nodes.astype(BF16)
    no_f, dn_f = node_out.astype(F32), dn.astype(F32)
    dnb_ref[:nodes_n] = dn
    dnb_ref[nodes_n:] = jnp.zeros((nodes_n, cr), BF16)
    mix_ref[...] = jnp.zeros_like(mix_ref)
    mix_ref[:nodes_n, :cr] = dn
    mix_ref[cr : cr + nodes_n, cr:] = node_out
    copies = []
    for i, (start, stop) in enumerate(zip(cuts, cuts[1:])):
        c = pl.ds(start, stop - start)
        rdp = rdp_ref[c]
        mixed = mxu(rdp[:, :wide], mix_ref[...], ((1,), (1,)))
        d_proj = (mixed[:, cr:] + scale * mixed[:, :cr]).astype(BF16)
        d_red = (scale * mxu(rdp[:, wide:], dnb_ref[...])).astype(BF16)
        both = jnp.concatenate([d_red, d_proj], axis=1)
        out = g_ref[c].astype(F32) + mxu(both, wcat_ref[...], ((1,), (1,)))
        out_ref[c] = out.astype(BF16)
        copies.append(pltpu.make_async_copy(out_ref.at[c], out_hbm.at[c], out_sem.at[i]))
        copies[-1].start()
    gn_ref[...] = scale * exact(hidden, d_pre, ((0,), (0,)))
    ga_ref[...] = -scale * exact(d_hidden, nodes, ((1,), (1,)))
    size = gr_ref.shape[0]
    x_red, x_dm, with_proj = (sums_ref[k * size : (k + 1) * size] for k in range(3))
    gr_ref[...] = scale * scale * exact(with_proj[:, :nodes_n], dn_f)
    gp_ref[...] = scale * exact(x_dm, no_f, ((1,), (1,))) + scale * scale * exact(
        x_red, dn_f, ((1,), (1,))
    )
    ge_ref[...] = scale * exact(with_proj[:, nodes_n:], no_f)
    for copy in copies:
        copy.wait()


def feature_grads(plan, where, mine, other, sums, adjacency, node_weight, wcat, rdp, g, scale):
    rows, chan = g.shape
    nodes, cr = adjacency.shape[0], node_weight.shape[0]
    unit = row_block(rows // 12, 256)
    cuts = sorted({0, *(rows - k * unit for k in (1, 4, 8) if k * unit < rows), rows})
    size = chan // plan.count
    there = [
        pltpu.with_memory_space_constraint(value, pltpu.VMEM)
        for value in (mine, other, sums, adjacency, node_weight, wcat, rdp, g)
    ]
    return pl.pallas_call(
        functools.partial(feature_kernel, cuts, scale, plan),
        in_specs=[SMEM] + [VMEM] * len(there),
        out_specs=[HBM] + [VMEM] * 5,
        out_shape=[
            pltpu.HBM((rows, chan), BF16),
            jax.ShapeDtypeStruct((size, cr), F32),
            jax.ShapeDtypeStruct((size, nodes), F32),
            jax.ShapeDtypeStruct((size, cr), F32),
            jax.ShapeDtypeStruct((nodes, nodes), F32),
            jax.ShapeDtypeStruct((cr, cr), F32),
        ],
        scratch_shapes=[
            pltpu.VMEM((rows, chan), BF16),
            pltpu.VMEM((2 * cr, 2 * cr), BF16),
            pltpu.VMEM((2 * nodes, cr), BF16),
            pltpu.SemaphoreType.DMA((len(cuts) - 1,)),
        ],
        compiler_params=params(),
        cost_estimate=cost(2 * rows * 4 * 65536, rows * chan * 4 + rows * 768),
        name="feature_grads",
    )(where, *there)


def on_device(
    plan, features, cotangent, reduce_weight, project_weight, expand_weight, adjacency, node_weight
):
    size_x, size_y, size_z, chan = features.shape
    local = size_x * size_y * size_z
    scale = 1.0 / math.sqrt(local * plan.count)
    flat_x = features.transpose(0, 2, 1, 3).reshape(local, chan)
    flat_g = cotangent.transpose(0, 2, 1, 3).reshape(local, chan)
    me = lax.axis_index(AXES).astype(jnp.int32)
    where = me.reshape(1)

    rdp, wcat, kept, sent = gather(
        plan, where, flat_x, flat_g, reduce_weight, project_weight.T, expand_weight
    )
    head = adjacency.shape[0]
    terms = [kept, plan.swap(sent, plan.core)]
    ready = None
    for group in plan.groups:
        parts = step(head, len(group), terms, ready[:1] if ready else ())
        terms = [plan.swap(part, mask) if mask else part for part, mask in zip(parts, group)]
        ready = ready or fetch(parts[0], adjacency, node_weight, wcat, rdp, flat_g)
    mine, sums = step(head, 1, terms)
    other = plan.swap(mine, plan.core)

    flat_out, grad_reduce, grad_project, grad_expand, grad_adjacency, grad_node = feature_grads(
        plan, where, mine, other, sums, *ready, scale
    )
    grad_features = flat_out.reshape(size_x, size_z, size_y, chan).transpose(0, 2, 1, 3)
    return (grad_features, grad_reduce, grad_project, grad_expand, grad_adjacency, grad_node)


def solution(mesh):
    return jax.shard_map(
        functools.partial(on_device, Plan(mesh)),
        mesh=mesh,
        in_specs=(P("gx", "gy", "gz", None), P("gx", "gy", "gz", None), P(), P(), P(), P(), P()),
        out_specs=(
            P("gx", "gy", "gz", None),
            P(AXES, None),
            P(AXES, None),
            P(AXES, None),
            P(),
            P(),
        ),
        check_vma=False,
    )
```

```python
import functools
import math

import jax
import jax.numpy as jnp
from jax import lax
from jax.experimental import pallas as pl
from jax.experimental.pallas import tpu as pltpu
from jax.sharding import PartitionSpec as P

AXES = ("gx", "gy", "gz")
F32 = jnp.float32
BF16 = jnp.bfloat16
HBM = pl.BlockSpec(memory_space=pltpu.HBM)
VMEM = pl.BlockSpec(memory_space=pltpu.VMEM)
SMEM = pl.BlockSpec(memory_space=pltpu.SMEM)
VMEM_LIMIT = 24 * 1024 * 1024
SMALL_LIMIT = 4 * 1024 * 1024


def exact(a, b, dims=((1,), (0,))):
    return lax.dot_general(
        a, b, (dims, ((), ())), precision=lax.Precision.HIGHEST, preferred_element_type=F32
    )


def mxu(a, b, dims=((1,), (0,))):
    return lax.dot_general(a, b, (dims, ((), ())), preferred_element_type=F32)


def params(limit=VMEM_LIMIT):
    return pltpu.CompilerParams(vmem_limit_bytes=limit)


def cost(flops, nbytes):
    return pl.CostEstimate(flops=flops, bytes_accessed=nbytes, transcendentals=0)


def in_hbm(*values):
    return [pltpu.with_memory_space_constraint(value, pltpu.HBM) for value in values]


def row_block(total, largest):
    for size in (1536, 1024, 768, 512, 384, 256, 128, 64, 32, 16):
        if size <= largest and total % size == 0:
            return size
    return total


class Plan:
    def __init__(self, mesh):
        size = {axis: mesh.shape[axis] for axis in AXES}
        self.count = math.prod(size.values())
        stride = {"gx": size["gy"] * size["gz"], "gy": size["gz"], "gz": 1}
        self.core = stride["gy"]
        spans = (
            ([0, *sorted(range(1, size["gx"]), key=lambda k: -k.bit_count())], stride["gx"]),
            (range(size["gy"] // 2), 2 * stride["gy"]),
            ([0, *range(2, size["gz"]), 1], stride["gz"]),
        )
        self.groups = [[k * step for k in order] for order, step in spans if len(order) > 1]
        self.masks = [0]
        for group in self.groups:
            self.masks = [mask | bits for mask in self.masks for bits in group]

    def side(self, device):
        return lax.bitwise_and(lax.div(device, jnp.int32(self.core)), jnp.int32(1))

    def swap(self, value, mask):
        return lax.ppermute(value, AXES, [(d, d ^ mask) for d in range(self.count)])


def gather_kernel(
    plan, step, sorted_here, where_ref, x_hbm, g_hbm, wr_hbm, wpt_hbm, we_hbm, rdp_ref, cat_ref, *rest
):
    if sorted_here:
        kept_ref, sent_ref, turned_ref, *rest = rest
    else:
        keep_ref, send_ref, turned_ref, *rest = rest
    x_ref, g_ref, wpt_ref, we_ref, sums_ref, term_ref, small_sem, in_sem = rest
    rows = x_ref.shape[0]
    cr = we_ref.shape[1]
    nodes = wpt_ref.shape[0]
    wide = 2 * cr
    count = rows // step
    move = pltpu.make_async_copy
    small = [
        move(wr_hbm, cat_ref.at[:, pl.ds(0, cr)], small_sem.at[0]),
        move(wpt_hbm, wpt_ref, small_sem.at[1]),
        move(we_hbm, we_ref, small_sem.at[2]),
    ]
    load_cuts = sorted({0, min(1, count), min(2, count), count})
    span = lambda cuts, i: pl.ds(cuts[i] * step, (cuts[i + 1] - cuts[i]) * step)
    loads = [
        (
            move(x_hbm.at[span(load_cuts, i)], x_ref.at[span(load_cuts, i)], in_sem.at[0, i]),
            move(g_hbm.at[span(load_cuts, i)], g_ref.at[span(load_cuts, i)], in_sem.at[1, i]),
        )
        for i in range(len(load_cuts) - 1)
    ]
    for copy in (*small, *loads[0]):
        copy.start()
    sums_ref[...] = jnp.zeros_like(sums_ref)
    term_ref[...] = jnp.zeros_like(term_ref)
    small[0].wait()
    small[1].wait()
    padded = jnp.concatenate([wpt_ref[...], jnp.zeros_like(wpt_ref)], axis=0)
    cat_ref[:, cr:] = padded.T
    small[2].wait()

    @pl.loop(0, count)
    def _(i):
        for k, pair in enumerate(loads):
            @pl.when(i == load_cuts[k])
            def _():
                for copy in pair:
                    copy.wait()
                if k + 1 < len(loads):
                    for copy in loads[k + 1]:
                        copy.start()

        c = pl.ds(pl.multiple_of(i * step, step), step)
        x, g = x_ref[c], g_ref[c]
        both = mxu(x, cat_ref[...]).astype(BF16)
        mapped = mxu(g, we_ref[...]).astype(BF16)
        rdp = jnp.concatenate([both[:, :cr], mapped, both[:, cr:]], axis=1)
        rdp_ref[c] = rdp
        turned = rdp.T
        proj = turned[wide : wide + nodes]
        sums_ref[: wide + nodes] += mxu(turned[: wide + nodes], x)
        sums_ref[wide + nodes :] += mxu(proj, g)
        term_ref[...] += mxu(proj, rdp[:, :wide])

    me = where_ref[0]
    side = plan.side(me)
    turned_ref[...] = sums_ref[...].T
    if not sorted_here:
        heads = (keep_ref, send_ref)
    else:
        heads = (kept_ref.at[:nodes], sent_ref.at[:nodes])
    left, right = term_ref[:, :cr], term_ref[:, cr:]
    heads[0][...] = jnp.where(side == 0, left, right)
    heads[1][...] = jnp.where(side == 0, right, left)
    if sorted_here:
        size = turned_ref.shape[0] // plan.count
        for base, out_ref in ((me, kept_ref), (me ^ plan.core, sent_ref)):
            to = nodes
            for mask in plan.masks:
                at = pl.multiple_of((base ^ mask) * size, size)
                block = turned_ref[pl.ds(at, size), :]
                for lane in range(0, block.shape[1], cr):
                    out_ref[to : to + size] = block[:, lane : lane + cr]
                    to += size


def gather(plan, where, x, g, wr, wpt, we):
    rows, chan = x.shape
    cr, nodes = wr.shape[1], wpt.shape[0]
    step = row_block(rows, 1536)
    width = 2 * cr + 2 * nodes
    half = plan.count // 2
    size = chan // plan.count
    sorted_here = size % 8 == 0
    outs = [
        (VMEM, pltpu.VMEM((rows, width), BF16)),
        (VMEM, pltpu.VMEM((chan, cr + 2 * nodes), BF16)),
    ]
    scratch = []
    if sorted_here:
        outs += [(VMEM, pltpu.VMEM((nodes + half * size * width // cr, cr), F32))] * 2
        scratch += [pltpu.VMEM((chan, width), F32)]
    else:
        outs += [(VMEM, jax.ShapeDtypeStruct((nodes, cr), F32))] * 2
        outs += [(VMEM, jax.ShapeDtypeStruct((chan, width), F32))]
    scratch += [
        pltpu.VMEM((rows, chan), BF16),
        pltpu.VMEM((rows, chan), BF16),
        pltpu.VMEM(wpt.shape, BF16),
        pltpu.VMEM(we.shape, BF16),
        pltpu.VMEM((width, chan), F32),
        pltpu.VMEM((nodes, 2 * cr), F32),
        pltpu.SemaphoreType.DMA((3,)),
        pltpu.SemaphoreType.DMA((2, 3)),
    ]
    rdp, wcat, kept, sent, *sums = pl.pallas_call(
        functools.partial(gather_kernel, plan, step, sorted_here),
        in_specs=[SMEM] + [HBM] * 5,
        out_specs=[spec for spec, _ in outs],
        out_shape=[shape for _, shape in outs],
        scratch_shapes=scratch,
        compiler_params=params(),
        cost_estimate=cost(2 * rows * chan * 1024, rows * chan * 4 + rows * 768),
        name="gather",
    )(where, *in_hbm(x, g, wr, wpt, we))
    if not sorted_here:
        table = jnp.array(plan.masks, jnp.int32)
        cut = sums[0].reshape(plan.count, size, width // cr, cr).transpose(0, 2, 1, 3)
        lay = lambda head, index: jnp.concatenate([head, cut[index].reshape(-1, cr)])
        kept = lay(kept, where[0] ^ table)
        sent = lay(sent, where[0] ^ plan.core ^ table)
    return rdp, wcat, kept, sent


def step_kernel(head, ins, parts, after, *refs):
    terms, outs = refs[:ins], refs[ins + after :]

    def total(start, size):
        value = terms[0][start : start + size]
        for ref in terms[1:]:
            value = value + ref[start : start + size]
        return value

    nodes = total(0, head)
    rest = terms[0].shape[0] - head
    if parts == 1:
        outs[0][...] = nodes
        outs[1][...] = total(head, rest)
        return
    size = rest // parts
    for k, ref in enumerate(outs):
        ref[:head] = nodes
        ref[head:] = total(head + k * size, size)


def step(head, parts, terms, after=()):
    rest, lanes = terms[0].shape[0] - head, terms[0].shape[1]
    shapes = (head, rest) if parts == 1 else (head + rest // parts,) * parts
    return pl.pallas_call(
        functools.partial(step_kernel, head, len(terms), parts, len(after)),
        in_specs=[VMEM] * len(terms) + [pl.BlockSpec(memory_space=pl.ANY)] * len(after),
        out_specs=[VMEM] * len(shapes),
        out_shape=[pltpu.VMEM((size, lanes), F32) for size in shapes],
        compiler_params=params(SMALL_LIMIT),
        cost_estimate=cost(terms[0].size, 12 * terms[0].size),
        name="step",
    )(*terms, *after)


def fetch_kernel(_, *refs):
    sems = refs[-1]
    count = len(refs) // 2
    copies = [
        pltpu.make_async_copy(src, dst, sems.at[k])
        for k, (src, dst) in enumerate(zip(refs[:count], refs[count:-1]))
    ]
    for copy in copies:
        copy.start()
    for copy in copies:
        copy.wait()


def fetch(after, *values):
    return pl.pallas_call(
        fetch_kernel,
        in_specs=[pl.BlockSpec(memory_space=pl.ANY)] + [HBM] * len(values),
        out_specs=[VMEM] * len(values),
        out_shape=[pltpu.VMEM(value.shape, value.dtype) for value in values],
        scratch_shapes=[pltpu.SemaphoreType.DMA((len(values),))],
        compiler_params=params(SMALL_LIMIT),
        cost_estimate=cost(0, sum(value.size * value.dtype.itemsize for value in values)),
        name="fetch",
    )(after, *in_hbm(*values))


def feature_kernel(
    cuts, scale, plan, where_ref, mine_ref, other_ref, sums_ref, adj_ref, nw_ref, wcat_ref, rdp_ref, g_ref,
    out_hbm, gr_ref, gp_ref, ge_ref, ga_ref, gn_ref, out_ref, mix_ref, dnb_ref, out_sem,
):
    nodes_n, cr = mine_ref.shape
    wide = 2 * cr
    first = plan.side(where_ref[0]) == 0
    mine, other = mine_ref[...], other_ref[...]
    nodes = scale * jnp.where(first, mine, other)
    d_node_out = jnp.where(first, other, mine)
    adj, nw = adj_ref[...], nw_ref[...]
    hidden = nodes - exact(adj, nodes)
    pre = exact(hidden, nw)
    node_out = jnp.maximum(pre, 0.0).astype(BF16)
    d_pre = jnp.where(pre > 0.0, d_node_out, 0.0)
    d_hidden = exact(d_pre, nw, ((1,), (1,)))
    d_nodes = d_hidden - exact(adj, d_hidden, ((0,), (0,)))
    dn = d_nodes.astype(BF16)
    no_f, dn_f = node_out.astype(F32), dn.astype(F32)
    dnb_ref[:nodes_n] = dn
    dnb_ref[nodes_n:] = jnp.zeros((nodes_n, cr), BF16)
    mix_ref[...] = jnp.zeros_like(mix_ref)
    mix_ref[:nodes_n, :cr] = dn
    mix_ref[cr : cr + nodes_n, cr:] = node_out
    copies = []
    for i, (start, stop) in enumerate(zip(cuts, cuts[1:])):
        c = pl.ds(start, stop - start)
        rdp = rdp_ref[c]
        mixed = mxu(rdp[:, :wide], mix_ref[...], ((1,), (1,)))
        d_proj = (mixed[:, cr:] + scale * mixed[:, :cr]).astype(BF16)
        d_red = (scale * mxu(rdp[:, wide:], dnb_ref[...])).astype(BF16)
        both = jnp.concatenate([d_red, d_proj], axis=1)
        out = g_ref[c].astype(F32) + mxu(both, wcat_ref[...], ((1,), (1,)))
        out_ref[c] = out.astype(BF16)
        copies.append(pltpu.make_async_copy(out_ref.at[c], out_hbm.at[c], out_sem.at[i]))
        copies[-1].start()
    gn_ref[...] = scale * exact(hidden, d_pre, ((0,), (0,)))
    ga_ref[...] = -scale * exact(d_hidden, nodes, ((1,), (1,)))
    size = gr_ref.shape[0]
    x_red, x_dm, with_proj = (sums_ref[k * size : (k + 1) * size] for k in range(3))
    gr_ref[...] = scale * scale * exact(with_proj[:, :nodes_n], dn_f)
    gp_ref[...] = scale * exact(x_dm, no_f, ((1,), (1,))) + scale * scale * exact(
        x_red, dn_f, ((1,), (1,))
    )
    ge_ref[...] = scale * exact(with_proj[:, nodes_n:], no_f)
    for copy in copies:
        copy.wait()


def feature_grads(plan, where, mine, other, sums, adjacency, node_weight, wcat, rdp, g, scale):
    rows, chan = g.shape
    nodes, cr = adjacency.shape[0], node_weight.shape[0]
    unit = row_block(rows // 12, 256)
    cuts = sorted({0, *(rows - k * unit for k in (1, 4, 8) if k * unit < rows), rows})
    size = chan // plan.count
    there = [
        pltpu.with_memory_space_constraint(value, pltpu.VMEM)
        for value in (mine, other, sums, adjacency, node_weight, wcat, rdp, g)
    ]
    return pl.pallas_call(
        functools.partial(feature_kernel, cuts, scale, plan),
        in_specs=[SMEM] + [VMEM] * len(there),
        out_specs=[HBM] + [VMEM] * 5,
        out_shape=[
            pltpu.HBM((rows, chan), BF16),
            jax.ShapeDtypeStruct((size, cr), F32),
            jax.ShapeDtypeStruct((size, nodes), F32),
            jax.ShapeDtypeStruct((size, cr), F32),
            jax.ShapeDtypeStruct((nodes, nodes), F32),
            jax.ShapeDtypeStruct((cr, cr), F32),
        ],
        scratch_shapes=[
            pltpu.VMEM((rows, chan), BF16),
            pltpu.VMEM((2 * cr, 2 * cr), BF16),
            pltpu.VMEM((2 * nodes, cr), BF16),
            pltpu.SemaphoreType.DMA((len(cuts) - 1,)),
        ],
        compiler_params=params(),
        cost_estimate=cost(2 * rows * 4 * 65536, rows * chan * 4 + rows * 768),
        name="feature_grads",
    )(where, *there)


def on_device(
    plan, features, cotangent, reduce_weight, project_weight, expand_weight, adjacency, node_weight
):
    size_x, size_y, size_z, chan = features.shape
    local = size_x * size_y * size_z
    scale = 1.0 / math.sqrt(local * plan.count)
    flat_x = features.transpose(0, 2, 1, 3).reshape(local, chan)
    flat_g = cotangent.transpose(0, 2, 1, 3).reshape(local, chan)
    me = lax.axis_index(AXES).astype(jnp.int32)
    where = me.reshape(1)

    rdp, wcat, kept, sent = gather(
        plan, where, flat_x, flat_g, reduce_weight, project_weight.T, expand_weight
    )
    head = adjacency.shape[0]
    terms = [kept, plan.swap(sent, plan.core)]
    ready = None
    for group in plan.groups:
        parts = step(head, len(group), terms, ready[:1] if ready else ())
        terms = [plan.swap(part, mask) if mask else part for part, mask in zip(parts, group)]
        ready = ready or fetch(parts[0], adjacency, node_weight, flat_g)
    mine, sums = step(head, 1, terms)
    other = plan.swap(mine, plan.core)

    flat_out, grad_reduce, grad_project, grad_expand, grad_adjacency, grad_node = feature_grads(
        plan, where, mine, other, sums, *ready[:2], wcat, rdp, ready[2], scale
    )
    grad_features = flat_out.reshape(size_x, size_z, size_y, chan).transpose(0, 2, 1, 3)
    return (grad_features, grad_reduce, grad_project, grad_expand, grad_adjacency, grad_node)


def solution(mesh):
    return jax.shard_map(
        functools.partial(on_device, Plan(mesh)),
        mesh=mesh,
        in_specs=(P("gx", "gy", "gz", None), P("gx", "gy", "gz", None), P(), P(), P(), P(), P()),
        out_specs=(
            P("gx", "gy", "gz", None),
            P(AXES, None),
            P(AXES, None),
            P(AXES, None),
            P(),
            P(),
        ),
        check_vma=False,
    )
```

```python
import functools
import math

import jax
import jax.numpy as jnp
from jax import lax
from jax.experimental import pallas as pl
from jax.experimental.pallas import tpu as pltpu
from jax.sharding import PartitionSpec as P

AXES = ("gx", "gy", "gz")
F32 = jnp.float32
BF16 = jnp.bfloat16
HBM = pl.BlockSpec(memory_space=pltpu.HBM)
VMEM = pl.BlockSpec(memory_space=pltpu.VMEM)
SMEM = pl.BlockSpec(memory_space=pltpu.SMEM)
VMEM_LIMIT = 24 * 1024 * 1024
SMALL_LIMIT = 4 * 1024 * 1024


def exact(a, b, dims=((1,), (0,))):
    return lax.dot_general(
        a, b, (dims, ((), ())), precision=lax.Precision.HIGHEST, preferred_element_type=F32
    )


def mxu(a, b, dims=((1,), (0,))):
    return lax.dot_general(a, b, (dims, ((), ())), preferred_element_type=F32)


def params(limit=VMEM_LIMIT):
    return pltpu.CompilerParams(vmem_limit_bytes=limit)


def cost(flops, nbytes):
    return pl.CostEstimate(flops=flops, bytes_accessed=nbytes, transcendentals=0)


def in_hbm(*values):
    return [pltpu.with_memory_space_constraint(value, pltpu.HBM) for value in values]


def row_block(total, largest):
    for size in (1536, 1024, 768, 512, 384, 256, 128, 64, 32, 16):
        if size <= largest and total % size == 0:
            return size
    return total


class Plan:
    def __init__(self, mesh):
        size = {axis: mesh.shape[axis] for axis in AXES}
        self.count = math.prod(size.values())
        stride = {"gx": size["gy"] * size["gz"], "gy": size["gz"], "gz": 1}
        self.core = stride["gy"]
        spans = (
            ([0, *sorted(range(1, size["gx"]), key=lambda k: -k.bit_count())], stride["gx"]),
            (range(size["gy"] // 2), 2 * stride["gy"]),
            ([0, *range(2, size["gz"]), 1], stride["gz"]),
        )
        self.groups = [[k * step for k in order] for order, step in spans if len(order) > 1]
        self.masks = [0]
        for group in self.groups:
            self.masks = [mask | bits for mask in self.masks for bits in group]

    def side(self, device):
        return lax.bitwise_and(lax.div(device, jnp.int32(self.core)), jnp.int32(1))

    def swap(self, value, mask):
        return lax.ppermute(value, AXES, [(d, d ^ mask) for d in range(self.count)])


def gather_kernel(
    plan, step, sorted_here, where_ref, x_hbm, g_hbm, wr_hbm, wpt_hbm, we_hbm, rdp_ref, cat_ref, *rest
):
    if sorted_here:
        kept_ref, sent_ref, turned_ref, *rest = rest
    else:
        keep_ref, send_ref, turned_ref, *rest = rest
    x_ref, g_ref, wpt_ref, we_ref, sums_ref, term_ref, small_sem, in_sem = rest
    rows = x_ref.shape[0]
    cr = we_ref.shape[1]
    nodes = wpt_ref.shape[0]
    wide = 2 * cr
    count = rows // step
    move = pltpu.make_async_copy
    small = [
        move(wr_hbm, cat_ref.at[:, pl.ds(0, cr)], small_sem.at[0]),
        move(wpt_hbm, wpt_ref, small_sem.at[1]),
        move(we_hbm, we_ref, small_sem.at[2]),
    ]
    load_cuts = sorted({0, min(1, count), min(2, count), count})
    span = lambda cuts, i: pl.ds(cuts[i] * step, (cuts[i + 1] - cuts[i]) * step)
    loads = [
        (
            move(x_hbm.at[span(load_cuts, i)], x_ref.at[span(load_cuts, i)], in_sem.at[0, i]),
            move(g_hbm.at[span(load_cuts, i)], g_ref.at[span(load_cuts, i)], in_sem.at[1, i]),
        )
        for i in range(len(load_cuts) - 1)
    ]
    for copy in (*small, *loads[0]):
        copy.start()
    sums_ref[...] = jnp.zeros_like(sums_ref)
    term_ref[...] = jnp.zeros_like(term_ref)
    small[0].wait()
    small[1].wait()
    padded = jnp.concatenate([wpt_ref[...], jnp.zeros_like(wpt_ref)], axis=0)
    cat_ref[:, cr:] = padded.T
    small[2].wait()

    @pl.loop(0, count)
    def _(i):
        for k, pair in enumerate(loads):
            @pl.when(i == load_cuts[k])
            def _():
                for copy in pair:
                    copy.wait()
                if k + 1 < len(loads):
                    for copy in loads[k + 1]:
                        copy.start()

        c = pl.ds(pl.multiple_of(i * step, step), step)
        x, g = x_ref[c], g_ref[c]
        both = mxu(x, cat_ref[...]).astype(BF16)
        mapped = mxu(g, we_ref[...]).astype(BF16)
        rdp = jnp.concatenate([both[:, :cr], mapped, both[:, cr:]], axis=1)
        rdp_ref[c] = rdp
        turned = rdp.T
        proj = turned[wide : wide + nodes]
        sums_ref[: wide + nodes] += mxu(turned[: wide + nodes], x)
        sums_ref[wide + nodes :] += mxu(proj, g)
        term_ref[...] += mxu(proj, rdp[:, :wide])

    me = where_ref[0]
    side = plan.side(me)
    turned_ref[...] = sums_ref[...].T
    if not sorted_here:
        heads = (keep_ref, send_ref)
    else:
        heads = (kept_ref.at[:nodes], sent_ref.at[:nodes])
    left, right = term_ref[:, :cr], term_ref[:, cr:]
    heads[0][...] = jnp.where(side == 0, left, right)
    heads[1][...] = jnp.where(side == 0, right, left)
    if sorted_here:
        size = turned_ref.shape[0] // plan.count
        for base, out_ref in ((me, kept_ref), (me ^ plan.core, sent_ref)):
            to = nodes
            for mask in plan.masks:
                at = pl.multiple_of((base ^ mask) * size, size)
                block = turned_ref[pl.ds(at, size), :]
                for lane in range(0, block.shape[1], cr):
                    out_ref[to : to + size] = block[:, lane : lane + cr]
                    to += size


def gather(plan, where, x, g, wr, wpt, we):
    rows, chan = x.shape
    cr, nodes = wr.shape[1], wpt.shape[0]
    step = row_block(rows, 1024)
    width = 2 * cr + 2 * nodes
    half = plan.count // 2
    size = chan // plan.count
    sorted_here = size % 8 == 0
    outs = [
        (VMEM, pltpu.VMEM((rows, width), BF16)),
        (VMEM, pltpu.VMEM((chan, cr + 2 * nodes), BF16)),
    ]
    scratch = []
    if sorted_here:
        outs += [(VMEM, pltpu.VMEM((nodes + half * size * width // cr, cr), F32))] * 2
        scratch += [pltpu.VMEM((chan, width), F32)]
    else:
        outs += [(VMEM, jax.ShapeDtypeStruct((nodes, cr), F32))] * 2
        outs += [(VMEM, jax.ShapeDtypeStruct((chan, width), F32))]
    scratch += [
        pltpu.VMEM((rows, chan), BF16),
        pltpu.VMEM((rows, chan), BF16),
        pltpu.VMEM(wpt.shape, BF16),
        pltpu.VMEM(we.shape, BF16),
        pltpu.VMEM((width, chan), F32),
        pltpu.VMEM((nodes, 2 * cr), F32),
        pltpu.SemaphoreType.DMA((3,)),
        pltpu.SemaphoreType.DMA((2, 3)),
    ]
    rdp, wcat, kept, sent, *sums = pl.pallas_call(
        functools.partial(gather_kernel, plan, step, sorted_here),
        in_specs=[SMEM] + [HBM] * 5,
        out_specs=[spec for spec, _ in outs],
        out_shape=[shape for _, shape in outs],
        scratch_shapes=scratch,
        compiler_params=params(),
        cost_estimate=cost(2 * rows * chan * 1024, rows * chan * 4 + rows * 768),
        name="gather",
    )(where, *in_hbm(x, g, wr, wpt, we))
    if not sorted_here:
        table = jnp.array(plan.masks, jnp.int32)
        cut = sums[0].reshape(plan.count, size, width // cr, cr).transpose(0, 2, 1, 3)
        lay = lambda head, index: jnp.concatenate([head, cut[index].reshape(-1, cr)])
        kept = lay(kept, where[0] ^ table)
        sent = lay(sent, where[0] ^ plan.core ^ table)
    return rdp, wcat, kept, sent


def step_kernel(head, ins, parts, after, *refs):
    terms, outs = refs[:ins], refs[ins + after :]

    def total(start, size):
        value = terms[0][start : start + size]
        for ref in terms[1:]:
            value = value + ref[start : start + size]
        return value

    nodes = total(0, head)
    rest = terms[0].shape[0] - head
    if parts == 1:
        outs[0][...] = nodes
        outs[1][...] = total(head, rest)
        return
    size = rest // parts
    for k, ref in enumerate(outs):
        ref[:head] = nodes
        ref[head:] = total(head + k * size, size)


def step(head, parts, terms, after=()):
    rest, lanes = terms[0].shape[0] - head, terms[0].shape[1]
    shapes = (head, rest) if parts == 1 else (head + rest // parts,) * parts
    return pl.pallas_call(
        functools.partial(step_kernel, head, len(terms), parts, len(after)),
        in_specs=[VMEM] * len(terms) + [pl.BlockSpec(memory_space=pl.ANY)] * len(after),
        out_specs=[VMEM] * len(shapes),
        out_shape=[pltpu.VMEM((size, lanes), F32) for size in shapes],
        compiler_params=params(SMALL_LIMIT),
        cost_estimate=cost(terms[0].size, 12 * terms[0].size),
        name="step",
    )(*terms, *after)


def fetch_kernel(_, *refs):
    sems = refs[-1]
    count = len(refs) // 2
    copies = [
        pltpu.make_async_copy(src, dst, sems.at[k])
        for k, (src, dst) in enumerate(zip(refs[:count], refs[count:-1]))
    ]
    for copy in copies:
        copy.start()
    for copy in copies:
        copy.wait()


def fetch(after, *values):
    return pl.pallas_call(
        fetch_kernel,
        in_specs=[pl.BlockSpec(memory_space=pl.ANY)] + [HBM] * len(values),
        out_specs=[VMEM] * len(values),
        out_shape=[pltpu.VMEM(value.shape, value.dtype) for value in values],
        scratch_shapes=[pltpu.SemaphoreType.DMA((len(values),))],
        compiler_params=params(SMALL_LIMIT),
        cost_estimate=cost(0, sum(value.size * value.dtype.itemsize for value in values)),
        name="fetch",
    )(after, *in_hbm(*values))


def feature_kernel(
    cuts, scale, plan, where_ref, mine_ref, other_ref, sums_ref, adj_ref, nw_ref, wcat_ref, rdp_ref, g_ref,
    out_hbm, gr_ref, gp_ref, ge_ref, ga_ref, gn_ref, out_ref, mix_ref, dnb_ref, out_sem,
):
    nodes_n, cr = mine_ref.shape
    wide = 2 * cr
    first = plan.side(where_ref[0]) == 0
    mine, other = mine_ref[...], other_ref[...]
    nodes = scale * jnp.where(first, mine, other)
    d_node_out = jnp.where(first, other, mine)
    adj, nw = adj_ref[...], nw_ref[...]
    hidden = nodes - exact(adj, nodes)
    pre = exact(hidden, nw)
    node_out = jnp.maximum(pre, 0.0).astype(BF16)
    d_pre = jnp.where(pre > 0.0, d_node_out, 0.0)
    d_hidden = exact(d_pre, nw, ((1,), (1,)))
    d_nodes = d_hidden - exact(adj, d_hidden, ((0,), (0,)))
    dn = d_nodes.astype(BF16)
    no_f, dn_f = node_out.astype(F32), dn.astype(F32)
    dnb_ref[:nodes_n] = dn
    dnb_ref[nodes_n:] = jnp.zeros((nodes_n, cr), BF16)
    mix_ref[...] = jnp.zeros_like(mix_ref)
    mix_ref[:nodes_n, :cr] = dn
    mix_ref[cr : cr + nodes_n, cr:] = node_out
    copies = []
    for i, (start, stop) in enumerate(zip(cuts, cuts[1:])):
        c = pl.ds(start, stop - start)
        rdp = rdp_ref[c]
        mixed = mxu(rdp[:, :wide], mix_ref[...], ((1,), (1,)))
        d_proj = (mixed[:, cr:] + scale * mixed[:, :cr]).astype(BF16)
        d_red = (scale * mxu(rdp[:, wide:], dnb_ref[...])).astype(BF16)
        both = jnp.concatenate([d_red, d_proj], axis=1)
        out = g_ref[c].astype(F32) + mxu(both, wcat_ref[...], ((1,), (1,)))
        out_ref[c] = out.astype(BF16)
        copies.append(pltpu.make_async_copy(out_ref.at[c], out_hbm.at[c], out_sem.at[i]))
        copies[-1].start()
    gn_ref[...] = scale * exact(hidden, d_pre, ((0,), (0,)))
    ga_ref[...] = -scale * exact(d_hidden, nodes, ((1,), (1,)))
    size = gr_ref.shape[0]
    x_red, x_dm, with_proj = (sums_ref[k * size : (k + 1) * size] for k in range(3))
    dn_s = scale * dn_f
    beside = jnp.concatenate([no_f, dn_s], axis=1)
    gp_ref[...] = scale * exact(jnp.concatenate([x_dm, x_red], axis=1), beside, ((1,), (1,)))
    blank = jnp.zeros_like(no_f)
    corners = jnp.concatenate(
        [jnp.concatenate([dn_s, blank], axis=1), jnp.concatenate([blank, no_f], axis=1)], axis=0
    )
    pair = scale * exact(with_proj, corners)
    gr_ref[...] = pair[:, :cr]
    ge_ref[...] = pair[:, cr:]
    for copy in copies:
        copy.wait()


def feature_grads(plan, where, mine, other, sums, adjacency, node_weight, wcat, rdp, g, scale):
    rows, chan = g.shape
    nodes, cr = adjacency.shape[0], node_weight.shape[0]
    unit = row_block(rows // 12, 256)
    cuts = sorted({0, *(rows - k * unit for k in (1, 4, 8) if k * unit < rows), rows})
    size = chan // plan.count
    there = [
        pltpu.with_memory_space_constraint(value, pltpu.VMEM)
        for value in (mine, other, sums, adjacency, node_weight, wcat, rdp, g)
    ]
    return pl.pallas_call(
        functools.partial(feature_kernel, cuts, scale, plan),
        in_specs=[SMEM] + [VMEM] * len(there),
        out_specs=[HBM] + [VMEM] * 5,
        out_shape=[
            pltpu.HBM((rows, chan), BF16),
            jax.ShapeDtypeStruct((size, cr), F32),
            jax.ShapeDtypeStruct((size, nodes), F32),
            jax.ShapeDtypeStruct((size, cr), F32),
            jax.ShapeDtypeStruct((nodes, nodes), F32),
            jax.ShapeDtypeStruct((cr, cr), F32),
        ],
        scratch_shapes=[
            pltpu.VMEM((rows, chan), BF16),
            pltpu.VMEM((2 * cr, 2 * cr), BF16),
            pltpu.VMEM((2 * nodes, cr), BF16),
            pltpu.SemaphoreType.DMA((len(cuts) - 1,)),
        ],
        compiler_params=params(),
        cost_estimate=cost(2 * rows * 4 * 65536, rows * chan * 4 + rows * 768),
        name="feature_grads",
    )(where, *there)


def on_device(
    plan, features, cotangent, reduce_weight, project_weight, expand_weight, adjacency, node_weight
):
    size_x, size_y, size_z, chan = features.shape
    local = size_x * size_y * size_z
    scale = 1.0 / math.sqrt(local * plan.count)
    flat_x = features.transpose(0, 2, 1, 3).reshape(local, chan)
    flat_g = cotangent.transpose(0, 2, 1, 3).reshape(local, chan)
    me = lax.axis_index(AXES).astype(jnp.int32)
    where = me.reshape(1)

    rdp, wcat, kept, sent = gather(
        plan, where, flat_x, flat_g, reduce_weight, project_weight.T, expand_weight
    )
    head = adjacency.shape[0]
    terms = [kept, plan.swap(sent, plan.core)]
    ready = None
    for group in plan.groups:
        parts = step(head, len(group), terms, ready[:1] if ready else ())
        terms = [plan.swap(part, mask) if mask else part for part, mask in zip(parts, group)]
        ready = ready or fetch(parts[0], adjacency, node_weight, flat_g)
    mine, sums = step(head, 1, terms)
    other = plan.swap(mine, plan.core)

    flat_out, grad_reduce, grad_project, grad_expand, grad_adjacency, grad_node = feature_grads(
        plan, where, mine, other, sums, *ready[:2], wcat, rdp, ready[2], scale
    )
    grad_features = flat_out.reshape(size_x, size_z, size_y, chan).transpose(0, 2, 1, 3)
    return (grad_features, grad_reduce, grad_project, grad_expand, grad_adjacency, grad_node)


def solution(mesh):
    return jax.shard_map(
        functools.partial(on_device, Plan(mesh)),
        mesh=mesh,
        in_specs=(P("gx", "gy", "gz", None), P("gx", "gy", "gz", None), P(), P(), P(), P(), P()),
        out_specs=(
            P("gx", "gy", "gz", None),
            P(AXES, None),
            P(AXES, None),
            P(AXES, None),
            P(),
            P(),
        ),
        check_vma=False,
    )
```

```python
import functools
import math

import jax
import jax.numpy as jnp
from jax import lax
from jax.experimental import pallas as pl
from jax.experimental.pallas import tpu as pltpu
from jax.sharding import PartitionSpec as P

AXES = ("gx", "gy", "gz")
F32 = jnp.float32
BF16 = jnp.bfloat16
HBM = pl.BlockSpec(memory_space=pltpu.HBM)
VMEM = pl.BlockSpec(memory_space=pltpu.VMEM)
SMEM = pl.BlockSpec(memory_space=pltpu.SMEM)
VMEM_LIMIT = 24 * 1024 * 1024
SMALL_LIMIT = 4 * 1024 * 1024


def exact(a, b, dims=((1,), (0,))):
    return lax.dot_general(
        a, b, (dims, ((), ())), precision=lax.Precision.HIGHEST, preferred_element_type=F32
    )


def mxu(a, b, dims=((1,), (0,))):
    return lax.dot_general(a, b, (dims, ((), ())), preferred_element_type=F32)


def params(limit=VMEM_LIMIT):
    return pltpu.CompilerParams(vmem_limit_bytes=limit)


def cost(flops, nbytes):
    return pl.CostEstimate(flops=flops, bytes_accessed=nbytes, transcendentals=0)


def in_hbm(*values):
    return [pltpu.with_memory_space_constraint(value, pltpu.HBM) for value in values]


def row_block(total, largest):
    for size in (1536, 1024, 768, 512, 384, 256, 128, 64, 32, 16):
        if size <= largest and total % size == 0:
            return size
    return total


class Plan:
    def __init__(self, mesh):
        size = {axis: mesh.shape[axis] for axis in AXES}
        self.count = math.prod(size.values())
        stride = {"gx": size["gy"] * size["gz"], "gy": size["gz"], "gz": 1}
        self.core = stride["gy"]
        wide = [0, *sorted(range(1, size["gx"]), key=lambda k: -k.bit_count())]
        turned = [0, *sorted(range(1, size["gx"]), key=lambda k: (-k.bit_count(), -k))]
        rest = range(size["gy"] // 2)
        deep = [0, *range(2, size["gz"]), 1]
        spans = (
            (wide, turned, stride["gx"]), (rest, rest, 2 * stride["gy"]), (deep, deep, stride["gz"])
        )
        self.groups = [
            [(a * step, b * step) for a, b in zip(one, other)] for one, other, step in spans if len(one) > 1
        ]
        self.masks = [(0, 0)]
        for group in self.groups:
            self.masks = [(a | x, b | y) for a, b in self.masks for x, y in group]

    def side(self, device):
        return lax.bitwise_and(lax.div(device, jnp.int32(self.core)), jnp.int32(1))

    def swap(self, value, mask):
        return lax.ppermute(value, AXES, [(d, d ^ mask[d // self.core & 1]) for d in range(self.count)])


def gather_kernel(
    plan, step, sorted_here, where_ref, x_hbm, g_hbm, wr_hbm, wpt_hbm, we_hbm, rdp_ref, cat_ref, *rest
):
    if sorted_here:
        kept_ref, sent_ref, turned_ref, *rest = rest
    else:
        keep_ref, send_ref, turned_ref, *rest = rest
    x_ref, g_ref, wpt_ref, we_ref, sums_ref, term_ref, small_sem, in_sem = rest
    rows = x_ref.shape[0]
    cr = we_ref.shape[1]
    nodes = wpt_ref.shape[0]
    wide = 2 * cr
    count = rows // step
    move = pltpu.make_async_copy
    small = [
        move(wr_hbm, cat_ref.at[:, pl.ds(0, cr)], small_sem.at[0]),
        move(wpt_hbm, wpt_ref, small_sem.at[1]),
        move(we_hbm, we_ref, small_sem.at[2]),
    ]
    load_cuts = sorted({0, min(1, count), min(2, count), count})
    span = lambda cuts, i: pl.ds(cuts[i] * step, (cuts[i + 1] - cuts[i]) * step)
    loads = [
        (
            move(x_hbm.at[span(load_cuts, i)], x_ref.at[span(load_cuts, i)], in_sem.at[0, i]),
            move(g_hbm.at[span(load_cuts, i)], g_ref.at[span(load_cuts, i)], in_sem.at[1, i]),
        )
        for i in range(len(load_cuts) - 1)
    ]
    for copy in (*small, *loads[0]):
        copy.start()
    sums_ref[...] = jnp.zeros_like(sums_ref)
    term_ref[...] = jnp.zeros_like(term_ref)
    small[0].wait()
    small[1].wait()
    padded = jnp.concatenate([wpt_ref[...], jnp.zeros_like(wpt_ref)], axis=0)
    cat_ref[:, cr:] = padded.T
    small[2].wait()

    @pl.loop(0, count)
    def _(i):
        for k, pair in enumerate(loads):
            @pl.when(i == load_cuts[k])
            def _():
                for copy in pair:
                    copy.wait()
                if k + 1 < len(loads):
                    for copy in loads[k + 1]:
                        copy.start()

        c = pl.ds(pl.multiple_of(i * step, step), step)
        x, g = x_ref[c], g_ref[c]
        both = mxu(x, cat_ref[...]).astype(BF16)
        mapped = mxu(g, we_ref[...]).astype(BF16)
        rdp = jnp.concatenate([both[:, :cr], mapped, both[:, cr:]], axis=1)
        rdp_ref[c] = rdp
        turned = rdp.T
        proj = turned[wide : wide + nodes]
        sums_ref[: wide + nodes] += mxu(turned[: wide + nodes], x)
        sums_ref[wide + nodes :] += mxu(proj, g)
        term_ref[...] += mxu(proj, rdp[:, :wide])

    me = where_ref[0]
    side = plan.side(me)
    turned_ref[...] = sums_ref[...].T
    if not sorted_here:
        heads = (keep_ref, send_ref)
    else:
        heads = (kept_ref.at[:nodes], sent_ref.at[:nodes])
    left, right = term_ref[:, :cr], term_ref[:, cr:]
    heads[0][...] = jnp.where(side == 0, left, right)
    heads[1][...] = jnp.where(side == 0, right, left)
    if sorted_here:
        size = turned_ref.shape[0] // plan.count
        for base, of, out_ref in ((me, side, kept_ref), (me ^ plan.core, 1 - side, sent_ref)):
            to = nodes
            for masks in plan.masks:
                mask = jnp.where(of == 0, *masks)
                at = pl.multiple_of((base ^ mask) * size, size)
                block = turned_ref[pl.ds(at, size), :]
                for lane in range(0, block.shape[1], cr):
                    out_ref[to : to + size] = block[:, lane : lane + cr]
                    to += size


def gather(plan, where, x, g, wr, wpt, we):
    rows, chan = x.shape
    cr, nodes = wr.shape[1], wpt.shape[0]
    step = row_block(rows, 1536)
    width = 2 * cr + 2 * nodes
    half = plan.count // 2
    size = chan // plan.count
    sorted_here = size % 8 == 0
    outs = [
        (VMEM, pltpu.VMEM((rows, width), BF16)),
        (VMEM, pltpu.VMEM((chan, cr + 2 * nodes), BF16)),
    ]
    scratch = []
    if sorted_here:
        outs += [(VMEM, pltpu.VMEM((nodes + half * size * width // cr, cr), F32))] * 2
        scratch += [pltpu.VMEM((chan, width), F32)]
    else:
        outs += [(VMEM, jax.ShapeDtypeStruct((nodes, cr), F32))] * 2
        outs += [(VMEM, jax.ShapeDtypeStruct((chan, width), F32))]
    scratch += [
        pltpu.VMEM((rows, chan), BF16),
        pltpu.VMEM((rows, chan), BF16),
        pltpu.VMEM(wpt.shape, BF16),
        pltpu.VMEM(we.shape, BF16),
        pltpu.VMEM((width, chan), F32),
        pltpu.VMEM((nodes, 2 * cr), F32),
        pltpu.SemaphoreType.DMA((3,)),
        pltpu.SemaphoreType.DMA((2, 3)),
    ]
    rdp, wcat, kept, sent, *sums = pl.pallas_call(
        functools.partial(gather_kernel, plan, step, sorted_here),
        in_specs=[SMEM] + [HBM] * 5,
        out_specs=[spec for spec, _ in outs],
        out_shape=[shape for _, shape in outs],
        scratch_shapes=scratch,
        compiler_params=params(),
        cost_estimate=cost(2 * rows * chan * 1024, rows * chan * 4 + rows * 768),
        name="gather",
    )(where, *in_hbm(x, g, wr, wpt, we))
    if not sorted_here:
        table = jnp.array(plan.masks, jnp.int32)
        cut = sums[0].reshape(plan.count, size, width // cr, cr).transpose(0, 2, 1, 3)
        lay = lambda head, index: jnp.concatenate([head, cut[index].reshape(-1, cr)])
        side = plan.side(where[0])
        kept = lay(kept, where[0] ^ table[:, side])
        sent = lay(sent, where[0] ^ plan.core ^ table[:, 1 - side])
    return rdp, wcat, kept, sent


def step_kernel(head, ins, parts, after, *refs):
    terms, outs = refs[:ins], refs[ins + after :]

    def total(start, size):
        value = terms[0][start : start + size]
        for ref in terms[1:]:
            value = value + ref[start : start + size]
        return value

    nodes = total(0, head)
    rest = terms[0].shape[0] - head
    if parts == 1:
        outs[0][...] = nodes
        outs[1][...] = total(head, rest)
        return
    size = rest // parts
    for k, ref in enumerate(outs):
        ref[:head] = nodes
        ref[head:] = total(head + k * size, size)


def step(head, parts, terms, after=()):
    rest, lanes = terms[0].shape[0] - head, terms[0].shape[1]
    shapes = (head, rest) if parts == 1 else (head + rest // parts,) * parts
    return pl.pallas_call(
        functools.partial(step_kernel, head, len(terms), parts, len(after)),
        in_specs=[VMEM] * len(terms) + [pl.BlockSpec(memory_space=pl.ANY)] * len(after),
        out_specs=[VMEM] * len(shapes),
        out_shape=[pltpu.VMEM((size, lanes), F32) for size in shapes],
        compiler_params=params(SMALL_LIMIT),
        cost_estimate=cost(terms[0].size, 12 * terms[0].size),
        name="step",
    )(*terms, *after)


def fetch_kernel(_, *refs):
    sems = refs[-1]
    count = len(refs) // 2
    copies = [
        pltpu.make_async_copy(src, dst, sems.at[k])
        for k, (src, dst) in enumerate(zip(refs[:count], refs[count:-1]))
    ]
    for copy in copies:
        copy.start()
    for copy in copies:
        copy.wait()


def fetch(after, *values):
    return pl.pallas_call(
        fetch_kernel,
        in_specs=[pl.BlockSpec(memory_space=pl.ANY)] + [HBM] * len(values),
        out_specs=[VMEM] * len(values),
        out_shape=[pltpu.VMEM(value.shape, value.dtype) for value in values],
        scratch_shapes=[pltpu.SemaphoreType.DMA((len(values),))],
        compiler_params=params(SMALL_LIMIT),
        cost_estimate=cost(0, sum(value.size * value.dtype.itemsize for value in values)),
        name="fetch",
    )(after, *in_hbm(*values))


def feature_kernel(
    cuts, scale, plan, where_ref, mine_ref, other_ref, sums_ref, adj_ref, nw_ref, wcat_ref, rdp_ref, g_ref,
    out_hbm, gr_ref, gp_ref, ge_ref, ga_ref, gn_ref, out_ref, mix_ref, dnb_ref, out_sem,
):
    nodes_n, cr = mine_ref.shape
    wide = 2 * cr
    first = plan.side(where_ref[0]) == 0
    mine, other = mine_ref[...], other_ref[...]
    nodes = scale * jnp.where(first, mine, other)
    d_node_out = jnp.where(first, other, mine)
    adj, nw = adj_ref[...], nw_ref[...]
    hidden = nodes - exact(adj, nodes)
    pre = exact(hidden, nw)
    node_out = jnp.maximum(pre, 0.0).astype(BF16)
    d_pre = jnp.where(pre > 0.0, d_node_out, 0.0)
    d_hidden = exact(d_pre, nw, ((1,), (1,)))
    d_nodes = d_hidden - exact(adj, d_hidden, ((0,), (0,)))
    dn = d_nodes.astype(BF16)
    no_f, dn_f = node_out.astype(F32), dn.astype(F32)
    dnb_ref[:nodes_n] = dn
    dnb_ref[nodes_n:] = jnp.zeros((nodes_n, cr), BF16)
    mix_ref[...] = jnp.zeros_like(mix_ref)
    mix_ref[:nodes_n, :cr] = dn
    mix_ref[cr : cr + nodes_n, cr:] = node_out
    copies = []
    for i, (start, stop) in enumerate(zip(cuts, cuts[1:])):
        c = pl.ds(start, stop - start)
        rdp = rdp_ref[c]
        mixed = mxu(rdp[:, :wide], mix_ref[...], ((1,), (1,)))
        d_proj = (mixed[:, cr:] + scale * mixed[:, :cr]).astype(BF16)
        d_red = (scale * mxu(rdp[:, wide:], dnb_ref[...])).astype(BF16)
        both = jnp.concatenate([d_red, d_proj], axis=1)
        out = g_ref[c].astype(F32) + mxu(both, wcat_ref[...], ((1,), (1,)))
        out_ref[c] = out.astype(BF16)
        copies.append(pltpu.make_async_copy(out_ref.at[c], out_hbm.at[c], out_sem.at[i]))
        copies[-1].start()
    gn_ref[...] = scale * exact(hidden, d_pre, ((0,), (0,)))
    ga_ref[...] = -scale * exact(d_hidden, nodes, ((1,), (1,)))
    size = gr_ref.shape[0]
    x_red, x_dm, with_proj = (sums_ref[k * size : (k + 1) * size] for k in range(3))
    gr_ref[...] = scale * scale * exact(with_proj[:, :nodes_n], dn_f)
    gp_ref[...] = scale * exact(x_dm, no_f, ((1,), (1,))) + scale * scale * exact(
        x_red, dn_f, ((1,), (1,))
    )
    ge_ref[...] = scale * exact(with_proj[:, nodes_n:], no_f)
    for copy in copies:
        copy.wait()


def feature_grads(plan, where, mine, other, sums, adjacency, node_weight, wcat, rdp, g, scale):
    rows, chan = g.shape
    nodes, cr = adjacency.shape[0], node_weight.shape[0]
    unit = row_block(rows // 12, 256)
    cuts = sorted({0, *(rows - k * unit for k in (1, 4, 8) if k * unit < rows), rows})
    size = chan // plan.count
    there = [
        pltpu.with_memory_space_constraint(value, pltpu.VMEM)
        for value in (mine, other, sums, adjacency, node_weight, wcat, rdp, g)
    ]
    return pl.pallas_call(
        functools.partial(feature_kernel, cuts, scale, plan),
        in_specs=[SMEM] + [VMEM] * len(there),
        out_specs=[HBM] + [VMEM] * 5,
        out_shape=[
            pltpu.HBM((rows, chan), BF16),
            jax.ShapeDtypeStruct((size, cr), F32),
            jax.ShapeDtypeStruct((size, nodes), F32),
            jax.ShapeDtypeStruct((size, cr), F32),
            jax.ShapeDtypeStruct((nodes, nodes), F32),
            jax.ShapeDtypeStruct((cr, cr), F32),
        ],
        scratch_shapes=[
            pltpu.VMEM((rows, chan), BF16),
            pltpu.VMEM((2 * cr, 2 * cr), BF16),
            pltpu.VMEM((2 * nodes, cr), BF16),
            pltpu.SemaphoreType.DMA((len(cuts) - 1,)),
        ],
        compiler_params=params(),
        cost_estimate=cost(2 * rows * 4 * 65536, rows * chan * 4 + rows * 768),
        name="feature_grads",
    )(where, *there)


def on_device(
    plan, features, cotangent, reduce_weight, project_weight, expand_weight, adjacency, node_weight
):
    size_x, size_y, size_z, chan = features.shape
    local = size_x * size_y * size_z
    scale = 1.0 / math.sqrt(local * plan.count)
    flat_x = features.transpose(0, 2, 1, 3).reshape(local, chan)
    flat_g = cotangent.transpose(0, 2, 1, 3).reshape(local, chan)
    me = lax.axis_index(AXES).astype(jnp.int32)
    where = me.reshape(1)

    rdp, wcat, kept, sent = gather(
        plan, where, flat_x, flat_g, reduce_weight, project_weight.T, expand_weight
    )
    head = adjacency.shape[0]
    terms = [kept, plan.swap(sent, (plan.core, plan.core))]
    ready = None
    for group in plan.groups:
        parts = step(head, len(group), terms, ready[:1] if ready else ())
        terms = [plan.swap(part, mask) if any(mask) else part for part, mask in zip(parts, group)]
        ready = ready or fetch(parts[0], adjacency, node_weight, flat_g)
    mine, sums = step(head, 1, terms)
    other = plan.swap(mine, (plan.core, plan.core))

    flat_out, grad_reduce, grad_project, grad_expand, grad_adjacency, grad_node = feature_grads(
        plan, where, mine, other, sums, *ready[:2], wcat, rdp, ready[2], scale
    )
    grad_features = flat_out.reshape(size_x, size_z, size_y, chan).transpose(0, 2, 1, 3)
    return (grad_features, grad_reduce, grad_project, grad_expand, grad_adjacency, grad_node)


def solution(mesh):
    return jax.shard_map(
        functools.partial(on_device, Plan(mesh)),
        mesh=mesh,
        in_specs=(P("gx", "gy", "gz", None), P("gx", "gy", "gz", None), P(), P(), P(), P(), P()),
        out_specs=(
            P("gx", "gy", "gz", None),
            P(AXES, None),
            P(AXES, None),
            P(AXES, None),
            P(),
            P(),
        ),
        check_vma=False,
    )
```
